32 devices in a mesh: ctx: 8 (over y, x, core), fsdp: 4 (over z).
Axes of the slice: x: 2, y: 2, z: 4, core: 2. Of those that a mesh axis runs over, the one named last changes fastest.
Arguments:
- hidden_states: bfloat16 [8, 2048, 768], P('fsdp', 'ctx'), may hold values from -6 to 6
- lengths: int32 [8], P('fsdp'), may hold values from 128 to 2048, as said below
- cotangent: bfloat16 [8, 2048, 768], P('fsdp', 'ctx'), may hold values from -6 to 6
- attend_weight: bfloat16 [768, 2304], P('fsdp'), may hold values from -0.21875 to 0.21875
- query_bias: bfloat16 [768], P('fsdp'), may hold values from -3 to 3
- value_bias: bfloat16 [768], P('fsdp'), may hold values from -0.119628906 to 0.119628906
- output_weight: bfloat16 [768, 768], P('fsdp'), may hold values from -3.5 to 3.5
- output_bias: bfloat16 [768], P('fsdp'), may hold values from -3 to 3
- first_gain: bfloat16 [768], P('fsdp'), may hold values from 0.099609375 to 1.8984375
- first_shift: bfloat16 [768], P('fsdp'), may hold values from -3 to 3
- raise_weight: bfloat16 [768, 3072], P('fsdp'), may hold values from -0.21875 to 0.21875
- raise_bias: bfloat16 [3072], P('fsdp'), may hold values from -3 to 3
- lower_weight: bfloat16 [3072, 768], P('fsdp'), may hold values from -0.109375 to 0.109375
- lower_bias: bfloat16 [768], P('fsdp'), may hold values from -3 to 3
- second_gain: bfloat16 [768], P('fsdp'), may hold values from 0.099609375 to 1.8984375
- second_shift: bfloat16 [768], P('fsdp'), may hold values from -3 to 3
Outputs:
- layer_output: bfloat16 [8, 2048, 768], P('fsdp', 'ctx')
- hidden_grad: float32 [8, 2048, 768], P('fsdp', 'ctx')
- grad_attend_weight: float32 [768, 2304], P('fsdp')
- grad_query_bias: float32 [768], P('fsdp')
- grad_value_bias: float32 [768], P('fsdp')
- grad_output_weight: float32 [768, 768], P('fsdp')
- grad_output_bias: float32 [768], P('fsdp')
- grad_first_gain: float32 [768], P('fsdp')
- grad_first_shift: float32 [768], P('fsdp')
- grad_raise_weight: float32 [768, 3072], P('fsdp')
- grad_raise_bias: float32 [3072], P('fsdp')
- grad_lower_weight: float32 [3072, 768], P('fsdp')
- grad_lower_bias: float32 [768], P('fsdp')
- grad_second_gain: float32 [768], P('fsdp')
- grad_second_shift: float32 [768], P('fsdp')
The draws below stay inside these ranges and needn't reach their ends.
Inputs may be any that keep to these rules, and one draw needn't show every extreme that they name: `lengths`: among the 2 sequences of each index of fsdp, one drawn from the seed has length exactly 2048; the others are drawn evenly.
All inputs are finite; a program needn't handle non-finite values.
Results may differ from the reference program's by a relative error of at most 0.02.
Values may be sent and summed in bfloat16 or wider, within the bound.
No kernel may reach another device: no remote copies, remote signals or barrier semaphores. Data moves between devices by JAX's collectives and lax.ppermute only.
A program may use at most 320 MiB of HBM per device.

```python
import math
import jax
import jax.numpy as jnp
from jax import lax

D = 768
HEADS = 12
HEAD_DIM = 64
FF = 3072
TOK_DEV = 256
SEQ_DEV = 2
LENGTH = 2048
SEQS = 8


def draw_lengths(key, part):
    key = jax.random.fold_in(key, 11)
    base_key, pick_key = jax.random.split(key)
    group_count = SEQS // SEQ_DEV
    drawn = jax.random.randint(base_key, (group_count, SEQ_DEV), TOK_DEV // 2, LENGTH + 1)
    chosen = jax.random.randint(pick_key, (group_count, 1), 0, SEQ_DEV)
    marked = jnp.arange(SEQ_DEV, dtype=jnp.int32)[None, :] == chosen
    return jnp.where(marked, LENGTH, drawn).reshape(SEQS).astype(jnp.int32)


def steps_of(key, dims, pieces, least, high):
    loudness, own = 1.0, jax.random.fold_in(key, 6)
    for axis_at, parts in pieces:
        draws = jnp.exp(jax.random.uniform(jax.random.fold_in(own, axis_at), (parts,), jnp.float32, least / len(pieces), high / len(pieces)))
        loudness = loudness * jnp.repeat(draws, dims[axis_at] // parts).reshape([-1 if axis == axis_at else 1 for axis in range(len(dims))])
    return loudness


def normal_values(key, shape, scale, limit, cuts=(), kind=jnp.bfloat16):
    values = jax.random.normal(key, shape, jnp.float32) * scale
    if len(cuts) > 0:
        values = steps_of(key, shape, cuts, -0.22, 0.18) * values
    return jnp.clip(values, min=-limit, max=limit).astype(kind)


def setup_inputs(seed: int = 0) -> dict:
    keys = jax.random.split(jax.random.key(seed), 17)
    hidden_states = normal_values(keys[0], (SEQS, LENGTH, D), 1.0, 6.0, ((0, 4), (1, 8)))
    lengths = draw_lengths(jax.random.fold_in(keys[16], 71), 0)
    cotangent = normal_values(keys[2], (SEQS, LENGTH, D), 1.0, 6.0, ((0, 4), (1, 8)))
    attend_weight = normal_values(keys[3], (D, 3 * D), D ** -0.5, 0.21875, ((0, 4),))
    query_bias = normal_values(keys[4], (D,), 0.5, 3.0, ((0, 4),))
    value_bias = normal_values(keys[5], (D,), 0.02, 0.119628906, ((0, 4),))
    output_weight = normal_values(keys[6], (D, D), (max(1, D * 8 // LENGTH)) ** -0.5, 3.5, ((0, 4),))
    output_bias = normal_values(keys[7], (D,), 0.5, 3.0, ((0, 4),))
    first_gain = jnp.clip(1.0 + 0.18 * jax.random.normal(keys[8], (D,), jnp.float32), 0.099609375, 1.8984375).astype(jnp.bfloat16)
    first_shift = normal_values(keys[9], (D,), 0.5, 3.0, ((0, 4),))
    raise_weight = normal_values(keys[10], (D, FF), D ** -0.5, 0.21875, ((0, 4),))
    raise_bias = normal_values(keys[11], (FF,), 0.5, 3.0, ((0, 4),))
    lower_weight = normal_values(keys[12], (FF, D), FF ** -0.5, 0.109375, ((0, 4),))
    lower_bias = normal_values(keys[13], (D,), 0.5, 3.0, ((0, 4),))
    second_gain = jnp.clip(1.0 + 0.18 * jax.random.normal(keys[14], (D,), jnp.float32), 0.099609375, 1.8984375).astype(jnp.bfloat16)
    second_shift = normal_values(keys[15], (D,), 0.5, 3.0, ((0, 4),))
    return {"hidden_states": hidden_states, "lengths": lengths, "cotangent": cotangent, "attend_weight": attend_weight, "query_bias": query_bias, "value_bias": value_bias, "output_weight": output_weight, "output_bias": output_bias, "first_gain": first_gain, "first_shift": first_shift, "raise_weight": raise_weight, "raise_bias": raise_bias, "lower_weight": lower_weight, "lower_bias": lower_bias, "second_gain": second_gain, "second_shift": second_shift}


HIGHEST = lax.Precision.HIGHEST

@jax.custom_vjp
def low(v):
    return lax.optimization_barrier(v.astype(jnp.bfloat16)).astype(jnp.float32)

@jax.custom_vjp
def low_back(v):
    return v

def low_keep(v):
    return (low(v), None)

def low_pass(kept, grad):
    return (grad,)

def back_keep(v):
    return (v, None)

def back_low(kept, grad):
    return (low(grad),)
low.defvjp(low_keep, low_pass)
low_back.defvjp(back_keep, back_low)

def layer_norm(hidden, gain, shift):
    average = lax.optimization_barrier(jnp.mean(hidden, axis=-1, keepdims=True))
    centred = hidden - average
    variance = lax.optimization_barrier(jnp.mean(centred * centred, axis=-1, keepdims=True))
    return centred * lax.rsqrt(variance + 1e-05) * gain + shift

def attend(queries, keys_all, values_all, usable):
    scale_factor = 1.0 / math.sqrt(HEAD_DIM)
    block_rows = math.gcd(LENGTH, 512)

    def one_block(query_rows):
        scores = jnp.einsum('qhd,khd->hqk', query_rows, keys_all, precision=HIGHEST) * scale_factor
        scores = low_back(scores)
        scores = jnp.where(usable[None, None, :], scores, -1000000000.0)
        weights = low(jax.nn.softmax(scores, axis=-1))
        return jnp.einsum('hqk,khd->qhd', weights, values_all, precision=HIGHEST)
    blocks = queries.reshape(LENGTH // block_rows, block_rows, HEADS, HEAD_DIM)
    return lax.map(jax.checkpoint(one_block), blocks).reshape(LENGTH, D)

def forward(token_rows, usable, attend_weight, query_bias, value_bias, output_weight, output_bias, first_gain, first_shift, raise_weight, raise_bias, lower_weight, lower_bias, second_gain, second_shift):
    mixture = jnp.dot(low(token_rows), attend_weight, precision=HIGHEST)
    queries = low(low_back(mixture[:, :D] + query_bias))
    keys_all = low(low_back(mixture[:, D:2 * D]))
    values_all = low(low_back(mixture[:, 2 * D:] + value_bias))
    head_shape = (LENGTH, HEADS, HEAD_DIM)
    attended = attend(queries.reshape(head_shape), keys_all.reshape(head_shape), values_all.reshape(head_shape), usable)
    projected = low_back(jnp.dot(low(low_back(attended)), output_weight, precision=HIGHEST) + output_bias)
    normed_first = layer_norm(token_rows + projected, first_gain, first_shift)
    raised = low_back(jnp.dot(low(normed_first), raise_weight, precision=HIGHEST) + raise_bias)
    active = jax.nn.gelu(raised, approximate=False)
    lowered = low_back(jnp.dot(low(active), lower_weight, precision=HIGHEST) + lower_bias)
    return layer_norm(normed_first + lowered, second_gain, second_shift)

def reference(hidden_states, lengths, cotangent, attend_weight, query_bias, value_bias, output_weight, output_bias, first_gain, first_shift, raise_weight, raise_bias, lower_weight, lower_bias, second_gain, second_shift):
    params = tuple((weight.astype(jnp.float32) for weight in (attend_weight, query_bias, value_bias, output_weight, output_bias, first_gain, first_shift, raise_weight, raise_bias, lower_weight, lower_bias, second_gain, second_shift)))
    key_places = jnp.arange(LENGTH, dtype=jnp.int32)

    def one_sequence(summed, element):
        token_rows, length, grad_rows = element
        usable = key_places < length

        def run_layer(inputs, *weights):
            return forward(inputs, usable, *weights)
        result, backward = jax.vjp(run_layer, token_rows.astype(jnp.float32), *params)
        gradients = backward(grad_rows.astype(jnp.float32))
        summed = tuple((total_now + extra for total_now, extra in zip(summed, gradients[1:])))
        return (summed, (result.astype(jnp.bfloat16), gradients[0]))
    initial = tuple((jnp.zeros_like(weight) for weight in params))
    summed, (layer_output, hidden_grad) = lax.scan(one_sequence, initial, (hidden_states, lengths, cotangent))
    return (layer_output, hidden_grad, summed[0], summed[1], summed[2], summed[3], summed[4], summed[5], summed[6], summed[7], summed[8], summed[9], summed[10], summed[11], summed[12])
```

```python
import functools
import math

import jax
import jax.numpy as jnp
from jax import lax
from jax.experimental import pallas as pl
from jax.experimental.pallas import tpu as pltpu
from jax.sharding import PartitionSpec as P

HEADS = 12
HEAD_DIM = 64
PAIR = 2 * HEAD_DIM
LOG2E = 1.4426950408889634
SCORE = LOG2E / math.sqrt(HEAD_DIM)
F32 = jnp.float32
BF16 = jnp.bfloat16
CHUNK_BLOCKS = 2
NT = (((1,), (1,)), ((), ()))


def layer_norm(hidden, gain, shift):
    average = jnp.mean(hidden, axis=-1, keepdims=True)
    centred = hidden - average
    variance = jnp.mean(centred * centred, axis=-1, keepdims=True)
    return centred * lax.rsqrt(variance + 1e-05) * gain + shift


def gelu_exact(inputs):
    return jax.nn.gelu(inputs, approximate=False)


def swap(value, bit):
    number = lax.axis_size("ctx")
    return lax.ppermute(value, "ctx", [(at, at ^ bit) for at in range(number)])


def shift_fsdp(value, step):
    number = lax.axis_size("fsdp")
    return lax.ppermute(value, "fsdp", [(at, (at + step) % number) for at in range(number)])


def ctx_bits():
    bits, bit = [], 2
    while bit < lax.axis_size("ctx"):
        bits.append(bit)
        bit *= 2
    return bits


def gather_ctx(piece, order):
    me = lax.axis_index("ctx")
    held, done = piece, []
    for bit in order:
        other = swap(held, bit)
        high = (me & bit) != 0
        place = sum(1 for earlier in done if earlier > bit)
        held = jnp.stack([jnp.where(high, other, held), jnp.where(high, held, other)], axis=place)
        done.append(bit)
    return held.reshape((lax.axis_size("ctx"),) + piece.shape)


def scatter_ctx_step(held, bits_left, bit):
    me = lax.axis_index("ctx")
    high = (me & bit) // bit
    axis = 1 + bits_left.index(bit)
    mine = lax.dynamic_index_in_dim(held, high, axis, keepdims=False)
    send = lax.dynamic_index_in_dim(held, 1 - high, axis, keepdims=False).astype(BF16)
    total = mine.astype(F32) + swap(send, bit).astype(F32)
    return total.astype(BF16), [left for left in bits_left if left != bit]


def sum_weight(partial):
    rows, columns = partial.shape
    number, groups = lax.axis_size("ctx"), lax.axis_size("fsdp")
    own = lax.axis_index("fsdp")
    chips = ctx_bits()
    all_bits = sorted(chips + [1], reverse=True)
    held = partial.reshape((groups,) + (2,) * len(all_bits) + (rows // (groups * number), columns))
    held, left = scatter_ctx_step(held, all_bits, 1)
    half = columns // 2
    pieces = []
    for part, order in ((held[..., :half], chips), (held[..., half:], chips[::-1])):
        part_left = left
        for bit in order:
            part, part_left = scatter_ctx_step(part, part_left, bit)
        pieces.append(part)
    piece = jnp.concatenate(pieces, axis=-1)
    total = lax.dynamic_index_in_dim(piece, own, 0, keepdims=False).astype(F32)
    for step in range(1, groups):
        send = lax.dynamic_index_in_dim(piece, (own + step) % groups, 0, keepdims=False)
        total = total + shift_fsdp(send, step).astype(F32)
    total = total.astype(BF16)
    left_half = gather_ctx(total[:, :half], chips[::-1] + [1])
    right_half = gather_ctx(total[:, half:], chips + [1])
    whole = jnp.concatenate([left_half, right_half], axis=-1)
    return whole.reshape(rows // groups, columns).astype(F32)


def sum_vectors(vectors):
    groups = lax.axis_size("fsdp")
    own = lax.axis_index("fsdp")
    packed = jnp.concatenate([vector.reshape(groups, -1) for vector in vectors], axis=1)
    for bit in [1] + ctx_bits():
        packed = packed + swap(packed, bit)
    total = lax.dynamic_index_in_dim(packed, own, 0, keepdims=False)
    for step in range(1, groups):
        send = lax.dynamic_index_in_dim(packed, (own + step) % groups, 0, keepdims=False)
        total = total + shift_fsdp(send, step)
    owned, at = [], 0
    for vector in vectors:
        width = vector.shape[0] // groups
        owned.append(total[at : at + width])
        at += width
    return owned


def gather_vectors(vectors):
    groups = lax.axis_size("fsdp")
    own = lax.axis_index("fsdp")
    packed = jnp.concatenate(vectors)[None]
    whole = jnp.zeros((groups, packed.shape[1]), packed.dtype)
    whole = lax.dynamic_update_slice(whole, packed, (own, 0))
    for step in range(1, groups):
        other = shift_fsdp(packed, step)
        whole = lax.dynamic_update_slice(whole, other, ((own - step) % groups, 0))
    gathered, at = [], 0
    for vector in vectors:
        width = vector.shape[0]
        gathered.append(whole[:, at : at + width].reshape(-1).astype(F32))
        at += width
    return gathered


def gather_weight_core(shard):
    rows, columns = shard.shape
    groups = lax.axis_size("fsdp")
    own = lax.axis_index("fsdp")
    core = lax.axis_index("ctx") % 2
    halves = shard.reshape(2, rows // 2, columns)
    whole = jnp.zeros((groups, 2, rows // 2, columns), shard.dtype)
    whole = lax.dynamic_update_slice(whole, halves[None], (own, 0, 0, 0))
    piece = lax.dynamic_index_in_dim(halves, core, 0, keepdims=False)
    for step in range(1, groups):
        piece = shift_fsdp(piece, 1)
        at = (own - step) % groups
        whole = lax.dynamic_update_slice(whole, piece[None, None], (at, core, 0, 0))
        whole = lax.dynamic_update_slice(whole, swap(piece, 1)[None, None], (at, 1 - core, 0, 0))
    return whole.reshape(groups * rows, columns)


def gather_weight_ctx(shard):
    rows, columns = shard.shape
    number, groups = lax.axis_size("ctx"), lax.axis_size("fsdp")
    own, me = lax.axis_index("fsdp"), lax.axis_index("ctx")
    chips = ctx_bits()
    half = columns // 2
    parts = shard.reshape(number, rows // number, columns)
    whole = jnp.zeros((groups, number, rows // number, columns), shard.dtype)
    whole = lax.dynamic_update_slice(whole, parts[None], (own, 0, 0, 0))
    piece = lax.dynamic_index_in_dim(parts, me, 0, keepdims=False)
    for step in range(1, groups):
        piece = shift_fsdp(piece, 1)
        at = (own - step) % groups
        left_half = gather_ctx(piece[:, :half], chips + [1])
        right_half = gather_ctx(piece[:, half:], chips[::-1] + [1])
        whole = lax.dynamic_update_slice(whole, left_half[None], (at, 0, 0, 0))
        whole = lax.dynamic_update_slice(whole, right_half[None], (at, 0, 0, half))
    return whole.reshape(groups * rows, columns)


def head_masks(rows):
    lane = lax.broadcasted_iota(jnp.int32, (rows, PAIR), 1)
    first = lane < HEAD_DIM
    return (first, jnp.logical_not(first))


def of_head(pair, mask):
    return jnp.where(mask, pair.astype(F32), 0.0).astype(BF16)


def lane_fold(values, combine):
    width = values.shape[1]
    folded = values[:, :PAIR]
    for at in range(PAIR, width, PAIR):
        folded = combine(folded, values[:, at : at + PAIR])
    return folded


def chunk_of(ref, index):
    part = ref[pl.ds(index * CHUNK_BLOCKS, CHUNK_BLOCKS)]
    return part.reshape(part.shape[0] * part.shape[1], PAIR)


def key_bias(length, index, width):
    place = index * width + lax.broadcasted_iota(jnp.int32, (1, width), 1)
    return jnp.where(place < length, 0.0, -1e30)


def forward_kernel(place_ref, q_ref, k_ref, v_ref, att_ref, low_ref, col_ref, row_ref, scores):
    length = place_ref[1]
    rows = q_ref.shape[1]
    width = CHUNK_BLOCKS * k_ref.shape[1]
    chunks = (length + width - 1) // width
    masks = head_masks(rows)
    queries = q_ref[0]
    split = [of_head(queries, mask) for mask in masks]

    def score_chunk(index, tops):
        keys = chunk_of(k_ref, index)
        bias = key_bias(length, index, width)
        new = []
        for head in range(2):
            part = lax.dot_general(split[head], keys, NT, preferred_element_type=F32) + bias
            scores[head, index] = part
            new.append(jnp.maximum(tops[head], lane_fold(part, jnp.maximum)))
        return tuple(new)

    low_start = jnp.full((rows, PAIR), -1e30, F32)
    tops = lax.fori_loop(0, chunks, score_chunk, (low_start, low_start))
    top = [jnp.max(one, axis=1, keepdims=True) * SCORE for one in tops]

    def weigh_chunk(index, state):
        values = chunk_of(v_ref, index)
        new = []
        for head in range(2):
            summed, weighted = state[head]
            weights = jnp.exp2(scores[head, index] * SCORE - top[head])
            summed = summed + lane_fold(weights, jnp.add)
            weighted = weighted + jnp.dot(
                weights.astype(BF16), values, preferred_element_type=F32
            )
            new.append((summed, weighted))
        return tuple(new)

    zero = jnp.zeros((rows, PAIR), F32)
    state = lax.fori_loop(0, chunks, weigh_chunk, ((zero, zero), (zero, zero)))
    totals = [jnp.sum(state[head][0], axis=1, keepdims=True) for head in range(2)]
    attended = jnp.where(masks[0], state[0][1] / totals[0], state[1][1] / totals[1])
    att_ref[...] = attended
    low_ref[...] = attended.astype(BF16)
    lse = [top[head] + jnp.log2(totals[head]) for head in range(2)]
    column = jnp.where(masks[0], lse[0], lse[1])
    col_ref[...] = column
    turned = jnp.transpose(column)
    row_ref[0, 0:1, :] = turned[0:1, :]
    row_ref[0, 1:2, :] = turned[HEAD_DIM : HEAD_DIM + 1, :]


def query_kernel(place_ref, q_ref, k_ref, v_ref, g_ref, att_ref, col_ref, out_ref):
    length = place_ref[1]
    rows = q_ref.shape[1]
    width = CHUNK_BLOCKS * k_ref.shape[1]
    chunks = (length + width - 1) // width
    masks = head_masks(rows)
    grads = g_ref[...]
    products = grads.astype(F32) * att_ref[...]
    query_split = [of_head(q_ref[0], mask) for mask in masks]
    grad_split = [of_head(grads, mask) for mask in masks]
    delta = [jnp.sum(jnp.where(mask, products, 0.0), axis=1, keepdims=True) for mask in masks]
    lse = [col_ref[:, 0:1], col_ref[:, HEAD_DIM : HEAD_DIM + 1]]

    def chunk(index, totals):
        keys = chunk_of(k_ref, index)
        values = chunk_of(v_ref, index)
        bias = key_bias(length, index, width)
        new = []
        for head in range(2):
            part = lax.dot_general(query_split[head], keys, NT, preferred_element_type=F32)
            weights = jnp.exp2(part * SCORE - lse[head] + bias)
            moved = lax.dot_general(grad_split[head], values, NT, preferred_element_type=F32)
            grad_scores = (weights * (moved - delta[head])).astype(BF16)
            new.append(totals[head] + jnp.dot(grad_scores, keys, preferred_element_type=F32))
        return tuple(new)

    zero = jnp.zeros((rows, PAIR), F32)
    totals = lax.fori_loop(0, chunks, chunk, (zero, zero))
    total = jnp.where(masks[0], totals[0], totals[1])
    out_ref[...] = (total * (1.0 / math.sqrt(HEAD_DIM))).astype(BF16)


def key_kernel(place_ref, k_ref, v_ref, q_ref, g_ref, stat_ref, dk_ref, dv_ref):
    offset, length = place_ref[0] * k_ref.shape[1], place_ref[1]
    rows = k_ref.shape[1]
    chunks = q_ref.shape[0] // CHUNK_BLOCKS
    masks = head_masks(rows)

    @pl.when(offset >= length)
    def _():
        dk_ref[...] = jnp.zeros(dk_ref.shape, BF16)
        dv_ref[...] = jnp.zeros(dv_ref.shape, BF16)

    @pl.when(offset < length)
    def _():
        key_split = [of_head(k_ref[0], mask) for mask in masks]
        value_split = [of_head(v_ref[0], mask) for mask in masks]

        def chunk(index, totals):
            queries = chunk_of(q_ref, index)
            grads = chunk_of(g_ref, index)
            stats = stat_ref[pl.ds(index * CHUNK_BLOCKS, CHUNK_BLOCKS), 0]

            def stat(which):
                return jnp.concatenate(
                    [stats[at, which : which + 1, :] for at in range(CHUNK_BLOCKS)], axis=1
                )

            new = []
            for head in range(2):
                part = lax.dot_general(key_split[head], queries, NT, preferred_element_type=F32)
                weights = jnp.exp2(part * SCORE - stat(head))
                moved = lax.dot_general(value_split[head], grads, NT, preferred_element_type=F32)
                grad_scores = (weights * (moved - stat(2 + head))).astype(BF16)
                grad_keys, grad_values = totals[head]
                grad_keys = grad_keys + jnp.dot(grad_scores, queries, preferred_element_type=F32)
                grad_values = grad_values + jnp.dot(
                    weights.astype(BF16), grads, preferred_element_type=F32
                )
                new.append((grad_keys, grad_values))
            return tuple(new)

        zero = jnp.zeros((rows, PAIR), F32)
        totals = lax.fori_loop(0, chunks, chunk, ((zero, zero), (zero, zero)))
        usable = offset + lax.broadcasted_iota(jnp.int32, (rows, PAIR), 0) < length
        grad_keys = jnp.where(masks[0], totals[0][0], totals[1][0])
        grad_values = jnp.where(masks[0], totals[0][1], totals[1][1])
        grad_keys = grad_keys * (1.0 / math.sqrt(HEAD_DIM))
        dk_ref[...] = jnp.where(usable, grad_keys, 0.0).astype(BF16)
        dv_ref[...] = jnp.where(usable, grad_values, 0.0).astype(BF16)


def kernel_call(body, place, operands, in_specs, outs, out_specs, pairs, scratch, flops):
    return pl.pallas_call(
        body,
        grid_spec=pltpu.PrefetchScalarGridSpec(
            num_scalar_prefetch=1,
            grid=(pairs,),
            in_specs=in_specs,
            out_specs=out_specs,
            scratch_shapes=scratch,
        ),
        out_shape=outs,
        compiler_params=pltpu.CompilerParams(vmem_limit_bytes=48 * 1024 * 1024),
        cost_estimate=pl.CostEstimate(flops=flops, bytes_accessed=10_000_000, transcendentals=0),
    )(place, *operands)


def mix_specs(number, tokens, pairs):
    def own(part):
        return pl.BlockSpec((1, tokens, PAIR), lambda h, place: (place[0], 0, part * pairs + h))

    def every(part):
        return pl.BlockSpec((number, tokens, PAIR), lambda h, place: (0, 0, part * pairs + h))

    return own, every


def attend_forward(place, mix):
    number, tokens, width = mix.shape
    model_width = width // 3
    pairs = model_width // PAIR
    own, every = mix_specs(number, tokens, pairs)
    chunk = CHUNK_BLOCKS * tokens
    block = pl.BlockSpec((tokens, PAIR), lambda h, place: (0, h))
    return kernel_call(
        forward_kernel,
        place,
        (mix, mix, mix),
        [own(0), every(1), every(2)],
        (
            jax.ShapeDtypeStruct((tokens, model_width), F32),
            jax.ShapeDtypeStruct((tokens, model_width), BF16),
            jax.ShapeDtypeStruct((tokens, model_width), F32),
            jax.ShapeDtypeStruct((pairs, 2, tokens), F32),
        ),
        (block, block, block, pl.BlockSpec((1, 2, tokens), lambda h, place: (h, 0, 0))),
        pairs,
        [pltpu.VMEM((2, number // CHUNK_BLOCKS, tokens, chunk), F32)],
        8 * number * tokens * tokens * model_width,
    )


def attend_queries(place, mix, grads, attended, column):
    number, tokens, width = mix.shape
    model_width = width // 3
    pairs = model_width // PAIR
    own, every = mix_specs(number, tokens, pairs)
    block = pl.BlockSpec((tokens, PAIR), lambda h, place: (0, h))
    return kernel_call(
        query_kernel,
        place,
        (mix, mix, mix, grads, attended, column),
        [own(0), every(1), every(2), block, block, block],
        jax.ShapeDtypeStruct((tokens, model_width), BF16),
        block,
        pairs,
        [],
        12 * number * tokens * tokens * model_width,
    )


def attend_keys(place, mix, all_grads, stats):
    number, tokens, width = mix.shape
    model_width = width // 3
    pairs = model_width // PAIR
    own, every = mix_specs(number, tokens, pairs)
    block = pl.BlockSpec((tokens, PAIR), lambda h, place: (0, h))
    return kernel_call(
        key_kernel,
        place,
        (mix, mix, mix, all_grads, stats),
        [
            own(1),
            own(2),
            every(0),
            every(0),
            pl.BlockSpec((number, 1, 4, tokens), lambda h, place: (0, h, 0, 0)),
        ],
        (
            jax.ShapeDtypeStruct((tokens, model_width), BF16),
            jax.ShapeDtypeStruct((tokens, model_width), BF16),
        ),
        (block, block),
        pairs,
        [],
        16 * number * tokens * tokens * model_width,
    )


def on_device(
    hidden_states,
    lengths,
    cotangent,
    attend_weight,
    query_bias,
    value_bias,
    output_weight,
    output_bias,
    first_gain,
    first_shift,
    raise_weight,
    raise_bias,
    lower_weight,
    lower_bias,
    second_gain,
    second_shift,
):
    seq_count, tok_count, model_width = hidden_states.shape
    row_count = seq_count * tok_count
    block_shape = (seq_count, tok_count, model_width)
    number = lax.axis_size("ctx")
    pairs = model_width // PAIR
    me = lax.axis_index("ctx")
    chips = ctx_bits()
    orders = (chips + [1], chips[::-1] + [1])

    def gather_tokens(blocked):
        return [gather_ctx(blocked[at], orders[at % 2]) for at in range(seq_count)]

    tokens_all = gather_tokens(hidden_states)
    attend_full = gather_weight_core(attend_weight)
    (
        query_add,
        value_add,
        output_add,
        gain_first,
        shift_first,
        raise_add,
        lower_add,
        gain_second,
        shift_second,
    ) = gather_vectors(
        [
            query_bias,
            value_bias,
            output_bias,
            first_gain,
            first_shift,
            raise_bias,
            lower_bias,
            second_gain,
            second_shift,
        ]
    )
    output_full = gather_weight_core(output_weight)
    raise_full = gather_weight_ctx(raise_weight)
    lower_full = gather_weight_ctx(lower_weight)

    mix_add = jnp.concatenate([query_add, jnp.zeros_like(query_add), value_add])
    places = [
        jnp.stack([me.astype(jnp.int32), lengths[at].astype(jnp.int32)]) for at in range(seq_count)
    ]
    mixes = []
    for at in range(seq_count):
        mixed = jnp.dot(
            tokens_all[at].reshape(number * tok_count, model_width),
            attend_full,
            preferred_element_type=F32,
        )
        mixes.append((mixed + mix_add).astype(BF16).reshape(number, tok_count, 3 * model_width))
    attended, attended_lows, columns, lse_rows = zip(
        *[attend_forward(places[at], mixes[at]) for at in range(seq_count)]
    )
    attended_low = jnp.concatenate(attended_lows, axis=0)

    token_rows = hidden_states.reshape(row_count, model_width)
    projected = jnp.dot(attended_low, output_full, preferred_element_type=F32) + output_add
    normed_first, first_back = jax.vjp(
        layer_norm, token_rows.astype(F32) + projected, gain_first, shift_first
    )
    first_low = normed_first.astype(BF16)
    raised = jnp.dot(first_low, raise_full, preferred_element_type=F32) + raise_add
    active, gelu_back = jax.vjp(gelu_exact, raised)
    active_low = active.astype(BF16)
    lowered = jnp.dot(active_low, lower_full, preferred_element_type=F32) + lower_add
    result, second_back = jax.vjp(layer_norm, normed_first + lowered, gain_second, shift_second)
    layer_output = result.astype(BF16).reshape(block_shape)
    grad_out = cotangent.reshape(row_count, model_width).astype(F32)
    grad_mid, grad_gain_second, grad_shift_second = second_back(grad_out)
    mid_low = grad_mid.astype(BF16)
    grad_lower_weight = jnp.einsum("rf,rd->fd", active_low, mid_low, preferred_element_type=F32)
    grad_lower_add = jnp.sum(mid_low.astype(F32), axis=0)
    grad_active = jnp.einsum("rd,fd->rf", mid_low, lower_full, preferred_element_type=F32)
    (grad_raised,) = gelu_back(grad_active)
    raised_low = grad_raised.astype(BF16)
    grad_raise_weight = jnp.einsum("rd,rf->df", first_low, raised_low, preferred_element_type=F32)
    grad_raise_add = jnp.sum(raised_low.astype(F32), axis=0)
    grad_first = grad_mid + jnp.einsum(
        "rf,df->rd", raised_low, raise_full, preferred_element_type=F32
    )
    grad_resid, grad_gain_first, grad_shift_first = first_back(grad_first)
    resid_low = grad_resid.astype(BF16)
    grad_output_weight = jnp.einsum(
        "rc,rd->cd", attended_low, resid_low, preferred_element_type=F32
    )
    grad_output_add = jnp.sum(resid_low.astype(F32), axis=0)
    grad_att = (
        jnp.einsum("rd,cd->rc", resid_low, output_full, preferred_element_type=F32)
        .astype(BF16)
        .reshape(block_shape)
    )
    grads_all = gather_tokens(grad_att)
    head_of = lax.broadcasted_iota(jnp.int32, (HEADS, model_width), 1) // HEAD_DIM
    pick = (head_of == lax.broadcasted_iota(jnp.int32, (HEADS, model_width), 0)).astype(F32)
    query_grads, key_grads, value_grads = [], [], []
    stats_all = []
    for at in range(seq_count):
        delta = jnp.einsum(
            "hd,td->ht",
            pick,
            grad_att[at].astype(F32) * attended[at],
            precision=lax.Precision.HIGHEST,
            preferred_element_type=F32,
        ).reshape(pairs, 2, tok_count)
        stats_all.append(
            gather_ctx(jnp.concatenate([lse_rows[at], delta], axis=1), orders[at % 2])
        )
    for at in range(seq_count):
        query_grads.append(
            attend_queries(places[at], mixes[at], grad_att[at], attended[at], columns[at])
        )
    for at in range(seq_count):
        grad_keys, grad_values = attend_keys(places[at], mixes[at], grads_all[at], stats_all[at])
        key_grads.append(grad_keys)
        value_grads.append(grad_values)
    query_low = jnp.concatenate(query_grads, axis=0)
    key_low = jnp.concatenate(key_grads, axis=0)
    value_low = jnp.concatenate(value_grads, axis=0)
    grad_mixture = jnp.concatenate([query_low, key_low, value_low], axis=1)
    grad_attend_weight = jnp.einsum(
        "rd,rc->dc", token_rows, grad_mixture, preferred_element_type=F32
    )
    grad_query_add = jnp.sum(query_low.astype(F32), axis=0)
    grad_value_add = jnp.sum(value_low.astype(F32), axis=0)
    hidden_grad = grad_resid + jnp.einsum(
        "rc,dc->rd", grad_mixture, attend_full, preferred_element_type=F32
    )
    (
        grad_output_add,
        grad_gain_first,
        grad_shift_first,
        grad_raise_add,
        grad_lower_add,
        grad_gain_second,
        grad_shift_second,
    ) = sum_vectors(
        [
            grad_output_add,
            grad_gain_first,
            grad_shift_first,
            grad_raise_add,
            grad_lower_add,
            grad_gain_second,
            grad_shift_second,
        ]
    )
    grad_query_add, grad_value_add = sum_vectors([grad_query_add, grad_value_add])
    return (
        layer_output,
        hidden_grad.reshape(block_shape),
        sum_weight(grad_attend_weight),
        grad_query_add,
        grad_value_add,
        sum_weight(grad_output_weight),
        grad_output_add,
        grad_gain_first,
        grad_shift_first,
        sum_weight(grad_raise_weight),
        grad_raise_add,
        sum_weight(grad_lower_weight),
        grad_lower_add,
        grad_gain_second,
        grad_shift_second,
    )


def solution(mesh):
    return jax.shard_map(
        on_device,
        mesh=mesh,
        in_specs=(
            P("fsdp", "ctx", None),
            P("fsdp"),
            P("fsdp", "ctx", None),
            P("fsdp", None),
            P("fsdp"),
            P("fsdp"),
            P("fsdp", None),
            P("fsdp"),
            P("fsdp"),
            P("fsdp"),
            P("fsdp", None),
            P("fsdp"),
            P("fsdp", None),
            P("fsdp"),
            P("fsdp"),
            P("fsdp"),
        ),
        out_specs=(
            P("fsdp", "ctx", None),
            P("fsdp", "ctx", None),
            P("fsdp", None),
            P("fsdp"),
            P("fsdp"),
            P("fsdp", None),
            P("fsdp"),
            P("fsdp"),
            P("fsdp"),
            P("fsdp", None),
            P("fsdp"),
            P("fsdp", None),
            P("fsdp"),
            P("fsdp"),
            P("fsdp"),
        ),
        check_vma=False,
    )
```

```python
import functools
import math

import jax
import jax.numpy as jnp
from jax import lax
from jax.experimental import pallas as pl
from jax.experimental.pallas import tpu as pltpu
from jax.sharding import PartitionSpec as P

HEADS = 12
HEAD_DIM = 64
PAIR = 2 * HEAD_DIM
LOG2E = 1.4426950408889634
SCORE = LOG2E / math.sqrt(HEAD_DIM)
F32 = jnp.float32
BF16 = jnp.bfloat16
CHUNK_BLOCKS = 2
NT = (((1,), (1,)), ((), ()))
TN = (((0,), (0,)), ((), ()))


def layer_norm(hidden, gain, shift):
    average = jnp.mean(hidden, axis=-1, keepdims=True)
    centred = hidden - average
    variance = jnp.mean(centred * centred, axis=-1, keepdims=True)
    return centred * lax.rsqrt(variance + 1e-05) * gain + shift


def gelu_exact(inputs):
    return jax.nn.gelu(inputs, approximate=False)


def swap(value, bit):
    number = lax.axis_size("ctx")
    return lax.ppermute(value, "ctx", [(at, at ^ bit) for at in range(number)])


def shift_fsdp(value, step):
    number = lax.axis_size("fsdp")
    return lax.ppermute(value, "fsdp", [(at, (at + step) % number) for at in range(number)])


def ctx_bits():
    bits, bit = [], 2
    while bit < lax.axis_size("ctx"):
        bits.append(bit)
        bit *= 2
    return bits


def gather_ctx(piece, order):
    me = lax.axis_index("ctx")
    held, done = piece, []
    for bit in order:
        other = swap(held, bit)
        high = (me & bit) != 0
        place = sum(1 for earlier in done if earlier > bit)
        held = jnp.stack([jnp.where(high, other, held), jnp.where(high, held, other)], axis=place)
        done.append(bit)
    return held.reshape((lax.axis_size("ctx"),) + piece.shape)


def scatter_ctx_step(held, bits_left, bit):
    me = lax.axis_index("ctx")
    high = (me & bit) // bit
    axis = 1 + bits_left.index(bit)
    mine = lax.dynamic_index_in_dim(held, high, axis, keepdims=False)
    send = lax.dynamic_index_in_dim(held, 1 - high, axis, keepdims=False).astype(BF16)
    total = mine.astype(F32) + swap(send, bit).astype(F32)
    return total.astype(BF16), [left for left in bits_left if left != bit]


def sum_weight(partial):
    rows, columns = partial.shape
    number, groups = lax.axis_size("ctx"), lax.axis_size("fsdp")
    own = lax.axis_index("fsdp")
    chips = ctx_bits()
    all_bits = sorted(chips + [1], reverse=True)
    held = partial.reshape((groups,) + (2,) * len(all_bits) + (rows // (groups * number), columns))
    held, left = scatter_ctx_step(held, all_bits, 1)
    half = columns // 2
    pieces = []
    for part, order in ((held[..., :half], chips), (held[..., half:], chips[::-1])):
        part_left = left
        for bit in order:
            part, part_left = scatter_ctx_step(part, part_left, bit)
        pieces.append(part)
    piece = jnp.concatenate(pieces, axis=-1)
    total = lax.dynamic_index_in_dim(piece, own, 0, keepdims=False).astype(F32)
    for step in range(1, groups):
        send = lax.dynamic_index_in_dim(piece, (own + step) % groups, 0, keepdims=False)
        total = total + shift_fsdp(send, step).astype(F32)
    total = total.astype(BF16)
    left_half = gather_ctx(total[:, :half], chips[::-1] + [1])
    right_half = gather_ctx(total[:, half:], chips + [1])
    whole = jnp.concatenate([left_half, right_half], axis=-1)
    return whole.reshape(rows // groups, columns).astype(F32)


def sum_vectors(vectors):
    groups = lax.axis_size("fsdp")
    own = lax.axis_index("fsdp")
    packed = jnp.concatenate([vector.reshape(groups, -1) for vector in vectors], axis=1)
    for bit in [1] + ctx_bits():
        packed = packed + swap(packed, bit)
    total = lax.dynamic_index_in_dim(packed, own, 0, keepdims=False)
    for step in range(1, groups):
        send = lax.dynamic_index_in_dim(packed, (own + step) % groups, 0, keepdims=False)
        total = total + shift_fsdp(send, step)
    owned, at = [], 0
    for vector in vectors:
        width = vector.shape[0] // groups
        owned.append(total[at : at + width])
        at += width
    return owned


def vector_kernel(number, at_ref, *refs):
    rows, (vectors_ref, wide_ref, mix_ref, held) = refs[:-4], refs[-4:]
    groups = len(rows)
    for step in range(groups):
        held[pl.ds(lax.rem(at_ref[1] + groups - step, groups), 1), :] = rows[step][...]
    width = vectors_ref.shape[1] // groups
    wide = wide_ref.shape[1] // groups
    for group in range(groups):
        for at in range(number):
            part = held[group : group + 1, at * width : (at + 1) * width]
            vectors_ref[at : at + 1, group * width : (group + 1) * width] = part
        wide_ref[:, group * wide : (group + 1) * wide] = held[group : group + 1, number * width :]
    model_width = vectors_ref.shape[1]
    mix_ref[...] = jnp.zeros(mix_ref.shape, F32)
    mix_ref[:, :model_width] = vectors_ref[0:1, :]
    mix_ref[:, 2 * model_width :] = vectors_ref[1:2, :]


def gather_vectors(vectors, wide, places):
    groups = lax.axis_size("fsdp")
    packed = jnp.concatenate(vectors + [wide])[None].astype(F32)
    rows = [packed] + [shift_fsdp(packed, step) for step in range(1, groups)]
    model_width, wide_width = groups * vectors[0].shape[0], groups * wide.shape[0]
    vmem = pl.BlockSpec(memory_space=pltpu.VMEM)
    return pl.pallas_call(
        functools.partial(vector_kernel, len(vectors)),
        in_specs=[pl.BlockSpec(memory_space=pltpu.SMEM)] + [vmem] * groups,
        out_specs=[vmem] * 3,
        out_shape=[
            jax.ShapeDtypeStruct((len(vectors), model_width), F32),
            jax.ShapeDtypeStruct((1, wide_width), F32),
            jax.ShapeDtypeStruct((1, 3 * model_width), F32),
        ],
        scratch_shapes=[pltpu.VMEM((groups, packed.shape[1]), F32)],
    )(places, *rows)


def after(values, *signs):
    return lax.optimization_barrier((values, signs))[0]


def spread_chips(block):
    found = {0: block}
    for bit in range(2, lax.axis_size("ctx"), 2):
        found[bit] = swap(block, bit)
    return found


def copy_kernel(plan, count, at_ref, *refs):
    sources, targets = refs[:count], refs[count : count + 1]
    slots, in_sems, out_sems = refs[count + 1 : -2], refs[-2], refs[-1]
    arrivals = []
    for at in range(count):
        arrivals.append(pltpu.make_async_copy(sources[at], slots[at], in_sems.at[at]))
        arrivals[at].start()
    leaving = []
    for at, moves in enumerate(plan(at_ref, slots, targets[0])):
        arrivals[at].wait()
        for source, target in moves:
            leaving.append(pltpu.make_async_copy(source, target, out_sems.at[len(leaving)]))
            leaving[-1].start()
    for copy in leaving:
        copy.wait()


def assemble(places, sources, shape, plan, copies):
    anywhere = pl.BlockSpec(memory_space=pl.ANY)
    return pl.pallas_call(
        functools.partial(copy_kernel, plan, len(sources)),
        in_specs=[pl.BlockSpec(memory_space=pltpu.SMEM)] + [anywhere] * len(sources),
        out_specs=anywhere,
        out_shape=shape,
        scratch_shapes=[pltpu.VMEM(source.shape, source.dtype) for source in sources]
        + [pltpu.SemaphoreType.DMA((len(sources),)), pltpu.SemaphoreType.DMA((copies,))],
        compiler_params=pltpu.CompilerParams(vmem_limit_bytes=32 * 1024 * 1024),
        cost_estimate=pl.CostEstimate(flops=0, bytes_accessed=10_000_000, transcendentals=0),
    )(places, *sources)


def shift_all(piece):
    return {step: shift_fsdp(piece, step) for step in range(1, lax.axis_size("fsdp"))}


def row_of_step(own, step, rows):
    groups = lax.axis_size("fsdp")
    return pl.ds(lax.rem(own + groups - step, groups) * rows, rows)


def halves_plan(rows, half):
    groups = lax.axis_size("fsdp")

    def plan(at_ref, slots, target):
        own, core_at = at_ref[1], at_ref[0] & 1
        moves = [[(slots[0], target.at[pl.ds(own * rows, rows)])]]
        for at, side in ((1, core_at), (2, 1 - core_at)):
            column = pl.ds(pl.multiple_of(side * half, 128), half)
            moves.append(
                [
                    (slots[at].at[step - 1], target.at[row_of_step(own, step, rows), column])
                    for step in range(1, groups)
                ]
            )
        return moves

    return plan


def core_half(shard):
    rows, columns = shard.shape
    core = lax.axis_index("ctx") % 2
    return lax.dynamic_slice(shard, (0, core * (columns // 2)), (rows, columns // 2))


def stack_steps(fetched):
    return jnp.stack([fetched[step] for step in sorted(fetched)])


def whole_of_halves(shard, mine, theirs, places):
    rows, columns = shard.shape
    groups = lax.axis_size("fsdp")
    shape = jax.ShapeDtypeStruct((groups * rows, columns), shard.dtype)
    plan = halves_plan(rows, columns // 2)
    return assemble(places, [shard, mine, theirs], shape, plan, 2 * groups - 1)


def weight_by_core(shard, places):
    piece = core_half(shard)
    sign = yield piece
    fetched = shift_all(piece)
    if sign is not None:
        fetched = after(fetched, sign)
    mine = stack_steps(fetched)
    yield whole_of_halves(shard, mine, swap(mine, 1), places)


def two_weights_by_ctx(shard, second, places):
    rows, columns = shard.shape
    number, groups = lax.axis_size("ctx"), lax.axis_size("fsdp")
    me = lax.axis_index("ctx")
    width = columns // number
    piece = lax.dynamic_slice(shard, (0, me * width), (rows, width))
    pieces = jnp.stack([piece, core_half(second)])
    sign = yield pieces
    fetched = shift_all(pieces)
    if sign is not None:
        fetched = after(fetched, sign)
    fetched = stack_steps(fetched)
    stack, mine = fetched[:, 0], fetched[:, 1]
    sign = yield stack
    near = spread_chips(stack)
    near_bits = sorted(near)
    near_list = after([near[bit] for bit in near_bits], sign)
    across = swap(jnp.stack(near_list + [mine]), 1)
    yield across

    def plan(at_ref, slots, target):
        own, at = at_ref[1], at_ref[0]

        def moves_of(slot, other):
            column = pl.ds(pl.multiple_of(other * width, 128), width)
            return [
                (slot.at[step - 1], target.at[row_of_step(own, step, rows), column])
                for step in range(1, groups)
            ]

        moves = [moves_of(slots[index], at ^ bit) for index, bit in enumerate(near_bits)]
        last = []
        for index, bit in enumerate(near_bits):
            last += moves_of(slots[-2].at[index], at ^ bit ^ 1)
        return moves + [last, [(slots[-1], target.at[pl.ds(own * rows, rows)])]]

    shape = jax.ShapeDtypeStruct((groups * rows, columns), shard.dtype)
    whole = assemble(
        places, near_list + [across, shard], shape, plan, number * (groups - 1) + 1
    )
    yield whole, whole_of_halves(second, mine, across[-1], places)


def stacked_pieces(grad, blocks):
    groups, chips = lax.axis_size("fsdp"), lax.axis_size("ctx") // 2
    rows, width = grad.shape[0], grad.shape[1] // blocks
    parts = [
        grad[:, at * width : (at + 1) * width].reshape(
            groups, chips, 2, rows // (2 * groups * chips), width
        )
        for at in range(blocks)
    ]
    return jnp.concatenate(parts, axis=3)


def pieces_of(grad, column_blocks):
    groups, chips = lax.axis_size("fsdp"), lax.axis_size("ctx") // 2
    rows, columns = grad.shape
    if column_blocks < 0:
        return stacked_pieces(grad, -column_blocks)
    if column_blocks == 1:
        return grad.reshape(groups, chips, 2, rows // (2 * groups * chips), columns)
    width = columns // chips
    viewed = jnp.stack([grad[:, at * width : (at + 1) * width] for at in range(chips)])
    viewed = viewed.reshape(chips, groups, 2, rows // (2 * groups), width)
    return jnp.swapaxes(viewed, 0, 1)


VECTOR_ROWS = 8


def finish_kernel(near_bits, parts, at_ref, *refs):
    me = at_ref[0]
    sources, outs = refs[: len(near_bits) + 1], refs[len(near_bits) + 1 :]

    def put(values, other):
        first = 0
        for out_ref, (rows, column_blocks) in zip(outs, parts):
            part = values[first : first + rows]
            width = part.shape[1]
            if column_blocks < 0:
                each = rows // -column_blocks
                row = pl.ds(pl.multiple_of(other * each, 8), each)
                for at in range(-column_blocks):
                    piece = part[at * each : (at + 1) * each]
                    out_ref[row, at * width : (at + 1) * width] = piece
            elif column_blocks == 1:
                out_ref[pl.ds(pl.multiple_of(other * rows, 8), rows), :] = part
            else:
                row = pl.ds(pl.multiple_of((other & 1) * rows, 8), rows)
                out_ref[row, pl.ds(pl.multiple_of((other >> 1) * width, 128), width)] = part
            first += rows

    for index, bit in enumerate(near_bits):
        put(sources[index][...].astype(F32), me ^ bit)
        put(sources[-1][index].astype(F32), me ^ bit ^ 1)


def sum_pack(grads, blocks, vectors, places):
    number, groups = lax.axis_size("ctx"), lax.axis_size("fsdp")
    me, own = lax.axis_index("ctx"), lax.axis_index("fsdp")
    core, chip, chips = me % 2, me // 2, number // 2
    views = [pieces_of(grad, block) for grad, block in zip(grads, blocks)]
    width = views[0].shape[4]
    if vectors:
        rows = [vector.reshape(groups, 1, -1) for vector in vectors]
        rows = [jnp.pad(row, ((0, 0), (0, 0), (0, width - row.shape[2]))) for row in rows]
        rows += [jnp.zeros_like(rows[0])] * (number - len(rows))
        view = jnp.concatenate(rows, axis=1).astype(BF16)
        view = view.reshape(groups, chips, 2, 1, width)
        views.append(jnp.pad(view, ((0, 0), (0, 0), (0, 0), (0, VECTOR_ROWS - 1), (0, 0))))

    def side(which):
        parts = [
            jnp.swapaxes(lax.dynamic_index_in_dim(view, which, 2, keepdims=False), 0, 1)
            for view in views
        ]
        return jnp.concatenate(parts, axis=2) if len(parts) > 1 else parts[0]

    send = side(1 - core)
    sign = yield send
    other = swap(send, 1)
    if sign is not None:
        other = after(other, sign)
    held = (side(core).astype(F32) + other.astype(F32)).astype(BF16)

    def chip_part(at):
        return lax.dynamic_index_in_dim(held, at, 0, keepdims=False)

    sends = [chip_part(chip ^ (bit // 2)) for bit in range(2, number, 2)]
    sign = yield sends
    others = [swap(send, bit) for send, bit in zip(sends, range(2, number, 2))]
    if sign is not None:
        others = after(others, sign)
    total = chip_part(chip).astype(F32)
    for other in others:
        total = total + other.astype(F32)
    piece = total.astype(BF16)
    sends = [
        lax.dynamic_index_in_dim(piece, (own + step) % groups, 0, keepdims=False)
        for step in range(1, groups)
    ]
    sign = yield sends
    others = [shift_fsdp(send, step) for send, step in zip(sends, range(1, groups))]
    if sign is not None:
        others = after(others, sign)
    total = lax.dynamic_index_in_dim(piece, own, 0, keepdims=False).astype(F32)
    for other in others:
        total = total + other.astype(F32)
    total = total.astype(BF16)
    yield total
    near = spread_chips(total)
    near_bits = sorted(near)
    stack = jnp.stack([near[bit] for bit in near_bits])
    yield stack
    across = swap(stack, 1)
    parts = [(view.shape[3], block) for view, block in zip(views, list(blocks) + [1])]
    shapes = [
        jax.ShapeDtypeStruct((grad.shape[0] // groups, grad.shape[1]), F32) for grad in grads
    ]
    if vectors:
        shapes.append(jax.ShapeDtypeStruct((number * VECTOR_ROWS, width), F32))
    vmem = pl.BlockSpec(memory_space=pltpu.VMEM)
    sums = pl.pallas_call(
        functools.partial(finish_kernel, near_bits, parts),
        in_specs=[pl.BlockSpec(memory_space=pltpu.SMEM)] + [vmem] * (len(near_bits) + 1),
        out_specs=[vmem] * len(shapes),
        out_shape=shapes,
        compiler_params=pltpu.CompilerParams(vmem_limit_bytes=32 * 1024 * 1024),
    )(places, *[near[bit] for bit in near_bits], across)
    owned = [
        sums[-1][at * VECTOR_ROWS, : vector.shape[0] // groups]
        for at, vector in enumerate(vectors)
    ]
    yield list(sums[: len(grads)]), owned


def head_masks(rows):
    lane = lax.broadcasted_iota(jnp.int32, (rows, PAIR), 1)
    first = lane < HEAD_DIM
    return (first, jnp.logical_not(first))


def of_head(pair, mask):
    return jnp.where(mask, pair.astype(F32), 0.0).astype(BF16)


def lane_fold(values, combine):
    width = values.shape[1]
    folded = values[:, :PAIR]
    for at in range(PAIR, width, PAIR):
        folded = combine(folded, values[:, at : at + PAIR])
    return folded


def chunk_of(ref, index):
    part = ref[pl.ds(index * CHUNK_BLOCKS, CHUNK_BLOCKS)]
    return part.reshape(part.shape[0] * part.shape[1], PAIR)


def key_bias(length, index, width):
    place = index * width + lax.broadcasted_iota(jnp.int32, (1, width), 1)
    return jnp.where(place < length, 0.0, -1e30)


def forward_kernel(place_ref, q_ref, k_ref, v_ref, att_ref, low_ref, col_ref, row_ref, scores):
    length = place_ref[1]
    rows = q_ref.shape[1]
    width = CHUNK_BLOCKS * k_ref.shape[1]
    chunks = (length + width - 1) // width
    masks = head_masks(rows)
    queries = q_ref[0]
    split = [of_head(queries, mask) for mask in masks]

    def score_chunk(index, tops):
        keys = chunk_of(k_ref, index)
        bias = key_bias(length, index, width)
        new = []
        for head in range(2):
            part = lax.dot_general(split[head], keys, NT, preferred_element_type=F32) + bias
            scores[head, index] = part
            new.append(jnp.maximum(tops[head], lane_fold(part, jnp.maximum)))
        return tuple(new)

    low_start = jnp.full((rows, PAIR), -1e30, F32)
    tops = lax.fori_loop(0, chunks, score_chunk, (low_start, low_start))
    top = [jnp.max(one, axis=1, keepdims=True) * SCORE for one in tops]

    def weigh_chunk(index, state):
        values = chunk_of(v_ref, index)
        new = []
        for head in range(2):
            summed, weighted = state[head]
            weights = jnp.exp2(scores[head, index] * SCORE - top[head])
            summed = summed + lane_fold(weights, jnp.add)
            weighted = weighted + jnp.dot(
                weights.astype(BF16), values, preferred_element_type=F32
            )
            new.append((summed, weighted))
        return tuple(new)

    zero = jnp.zeros((rows, PAIR), F32)
    state = lax.fori_loop(0, chunks, weigh_chunk, ((zero, zero), (zero, zero)))
    totals = [jnp.sum(state[head][0], axis=1, keepdims=True) for head in range(2)]
    attended = jnp.where(masks[0], state[0][1] / totals[0], state[1][1] / totals[1])
    att_ref[...] = attended
    low_ref[...] = attended.astype(BF16)
    lse = [top[head] + jnp.log2(totals[head]) for head in range(2)]
    column = jnp.where(masks[0], lse[0], lse[1])
    col_ref[...] = column
    turned = jnp.transpose(column)
    row_ref[0, 0:1, :] = turned[0:1, :]
    row_ref[0, 1:2, :] = turned[HEAD_DIM : HEAD_DIM + 1, :]


def query_kernel(place_ref, q_ref, k_ref, v_ref, g_ref, att_ref, col_ref, out_ref):
    length = place_ref[1]
    rows = q_ref.shape[1]
    width = CHUNK_BLOCKS * k_ref.shape[1]
    chunks = (length + width - 1) // width
    masks = head_masks(rows)
    grads = g_ref[...]
    products = grads.astype(F32) * att_ref[...]
    query_split = [of_head(q_ref[0], mask) for mask in masks]
    grad_split = [of_head(grads, mask) for mask in masks]
    delta = [jnp.sum(jnp.where(mask, products, 0.0), axis=1, keepdims=True) for mask in masks]
    lse = [col_ref[:, 0:1], col_ref[:, HEAD_DIM : HEAD_DIM + 1]]

    def chunk(index, totals):
        keys = chunk_of(k_ref, index)
        values = chunk_of(v_ref, index)
        bias = key_bias(length, index, width)
        new = []
        for head in range(2):
            part = lax.dot_general(query_split[head], keys, NT, preferred_element_type=F32)
            weights = jnp.exp2(part * SCORE - lse[head] + bias)
            moved = lax.dot_general(grad_split[head], values, NT, preferred_element_type=F32)
            grad_scores = (weights * (moved - delta[head])).astype(BF16)
            new.append(totals[head] + jnp.dot(grad_scores, keys, preferred_element_type=F32))
        return tuple(new)

    zero = jnp.zeros((rows, PAIR), F32)
    totals = lax.fori_loop(0, chunks, chunk, (zero, zero))
    total = jnp.where(masks[0], totals[0], totals[1])
    out_ref[...] = (total * (1.0 / math.sqrt(HEAD_DIM))).astype(BF16)


def key_kernel(place_ref, k_ref, v_ref, q_ref, g_ref, stat_ref, dk_ref, dv_ref):
    offset, length = place_ref[0] * k_ref.shape[1], place_ref[1]
    rows = k_ref.shape[1]
    chunks = q_ref.shape[0] // CHUNK_BLOCKS
    masks = head_masks(rows)

    @pl.when(offset >= length)
    def _():
        dk_ref[...] = jnp.zeros(dk_ref.shape, BF16)
        dv_ref[...] = jnp.zeros(dv_ref.shape, BF16)

    @pl.when(offset < length)
    def _():
        key_split = [of_head(k_ref[0], mask) for mask in masks]
        value_split = [of_head(v_ref[0], mask) for mask in masks]

        def chunk(index, totals):
            queries = chunk_of(q_ref, index)
            grads = chunk_of(g_ref, index)
            stats = stat_ref[pl.ds(index * CHUNK_BLOCKS, CHUNK_BLOCKS), 0]

            def stat(which):
                return jnp.concatenate(
                    [stats[at, which : which + 1, :] for at in range(CHUNK_BLOCKS)], axis=1
                )

            new = []
            for head in range(2):
                part = lax.dot_general(key_split[head], queries, NT, preferred_element_type=F32)
                weights = jnp.exp2(part * SCORE - stat(head))
                moved = lax.dot_general(value_split[head], grads, NT, preferred_element_type=F32)
                grad_scores = (weights * (moved - stat(2 + head))).astype(BF16)
                grad_keys, grad_values = totals[head]
                grad_keys = grad_keys + jnp.dot(grad_scores, queries, preferred_element_type=F32)
                grad_values = grad_values + jnp.dot(
                    weights.astype(BF16), grads, preferred_element_type=F32
                )
                new.append((grad_keys, grad_values))
            return tuple(new)

        zero = jnp.zeros((rows, PAIR), F32)
        totals = lax.fori_loop(0, chunks, chunk, ((zero, zero), (zero, zero)))
        usable = offset + lax.broadcasted_iota(jnp.int32, (rows, PAIR), 0) < length
        grad_keys = jnp.where(masks[0], totals[0][0], totals[1][0])
        grad_values = jnp.where(masks[0], totals[0][1], totals[1][1])
        grad_keys = grad_keys * (1.0 / math.sqrt(HEAD_DIM))
        dk_ref[...] = jnp.where(usable, grad_keys, 0.0).astype(BF16)
        dv_ref[...] = jnp.where(usable, grad_values, 0.0).astype(BF16)


def kernel_call(body, place, operands, in_specs, outs, out_specs, pairs, scratch, flops):
    return pl.pallas_call(
        body,
        grid_spec=pltpu.PrefetchScalarGridSpec(
            num_scalar_prefetch=1,
            grid=(pairs,),
            in_specs=in_specs,
            out_specs=out_specs,
            scratch_shapes=scratch,
        ),
        out_shape=outs,
        compiler_params=pltpu.CompilerParams(vmem_limit_bytes=48 * 1024 * 1024),
        cost_estimate=pl.CostEstimate(flops=flops, bytes_accessed=10_000_000, transcendentals=0),
    )(place, *operands)


def mix_specs(number, seq, tokens, pairs):
    def own(part):
        return pl.BlockSpec(
            (1, None, tokens, PAIR), lambda h, place: (place[0], seq, 0, part * pairs + h)
        )

    def every(part):
        return pl.BlockSpec(
            (number, None, tokens, PAIR), lambda h, place: (0, seq, 0, part * pairs + h)
        )

    return own, every


def mix_kernel(x_ref, weight_ref, add_ref, out_ref):
    for at in range(x_ref.shape[0]):
        mixed = jnp.dot(x_ref[at], weight_ref[...], preferred_element_type=F32)
        out_ref[at] = (mixed + add_ref[...]).astype(BF16)


def mix_tokens(tokens_all, weight, add):
    number, seqs, tokens, model_width = tokens_all.shape
    width = weight.shape[1]
    return pl.pallas_call(
        mix_kernel,
        grid=(number,),
        in_specs=[
            pl.BlockSpec((None, seqs, tokens, model_width), lambda at: (at, 0, 0, 0)),
            pl.BlockSpec((model_width, width), lambda at: (0, 0)),
            pl.BlockSpec((1, width), lambda at: (0, 0)),
        ],
        out_specs=pl.BlockSpec((None, seqs, tokens, width), lambda at: (at, 0, 0, 0)),
        out_shape=jax.ShapeDtypeStruct((number, seqs, tokens, width), BF16),
        compiler_params=pltpu.CompilerParams(vmem_limit_bytes=48 * 1024 * 1024),
        cost_estimate=pl.CostEstimate(
            flops=2 * number * seqs * tokens * model_width * width,
            bytes_accessed=2 * number * seqs * tokens * (model_width + width),
            transcendentals=0,
        ),
    )(tokens_all, weight, add)


def outer_kernel(left_ref, right_ref, out_ref):
    out_ref[...] = lax.dot_general(
        left_ref[...], right_ref[...], TN, preferred_element_type=F32
    ).astype(BF16)


def outer_products(left, parts):
    rows, model_width = left.shape
    number, _, columns = parts.shape
    return pl.pallas_call(
        outer_kernel,
        grid=(number,),
        in_specs=[
            pl.BlockSpec((rows, model_width), lambda at: (0, 0)),
            pl.BlockSpec((None, rows, columns), lambda at: (at, 0, 0)),
        ],
        out_specs=pl.BlockSpec((model_width, columns), lambda at: (0, at)),
        out_shape=jax.ShapeDtypeStruct((model_width, number * columns), BF16),
        compiler_params=pltpu.CompilerParams(vmem_limit_bytes=48 * 1024 * 1024),
        cost_estimate=pl.CostEstimate(
            flops=2 * model_width * rows * number * columns,
            bytes_accessed=6_000_000,
            transcendentals=0,
        ),
    )(left, parts)


def attend_forward(place, seq, mix):
    number, _, tokens, width = mix.shape
    model_width = width // 3
    pairs = model_width // PAIR
    own, every = mix_specs(number, seq, tokens, pairs)
    chunk = CHUNK_BLOCKS * tokens
    block = pl.BlockSpec((tokens, PAIR), lambda h, place: (0, h))
    return kernel_call(
        forward_kernel,
        place,
        (mix, mix, mix),
        [own(0), every(1), every(2)],
        (
            jax.ShapeDtypeStruct((tokens, model_width), F32),
            jax.ShapeDtypeStruct((tokens, model_width), BF16),
            jax.ShapeDtypeStruct((tokens, model_width), F32),
            jax.ShapeDtypeStruct((pairs, 2, tokens), F32),
        ),
        (block, block, block, pl.BlockSpec((1, 2, tokens), lambda h, place: (h, 0, 0))),
        pairs,
        [pltpu.VMEM((2, number // CHUNK_BLOCKS, tokens, chunk), F32)],
        56 * number * tokens * tokens * model_width,
    )


def attend_queries(place, seq, mix, grads, attended, column):
    number, _, tokens, width = mix.shape
    model_width = width // 3
    pairs = model_width // PAIR
    own, every = mix_specs(number, seq, tokens, pairs)
    block = pl.BlockSpec((tokens, PAIR), lambda h, place: (0, h))
    return kernel_call(
        query_kernel,
        place,
        (mix, mix, mix, grads, attended, column),
        [own(0), every(1), every(2), block, block, block],
        jax.ShapeDtypeStruct((tokens, model_width), BF16),
        block,
        pairs,
        [],
        56 * number * tokens * tokens * model_width,
    )


def attend_keys(place, seq, mix, all_grads, stats):
    number, _, tokens, width = mix.shape
    model_width = width // 3
    pairs = model_width // PAIR
    own, every = mix_specs(number, seq, tokens, pairs)
    block = pl.BlockSpec((tokens, PAIR), lambda h, place: (0, h))
    return kernel_call(
        key_kernel,
        place,
        (mix, mix, mix, all_grads, stats),
        [
            own(1),
            own(2),
            every(0),
            pl.BlockSpec((number, None, tokens, PAIR), lambda h, place: (0, seq, 0, h)),
            pl.BlockSpec((number, None, 1, 4, tokens), lambda h, place: (0, seq, h, 0, 0)),
        ],
        (
            jax.ShapeDtypeStruct((tokens, model_width), BF16),
            jax.ShapeDtypeStruct((tokens, model_width), BF16),
        ),
        (block, block),
        pairs,
        [],
        72 * number * tokens * tokens * model_width,
    )


def on_device(
    hidden_states,
    lengths,
    cotangent,
    attend_weight,
    query_bias,
    value_bias,
    output_weight,
    output_bias,
    first_gain,
    first_shift,
    raise_weight,
    raise_bias,
    lower_weight,
    lower_bias,
    second_gain,
    second_shift,
):
    seq_count, tok_count, model_width = hidden_states.shape
    row_count = seq_count * tok_count
    block_shape = (seq_count, tok_count, model_width)
    number = lax.axis_size("ctx")
    pairs = model_width // PAIR
    me = lax.axis_index("ctx")
    places = jnp.stack([me, lax.axis_index("fsdp")]).astype(jnp.int32)

    tokens_all = lax.all_gather(hidden_states, "ctx", axis=0, tiled=False)
    attend_stages = weight_by_core(attend_weight, places)
    attend_piece = next(attend_stages)
    attend_full = attend_stages.send(None)
    attend_sign = attend_full
    packed = (raise_weight.shape[1] // number) == output_weight.shape[1] // 2
    vectors = after(
        [
            query_bias,
            value_bias,
            output_bias,
            first_gain,
            first_shift,
            lower_bias,
            second_gain,
            second_shift,
        ],
        attend_piece,
    )
    vector_rows, raise_add, mix_add = gather_vectors(vectors, raise_bias, places)
    output_add, gain_first, shift_first, lower_add, gain_second, shift_second = [
        vector_rows[at : at + 1] for at in range(2, 8)
    ]
    if packed:
        raise_stages = two_weights_by_ctx(
            after(raise_weight, attend_sign), output_weight, places
        )
        raise_sign = next(raise_stages)
        lower_stages = weight_by_core(after(lower_weight, raise_sign), places)
        tokens_all = after(tokens_all, raise_sign)
        lower_sign = next(lower_stages)
    else:
        raise_stages = weight_by_core(raise_weight, places)
        output_stages = weight_by_core(output_weight, places)
        lower_stages = weight_by_core(lower_weight, places)
        next(lower_stages)
        next(raise_stages)
        next(output_stages)

    seq_places = [
        jnp.stack([me.astype(jnp.int32), lengths[at].astype(jnp.int32)]) for at in range(seq_count)
    ]
    mix = mix_tokens(tokens_all, attend_full, mix_add)
    attended, attended_lows, columns, lse_rows = [], [], [], []
    for at in range(seq_count):
        if packed and at == 0:
            raise_sign = raise_stages.send(mix)
            mix = after(mix, raise_sign, lower_sign)
        if packed and at == 1:
            raise_sign = raise_stages.send(attended_lows[0])
            mix = after(mix, raise_sign)
        one, low, column, lse_row = attend_forward(seq_places[at], at, mix)
        attended.append(one)
        attended_lows.append(low)
        columns.append(column)
        lse_rows.append(lse_row)
    if packed:
        raise_full, output_full = next(raise_stages)
    else:
        raise_full, output_full = raise_stages.send(None), output_stages.send(None)
    attended_low = jnp.concatenate(attended_lows, axis=0)

    token_rows = hidden_states.reshape(row_count, model_width)
    projected = jnp.dot(attended_low, output_full, preferred_element_type=F32) + output_add
    normed_first, first_back = jax.vjp(
        layer_norm, token_rows.astype(F32) + projected, gain_first, shift_first
    )
    first_low = normed_first.astype(BF16)
    raised = jnp.dot(first_low, raise_full, preferred_element_type=F32) + raise_add
    active, gelu_back = jax.vjp(gelu_exact, raised)
    active_low = active.astype(BF16)
    lower_full = lower_stages.send(first_low)
    lowered = jnp.dot(active_low, lower_full, preferred_element_type=F32) + lower_add
    result, second_back = jax.vjp(layer_norm, normed_first + lowered, gain_second, shift_second)
    layer_output = result.astype(BF16).reshape(block_shape)
    grad_out = cotangent.reshape(row_count, model_width).astype(F32)
    grad_mid, grad_gain_second, grad_shift_second = second_back(grad_out)
    grad_gain_second, grad_shift_second = grad_gain_second[0], grad_shift_second[0]
    mid_low = grad_mid.astype(BF16)
    shared = model_width % (8 * number * lax.axis_size("fsdp")) == 0
    grad_lower_weight = jnp.einsum("rf,rd->fd", active_low, mid_low, preferred_element_type=F32).astype(BF16)
    if shared:
        lower_pack = sum_pack([grad_lower_weight], [1], [], places)
        mid_low = after(mid_low, next(lower_pack))
    grad_lower_add = jnp.sum(mid_low.astype(F32), axis=0)
    grad_active = jnp.einsum("rd,fd->rf", mid_low, lower_full, preferred_element_type=F32)
    (grad_raised,) = gelu_back(grad_active)
    raised_low = grad_raised.astype(BF16)
    grad_raise_weight = jnp.einsum("rd,rf->df", first_low, raised_low, preferred_element_type=F32).astype(BF16)
    grad_raise_add = jnp.sum(raised_low.astype(F32), axis=0)
    grad_first = grad_mid + jnp.einsum(
        "rf,df->rd", raised_low, raise_full, preferred_element_type=F32
    )
    grad_resid, grad_gain_first, grad_shift_first = first_back(grad_first)
    grad_gain_first, grad_shift_first = grad_gain_first[0], grad_shift_first[0]
    resid_low = grad_resid.astype(BF16)
    grad_output_weight = jnp.einsum(
        "rc,rd->cd", attended_low, resid_low, preferred_element_type=F32
    ).astype(BF16)
    grad_output_add = jnp.sum(resid_low.astype(F32), axis=0)
    grad_att = (
        jnp.einsum("rd,cd->rc", resid_low, output_full, preferred_element_type=F32)
        .astype(BF16)
        .reshape(block_shape)
    )
    grads_all = lax.all_gather(grad_att, "ctx", axis=0, tiled=False)
    head_of = lax.broadcasted_iota(jnp.int32, (HEADS, model_width), 1) // HEAD_DIM
    pick = (head_of == lax.broadcasted_iota(jnp.int32, (HEADS, model_width), 0)).astype(F32)
    stats = []
    for at in range(seq_count):
        delta = jnp.einsum(
            "hd,td->ht",
            pick,
            grad_att[at].astype(F32) * attended[at],
            precision=lax.Precision.HIGHEST,
            preferred_element_type=F32,
        ).reshape(pairs, 2, tok_count)
        stats.append(jnp.concatenate([lse_rows[at], delta], axis=1))
    stats = jnp.stack(stats)
    stats_all = lax.all_gather(stats, "ctx", axis=0, tiled=False)
    early = [
        grad_output_add,
        grad_gain_first,
        grad_shift_first,
        grad_raise_add,
        grad_lower_add,
        grad_gain_second,
        grad_shift_second,
    ]
    query_grads, key_grads, value_grads = [], [], []
    if shared:
        raise_pack = sum_pack(
            [grad_raise_weight, grad_output_weight], [number // 2, 1], early, places
        )
        mix = after(mix, lower_pack.send(grad_att), next(raise_pack))
    for at in range(seq_count):
        query_grads.append(
            attend_queries(seq_places[at], at, mix, grad_att[at], attended[at], columns[at])
        )
        if shared and at == 0:
            mix = after(mix, raise_pack.send(query_grads[0]))
    if shared:
        mix = after(mix, lower_pack.send(query_grads[-1]))
    for at in range(seq_count):
        grad_keys, grad_values = attend_keys(seq_places[at], at, mix, grads_all, stats_all)
        key_grads.append(grad_keys)
        value_grads.append(grad_values)
        if shared and at == 0:
            mix = after(mix, raise_pack.send(grad_keys), lower_pack.send(grad_keys))
    if shared:
        value_grads[-1] = after(
            value_grads[-1], raise_pack.send(value_grads[-1]), next(lower_pack)
        )
    query_low = jnp.concatenate(query_grads, axis=0)
    key_low = jnp.concatenate(key_grads, axis=0)
    value_low = jnp.concatenate(value_grads, axis=0)
    grad_mixture = jnp.concatenate([query_low, key_low, value_low], axis=1)
    grad_attend_weight = outer_products(
        token_rows, jnp.stack([query_low, key_low, value_low])
    )
    grad_query_add = jnp.sum(query_low.astype(F32), axis=0)
    grad_value_add = jnp.sum(value_low.astype(F32), axis=0)
    hidden_grad = grad_resid + jnp.einsum(
        "rc,dc->rd", grad_mixture, attend_full, preferred_element_type=F32
    )
    late = [grad_query_add, grad_value_add]
    if shared:
        attend_pack = sum_pack([grad_attend_weight], [-3], late, places)
        next(attend_pack)
        for _ in range(4):
            attend_pack.send(None)
        (grad_attend_weight,), late = next(attend_pack)
        next(raise_pack)
        (grad_lower_weight,), _ = next(lower_pack)
        (grad_raise_weight, grad_output_weight), early = next(raise_pack)
    else:
        grad_lower_weight = sum_weight(grad_lower_weight)
        grad_raise_weight = sum_weight(grad_raise_weight)
        grad_output_weight = sum_weight(grad_output_weight)
        grad_attend_weight = sum_weight(grad_attend_weight)
        early, late = sum_vectors(early), sum_vectors(late)
    (
        grad_output_add,
        grad_gain_first,
        grad_shift_first,
        grad_raise_add,
        grad_lower_add,
        grad_gain_second,
        grad_shift_second,
    ) = early
    grad_query_add, grad_value_add = late
    return (
        layer_output,
        hidden_grad.reshape(block_shape),
        grad_attend_weight,
        grad_query_add,
        grad_value_add,
        grad_output_weight,
        grad_output_add,
        grad_gain_first,
        grad_shift_first,
        grad_raise_weight,
        grad_raise_add,
        grad_lower_weight,
        grad_lower_add,
        grad_gain_second,
        grad_shift_second,
    )


def solution(mesh):
    return jax.shard_map(
        on_device,
        mesh=mesh,
        in_specs=(
            P("fsdp", "ctx", None),
            P("fsdp"),
            P("fsdp", "ctx", None),
            P("fsdp", None),
            P("fsdp"),
            P("fsdp"),
            P("fsdp", None),
            P("fsdp"),
            P("fsdp"),
            P("fsdp"),
            P("fsdp", None),
            P("fsdp"),
            P("fsdp", None),
            P("fsdp"),
            P("fsdp"),
            P("fsdp"),
        ),
        out_specs=(
            P("fsdp", "ctx", None),
            P("fsdp", "ctx", None),
            P("fsdp", None),
            P("fsdp"),
            P("fsdp"),
            P("fsdp", None),
            P("fsdp"),
            P("fsdp"),
            P("fsdp"),
            P("fsdp", None),
            P("fsdp"),
            P("fsdp", None),
            P("fsdp"),
            P("fsdp"),
            P("fsdp"),
        ),
        check_vma=False,
    )
```

```python
import functools
import math

import jax
import jax.numpy as jnp
from jax import lax
from jax.experimental import pallas as pl
from jax.experimental.pallas import tpu as pltpu
from jax.sharding import PartitionSpec as P

HEADS = 12
HEAD_DIM = 64
PAIR = 2 * HEAD_DIM
LOG2E = 1.4426950408889634
SCORE = LOG2E / math.sqrt(HEAD_DIM)
F32 = jnp.float32
BF16 = jnp.bfloat16
CHUNK_BLOCKS = 2
NT = (((1,), (1,)), ((), ()))
TN = (((0,), (0,)), ((), ()))


def layer_norm(hidden, gain, shift):
    average = jnp.mean(hidden, axis=-1, keepdims=True)
    centred = hidden - average
    variance = jnp.mean(centred * centred, axis=-1, keepdims=True)
    return centred * lax.rsqrt(variance + 1e-05) * gain + shift


def gelu_and_slope(inputs):
    size = jnp.abs(inputs) * math.sqrt(0.5)
    bell = jnp.exp(-0.5 * inputs * inputs)
    step = 1.0 / (1.0 + 0.3275911 * size)
    series = 1.061405429 * step - 1.453152027
    series = series * step + 1.421413741
    series = series * step - 0.284496736
    series = series * step + 0.254829592
    tail = 0.5 * series * step * bell
    below = jnp.where(inputs < 0.0, tail, 1.0 - tail)
    return inputs * below, below + inputs * bell * (1.0 / math.sqrt(2.0 * math.pi))


def swap(value, bit):
    number = lax.axis_size("ctx")
    return lax.ppermute(value, "ctx", [(at, at ^ bit) for at in range(number)])


def shift_fsdp(value, step):
    number = lax.axis_size("fsdp")
    return lax.ppermute(value, "fsdp", [(at, (at + step) % number) for at in range(number)])


def ctx_bits():
    bits, bit = [], 2
    while bit < lax.axis_size("ctx"):
        bits.append(bit)
        bit *= 2
    return bits


def gather_ctx(piece, order):
    me = lax.axis_index("ctx")
    held, done = piece, []
    for bit in order:
        other = swap(held, bit)
        high = (me & bit) != 0
        place = sum(1 for earlier in done if earlier > bit)
        held = jnp.stack([jnp.where(high, other, held), jnp.where(high, held, other)], axis=place)
        done.append(bit)
    return held.reshape((lax.axis_size("ctx"),) + piece.shape)


def scatter_ctx_step(held, bits_left, bit):
    me = lax.axis_index("ctx")
    high = (me & bit) // bit
    axis = 1 + bits_left.index(bit)
    mine = lax.dynamic_index_in_dim(held, high, axis, keepdims=False)
    send = lax.dynamic_index_in_dim(held, 1 - high, axis, keepdims=False).astype(BF16)
    total = mine.astype(F32) + swap(send, bit).astype(F32)
    return total.astype(BF16), [left for left in bits_left if left != bit]


def sum_weight(partial):
    rows, columns = partial.shape
    number, groups = lax.axis_size("ctx"), lax.axis_size("fsdp")
    own = lax.axis_index("fsdp")
    chips = ctx_bits()
    all_bits = sorted(chips + [1], reverse=True)
    held = partial.reshape((groups,) + (2,) * len(all_bits) + (rows // (groups * number), columns))
    held, left = scatter_ctx_step(held, all_bits, 1)
    half = columns // 2
    pieces = []
    for part, order in ((held[..., :half], chips), (held[..., half:], chips[::-1])):
        part_left = left
        for bit in order:
            part, part_left = scatter_ctx_step(part, part_left, bit)
        pieces.append(part)
    piece = jnp.concatenate(pieces, axis=-1)
    total = lax.dynamic_index_in_dim(piece, own, 0, keepdims=False).astype(F32)
    for step in range(1, groups):
        send = lax.dynamic_index_in_dim(piece, (own + step) % groups, 0, keepdims=False)
        total = total + shift_fsdp(send, step).astype(F32)
    total = total.astype(BF16)
    left_half = gather_ctx(total[:, :half], chips[::-1] + [1])
    right_half = gather_ctx(total[:, half:], chips + [1])
    whole = jnp.concatenate([left_half, right_half], axis=-1)
    return whole.reshape(rows // groups, columns).astype(F32)


def sum_vectors(vectors):
    groups = lax.axis_size("fsdp")
    own = lax.axis_index("fsdp")
    packed = jnp.concatenate([vector.reshape(groups, -1) for vector in vectors], axis=1)
    for bit in [1] + ctx_bits():
        packed = packed + swap(packed, bit)
    total = lax.dynamic_index_in_dim(packed, own, 0, keepdims=False)
    for step in range(1, groups):
        send = lax.dynamic_index_in_dim(packed, (own + step) % groups, 0, keepdims=False)
        total = total + shift_fsdp(send, step)
    owned, at = [], 0
    for vector in vectors:
        width = vector.shape[0] // groups
        owned.append(total[at : at + width])
        at += width
    return owned


def vector_kernel(number, at_ref, *refs):
    rows, (vectors_ref, wide_ref, mix_ref, held) = refs[:-4], refs[-4:]
    groups = len(rows)
    for step in range(groups):
        held[pl.ds(lax.rem(at_ref[1] + groups - step, groups), 1), :] = rows[step][...]
    width = vectors_ref.shape[1] // groups
    wide = wide_ref.shape[1] // groups
    for group in range(groups):
        for at in range(number):
            part = held[group : group + 1, at * width : (at + 1) * width]
            vectors_ref[at : at + 1, group * width : (group + 1) * width] = part
        wide_ref[:, group * wide : (group + 1) * wide] = held[group : group + 1, number * width :]
    model_width = vectors_ref.shape[1]
    mix_ref[...] = jnp.zeros(mix_ref.shape, F32)
    mix_ref[:, :model_width] = vectors_ref[0:1, :]
    mix_ref[:, 2 * model_width :] = vectors_ref[1:2, :]


def pack_vectors(vectors, wide):
    return jnp.concatenate(vectors + [wide])[None].astype(F32)


def gather_vectors(packed, count, width, places):
    groups = lax.axis_size("fsdp")
    rows = [packed] + [shift_fsdp(packed, step) for step in range(1, groups)]
    model_width, wide_width = groups * width, groups * (packed.shape[1] - count * width)
    vmem = pl.BlockSpec(memory_space=pltpu.VMEM)
    return pl.pallas_call(
        functools.partial(vector_kernel, count),
        in_specs=[pl.BlockSpec(memory_space=pltpu.SMEM)] + [vmem] * groups,
        out_specs=[vmem] * 3,
        out_shape=[
            jax.ShapeDtypeStruct((count, model_width), F32),
            jax.ShapeDtypeStruct((1, wide_width), F32),
            jax.ShapeDtypeStruct((1, 3 * model_width), F32),
        ],
        scratch_shapes=[pltpu.VMEM((groups, packed.shape[1]), F32)],
    )(places, *rows)


def after(values, *signs):
    signs = [sign for sign in signs if sign is not None]
    if not signs:
        return values
    return lax.optimization_barrier((values, signs))[0]


def spread_chips(block):
    found = {0: block}
    for bit in range(2, lax.axis_size("ctx"), 2):
        found[bit] = swap(block, bit)
    return found


def copy_kernel(plan, count, at_ref, *refs):
    sources, targets = refs[:count], refs[count : count + 1]
    slots, in_sems, out_sems = refs[count + 1 : -2], refs[-2], refs[-1]
    arrivals = []
    for at in range(count):
        arrivals.append(pltpu.make_async_copy(sources[at], slots[at], in_sems.at[at]))
        arrivals[at].start()
    leaving = []
    for at, moves in enumerate(plan(at_ref, slots, targets[0])):
        arrivals[at].wait()
        for source, target in moves:
            leaving.append(pltpu.make_async_copy(source, target, out_sems.at[len(leaving)]))
            leaving[-1].start()
    for copy in leaving:
        copy.wait()


def assemble(places, sources, shape, plan, copies):
    anywhere = pl.BlockSpec(memory_space=pl.ANY)
    return pl.pallas_call(
        functools.partial(copy_kernel, plan, len(sources)),
        in_specs=[pl.BlockSpec(memory_space=pltpu.SMEM)] + [anywhere] * len(sources),
        out_specs=anywhere,
        out_shape=shape,
        scratch_shapes=[pltpu.VMEM(source.shape, source.dtype) for source in sources]
        + [pltpu.SemaphoreType.DMA((len(sources),)), pltpu.SemaphoreType.DMA((copies,))],
        compiler_params=pltpu.CompilerParams(vmem_limit_bytes=32 * 1024 * 1024),
        cost_estimate=pl.CostEstimate(flops=0, bytes_accessed=10_000_000, transcendentals=0),
    )(places, *sources)


def shift_all(piece):
    return {step: shift_fsdp(piece, step) for step in range(1, lax.axis_size("fsdp"))}


def row_of_step(own, step, rows):
    groups = lax.axis_size("fsdp")
    return pl.ds(lax.rem(own + groups - step, groups) * rows, rows)


def halves_plan(rows, half):
    groups = lax.axis_size("fsdp")

    def plan(at_ref, slots, target):
        own, core_at = at_ref[1], at_ref[0] & 1
        moves = [[(slots[0], target.at[pl.ds(own * rows, rows)])]]
        for at, side in ((1, core_at), (2, 1 - core_at)):
            column = pl.ds(pl.multiple_of(side * half, 128), half)
            moves.append(
                [
                    (slots[at].at[step - 1], target.at[row_of_step(own, step, rows), column])
                    for step in range(1, groups)
                ]
            )
        return moves

    return plan


def core_half(shard):
    rows, columns = shard.shape
    core = lax.axis_index("ctx") % 2
    return lax.dynamic_slice(shard, (0, core * (columns // 2)), (rows, columns // 2))


def stack_steps(fetched):
    return jnp.stack([fetched[step] for step in sorted(fetched)])


def whole_of_halves(shard, mine, theirs, places):
    rows, columns = shard.shape
    groups = lax.axis_size("fsdp")
    shape = jax.ShapeDtypeStruct((groups * rows, columns), shard.dtype)
    plan = halves_plan(rows, columns // 2)
    return assemble(places, [shard, mine, theirs], shape, plan, 2 * groups - 1)


def weight_by_core(shard, places):
    piece = core_half(shard)
    sign = yield piece
    fetched = shift_all(piece)
    last = fetched.pop(1)
    fetched = after(fetched, sign)
    sign = yield list(fetched.values())
    mine = stack_steps({**fetched, 1: after(last, sign)})
    yield mine
    yield whole_of_halves(shard, mine, swap(mine, 1), places)


def two_weights_by_ctx(shard, second, places):
    rows, columns = shard.shape
    number, groups = lax.axis_size("ctx"), lax.axis_size("fsdp")
    me = lax.axis_index("ctx")
    width = columns // number
    piece = lax.dynamic_slice(shard, (0, me * width), (rows, width))
    pieces = jnp.stack([piece, core_half(second)])
    sign = yield pieces
    fetched = stack_steps(after(shift_all(pieces), sign))
    stack, mine = fetched[:, 0], fetched[:, 1]
    sign = yield fetched
    theirs = swap(mine, 1)
    near = spread_chips(stack)
    near_bits = sorted(near)
    near_list = after([near[bit] for bit in near_bits], sign)
    near_stack = jnp.stack(near_list)
    yield near_stack
    across = swap(near_stack, 1)

    def plan(at_ref, slots, target):
        own, at = at_ref[1], at_ref[0]

        def moves_of(slot, other):
            column = pl.ds(pl.multiple_of(other * width, 128), width)
            return [
                (slot.at[step - 1], target.at[row_of_step(own, step, rows), column])
                for step in range(1, groups)
            ]

        moves = [moves_of(slots[index], at ^ bit) for index, bit in enumerate(near_bits)]
        last = []
        for index, bit in enumerate(near_bits):
            last += moves_of(slots[-2].at[index], at ^ bit ^ 1)
        return moves + [last, [(slots[-1], target.at[pl.ds(own * rows, rows)])]]

    shape = jax.ShapeDtypeStruct((groups * rows, columns), shard.dtype)
    whole = assemble(
        places, near_list + [across, shard], shape, plan, number * (groups - 1) + 1
    )
    yield whole, whole_of_halves(second, mine, theirs, places)


def stacked_pieces(grad, blocks):
    groups, chips = lax.axis_size("fsdp"), lax.axis_size("ctx") // 2
    rows, width = grad.shape[0], grad.shape[1] // blocks
    parts = [
        grad[:, at * width : (at + 1) * width].reshape(
            groups, chips, 2, rows // (2 * groups * chips), width
        )
        for at in range(blocks)
    ]
    return jnp.concatenate(parts, axis=3)


def pieces_of(grad, column_blocks):
    groups, chips = lax.axis_size("fsdp"), lax.axis_size("ctx") // 2
    rows, columns = grad.shape
    if column_blocks < 0:
        return stacked_pieces(grad, -column_blocks)
    if column_blocks == 1:
        return grad.reshape(groups, chips, 2, rows // (2 * groups * chips), columns)
    width = columns // chips
    viewed = jnp.stack([grad[:, at * width : (at + 1) * width] for at in range(chips)])
    viewed = viewed.reshape(chips, groups, 2, rows // (2 * groups), width)
    return jnp.swapaxes(viewed, 0, 1)


VECTOR_ROWS = 8


def finish_kernel(near_bits, parts, at_ref, *refs):
    me = at_ref[0]
    sources, outs = refs[: len(near_bits) + 1], refs[len(near_bits) + 1 :]

    def put(values, other):
        first = 0
        for out_ref, (rows, column_blocks) in zip(outs, parts):
            part = values[first : first + rows]
            width = part.shape[1]
            if column_blocks < 0:
                each = rows // -column_blocks
                row = pl.ds(pl.multiple_of(other * each, 8), each)
                for at in range(-column_blocks):
                    piece = part[at * each : (at + 1) * each]
                    out_ref[row, at * width : (at + 1) * width] = piece
            elif column_blocks == 1:
                out_ref[pl.ds(pl.multiple_of(other * rows, 8), rows), :] = part
            else:
                row = pl.ds(pl.multiple_of((other & 1) * rows, 8), rows)
                out_ref[row, pl.ds(pl.multiple_of((other >> 1) * width, 128), width)] = part
            first += rows

    for index, bit in enumerate(near_bits):
        put(sources[index][...].astype(F32), me ^ bit)
        put(sources[-1][index].astype(F32), me ^ bit ^ 1)


def sum_pack(grads, blocks, vectors, places, fsdp_first=False):
    number, groups = lax.axis_size("ctx"), lax.axis_size("fsdp")
    me, own = lax.axis_index("ctx"), lax.axis_index("fsdp")
    core, chip, chips = me % 2, me // 2, number // 2
    views = [pieces_of(grad, block) for grad, block in zip(grads, blocks)]
    width = views[0].shape[4]
    if vectors:
        rows = [vector.reshape(groups, 1, -1) for vector in vectors]
        rows = [jnp.pad(row, ((0, 0), (0, 0), (0, width - row.shape[2]))) for row in rows]
        rows += [jnp.zeros_like(rows[0])] * (number - len(rows))
        view = jnp.concatenate(rows, axis=1).astype(BF16)
        view = view.reshape(groups, chips, 2, 1, width)
        views.append(jnp.pad(view, ((0, 0), (0, 0), (0, 0), (0, VECTOR_ROWS - 1), (0, 0))))

    def side(which):
        parts = [
            jnp.swapaxes(lax.dynamic_index_in_dim(view, which, 2, keepdims=False), 0, 1)
            for view in views
        ]
        return jnp.concatenate(parts, axis=2) if len(parts) > 1 else parts[0]

    send = side(1 - core)
    done_after = yield send
    other = after(swap(send, 1), done_after)
    held = (side(core).astype(F32) + other.astype(F32)).astype(BF16)

    def over_chips(array, axis):
        def part(at):
            return lax.dynamic_index_in_dim(array, at, axis, keepdims=False)

        bits = range(2, number, 2)
        sends = [part(chip ^ (bit // 2)) for bit in bits]
        return part(chip), sends, lambda all_sends: [swap(*pair) for pair in zip(all_sends, bits)]

    def over_fsdp(array, axis):
        def part(at):
            return lax.dynamic_index_in_dim(array, at, axis, keepdims=False)

        steps = range(1, groups)
        sends = [part((own + step) % groups) for step in steps]
        return part(own), sends, lambda all_sends: [shift_fsdp(*p) for p in zip(all_sends, steps)]

    if fsdp_first:
        mine, sends, move = over_fsdp(held, 1)
    else:
        mine, sends, move = over_chips(held, 0)
    start_after, done_after = yield sends
    others = move(after(sends, start_after))
    early = 1 if fsdp_first else len(others) - 1
    total = mine.astype(F32)
    for other in after(others[:early], done_after):
        total = total + other.astype(F32)
    done_after = yield total
    for other in after(others[early:], done_after):
        total = total + other.astype(F32)
    piece = total.astype(BF16)
    mine, sends, move = over_chips(piece, 0) if fsdp_first else over_fsdp(piece, 0)
    done_after = yield sends
    total = mine.astype(F32)
    for other in after(move(sends), done_after):
        total = total + other.astype(F32)
    total = total.astype(BF16)
    done_after = yield total
    near = spread_chips(total)
    near_bits = sorted(near)
    stack = jnp.stack(after([near[bit] for bit in near_bits], done_after))
    yield stack
    across = swap(stack, 1)
    parts = [(view.shape[3], block) for view, block in zip(views, list(blocks) + [1])]
    shapes = [
        jax.ShapeDtypeStruct((grad.shape[0] // groups, grad.shape[1]), F32) for grad in grads
    ]
    if vectors:
        shapes.append(jax.ShapeDtypeStruct((number * VECTOR_ROWS, width), F32))
    vmem = pl.BlockSpec(memory_space=pltpu.VMEM)
    sums = pl.pallas_call(
        functools.partial(finish_kernel, near_bits, parts),
        in_specs=[pl.BlockSpec(memory_space=pltpu.SMEM)] + [vmem] * (len(near_bits) + 1),
        out_specs=[vmem] * len(shapes),
        out_shape=shapes,
        compiler_params=pltpu.CompilerParams(vmem_limit_bytes=32 * 1024 * 1024),
    )(places, *[near[bit] for bit in near_bits], across)
    owned = [
        sums[-1][at * VECTOR_ROWS, : vector.shape[0] // groups]
        for at, vector in enumerate(vectors)
    ]
    yield list(sums[: len(grads)]), owned


def head_masks(rows):
    lane = lax.broadcasted_iota(jnp.int32, (rows, PAIR), 1)
    first = lane < HEAD_DIM
    return (first, jnp.logical_not(first))


def of_head(pair, mask):
    return jnp.where(mask, pair.astype(F32), 0.0).astype(BF16)


def lane_fold(values, combine):
    width = values.shape[1]
    folded = values[:, :PAIR]
    for at in range(PAIR, width, PAIR):
        folded = combine(folded, values[:, at : at + PAIR])
    return folded


def chunk_of(ref, index):
    part = ref[pl.ds(index * CHUNK_BLOCKS, CHUNK_BLOCKS)]
    return part.reshape(part.shape[0] * part.shape[1], PAIR)


def key_bias(length, index, width):
    place = index * width + lax.broadcasted_iota(jnp.int32, (1, width), 1)
    return jnp.where(place < length, 0.0, -1e30)


def both_ways(length, full, width, run):
    @pl.when(length == full)
    def _():
        def loop(body, state):
            for index in range(full // width):
                state = body(index, state)
            return state

        run(loop, None)

    @pl.when(length < full)
    def _():
        chunks = (length + width - 1) // width
        run(
            lambda body, state: lax.fori_loop(0, chunks, body, state),
            lambda index: key_bias(length, index, width),
        )


def forward_kernel(place_ref, q_ref, k_ref, v_ref, att_ref, low_ref, col_ref, row_ref, scores):
    rows = q_ref.shape[1]
    width = CHUNK_BLOCKS * k_ref.shape[1]
    masks = head_masks(rows)
    queries = q_ref[0]
    split = [of_head(queries, mask) for mask in masks]

    def run(loop, bias_of):
        def score_chunk(index, tops):
            keys = chunk_of(k_ref, index)
            new = []
            for head in range(2):
                part = lax.dot_general(split[head], keys, NT, preferred_element_type=F32)
                if bias_of is not None:
                    part = part + bias_of(index)
                scores[head, index] = part
                new.append(jnp.maximum(tops[head], lane_fold(part, jnp.maximum)))
            return tuple(new)

        low_start = jnp.full((rows, PAIR), -1e30, F32)
        tops = loop(score_chunk, (low_start, low_start))
        top = [jnp.max(one, axis=1, keepdims=True) * SCORE for one in tops]

        def weigh_chunk(index, state):
            values = chunk_of(v_ref, index)
            new = []
            for head in range(2):
                summed, weighted = state[head]
                weights = jnp.exp2(scores[head, index] * SCORE - top[head])
                summed = summed + lane_fold(weights, jnp.add)
                weighted = weighted + jnp.dot(
                    weights.astype(BF16), values, preferred_element_type=F32
                )
                new.append((summed, weighted))
            return tuple(new)

        zero = jnp.zeros((rows, PAIR), F32)
        state = loop(weigh_chunk, ((zero, zero), (zero, zero)))
        totals = [jnp.sum(state[head][0], axis=1, keepdims=True) for head in range(2)]
        attended = jnp.where(masks[0], state[0][1] / totals[0], state[1][1] / totals[1])
        att_ref[...] = attended
        low_ref[...] = attended.astype(BF16)
        lse = [top[head] + jnp.log2(totals[head]) for head in range(2)]
        column = jnp.where(masks[0], lse[0], lse[1])
        col_ref[...] = column
        turned = jnp.transpose(column)
        row_ref[0, 0:1, :] = turned[0:1, :]
        row_ref[0, 1:2, :] = turned[HEAD_DIM : HEAD_DIM + 1, :]

    both_ways(place_ref[1], k_ref.shape[0] * k_ref.shape[1], width, run)


def query_kernel(place_ref, q_ref, k_ref, v_ref, g_ref, att_ref, col_ref, out_ref):
    rows = q_ref.shape[1]
    width = CHUNK_BLOCKS * k_ref.shape[1]
    masks = head_masks(rows)
    grads = g_ref[...]
    products = grads.astype(F32) * att_ref[...]
    query_split = [of_head(q_ref[0], mask) for mask in masks]
    grad_split = [of_head(grads, mask) for mask in masks]
    delta = [jnp.sum(jnp.where(mask, products, 0.0), axis=1, keepdims=True) for mask in masks]
    lse = [col_ref[:, 0:1], col_ref[:, HEAD_DIM : HEAD_DIM + 1]]

    def run(loop, bias_of):
        def chunk(index, totals):
            keys = chunk_of(k_ref, index)
            values = chunk_of(v_ref, index)
            new = []
            for head in range(2):
                part = lax.dot_general(query_split[head], keys, NT, preferred_element_type=F32)
                part = part * SCORE - lse[head]
                if bias_of is not None:
                    part = part + bias_of(index)
                moved = lax.dot_general(grad_split[head], values, NT, preferred_element_type=F32)
                grad_scores = (jnp.exp2(part) * (moved - delta[head])).astype(BF16)
                new.append(totals[head] + jnp.dot(grad_scores, keys, preferred_element_type=F32))
            return tuple(new)

        zero = jnp.zeros((rows, PAIR), F32)
        totals = loop(chunk, (zero, zero))
        total = jnp.where(masks[0], totals[0], totals[1])
        out_ref[...] = (total * (1.0 / math.sqrt(HEAD_DIM))).astype(BF16)

    both_ways(place_ref[1], k_ref.shape[0] * k_ref.shape[1], width, run)


def key_kernel(place_ref, k_ref, v_ref, q_ref, g_ref, stat_ref, dk_ref, dv_ref):
    offset, length = place_ref[0] * k_ref.shape[1], place_ref[1]
    rows = k_ref.shape[1]
    chunks = q_ref.shape[0] // CHUNK_BLOCKS
    masks = head_masks(rows)

    @pl.when(offset >= length)
    def _():
        dk_ref[...] = jnp.zeros(dk_ref.shape, BF16)
        dv_ref[...] = jnp.zeros(dv_ref.shape, BF16)

    @pl.when(offset < length)
    def _():
        key_split = [of_head(k_ref[0], mask) for mask in masks]
        value_split = [of_head(v_ref[0], mask) for mask in masks]

        def chunk(index, totals):
            queries = chunk_of(q_ref, index)
            grads = chunk_of(g_ref, index)
            stats = stat_ref[pl.ds(index * CHUNK_BLOCKS, CHUNK_BLOCKS), 0]

            def stat(which):
                return jnp.concatenate(
                    [stats[at, which : which + 1, :] for at in range(CHUNK_BLOCKS)], axis=1
                )

            new = []
            for head in range(2):
                part = lax.dot_general(key_split[head], queries, NT, preferred_element_type=F32)
                weights = jnp.exp2(part * SCORE - stat(head))
                moved = lax.dot_general(value_split[head], grads, NT, preferred_element_type=F32)
                grad_scores = (weights * (moved - stat(2 + head))).astype(BF16)
                grad_keys, grad_values = totals[head]
                grad_keys = grad_keys + jnp.dot(grad_scores, queries, preferred_element_type=F32)
                grad_values = grad_values + jnp.dot(
                    weights.astype(BF16), grads, preferred_element_type=F32
                )
                new.append((grad_keys, grad_values))
            return tuple(new)

        zero = jnp.zeros((rows, PAIR), F32)
        totals = ((zero, zero), (zero, zero))
        for index in range(chunks):
            totals = chunk(index, totals)
        usable = offset + lax.broadcasted_iota(jnp.int32, (rows, PAIR), 0) < length
        grad_keys = jnp.where(masks[0], totals[0][0], totals[1][0])
        grad_values = jnp.where(masks[0], totals[0][1], totals[1][1])
        grad_keys = grad_keys * (1.0 / math.sqrt(HEAD_DIM))
        dk_ref[...] = jnp.where(usable, grad_keys, 0.0).astype(BF16)
        dv_ref[...] = jnp.where(usable, grad_values, 0.0).astype(BF16)


def kernel_call(body, place, operands, in_specs, outs, out_specs, pairs, scratch, flops):
    return pl.pallas_call(
        body,
        grid_spec=pltpu.PrefetchScalarGridSpec(
            num_scalar_prefetch=1,
            grid=(pairs,),
            in_specs=in_specs,
            out_specs=out_specs,
            scratch_shapes=scratch,
        ),
        out_shape=outs,
        compiler_params=pltpu.CompilerParams(vmem_limit_bytes=48 * 1024 * 1024),
        cost_estimate=pl.CostEstimate(flops=flops, bytes_accessed=10_000_000, transcendentals=0),
    )(place, *operands)


def mix_specs(number, seq, tokens, pairs):
    def own(part):
        return pl.BlockSpec(
            (1, None, tokens, PAIR), lambda h, place: (place[0], seq, 0, part * pairs + h)
        )

    def every(part):
        return pl.BlockSpec(
            (number, None, tokens, PAIR), lambda h, place: (0, seq, 0, part * pairs + h)
        )

    return own, every


def mix_kernel(x_ref, weight_ref, add_ref, *refs):
    out_ref = refs[-1]
    for at in range(x_ref.shape[0]):
        mixed = jnp.dot(x_ref[at], weight_ref[...], preferred_element_type=F32)
        out_ref[at] = (mixed + add_ref[...]).astype(BF16)


def mix_tokens(tokens_all, weight, add, first, count, earlier):
    number, seqs, tokens, model_width = tokens_all.shape
    width = weight.shape[1]
    kept = [] if earlier is None else [earlier]
    return pl.pallas_call(
        mix_kernel,
        grid=(count,),
        in_specs=[
            pl.BlockSpec((None, seqs, tokens, model_width), lambda at: (first + at, 0, 0, 0)),
            pl.BlockSpec((model_width, width), lambda at: (0, 0)),
            pl.BlockSpec((1, width), lambda at: (0, 0)),
        ]
        + [pl.BlockSpec(memory_space=pl.ANY)] * len(kept),
        out_specs=pl.BlockSpec((None, seqs, tokens, width), lambda at: (first + at, 0, 0, 0)),
        out_shape=jax.ShapeDtypeStruct((number, seqs, tokens, width), BF16),
        input_output_aliases={3: 0} if kept else {},
        compiler_params=pltpu.CompilerParams(vmem_limit_bytes=48 * 1024 * 1024),
        cost_estimate=pl.CostEstimate(
            flops=2 * count * seqs * tokens * model_width * width,
            bytes_accessed=2 * count * seqs * tokens * (model_width + width),
            transcendentals=0,
        ),
    )(tokens_all, weight, add, *kept)


def outer_kernel(left_ref, right_ref, out_ref):
    out_ref[...] = lax.dot_general(
        left_ref[...], right_ref[...], TN, preferred_element_type=F32
    ).astype(BF16)


def outer_products(left, parts):
    rows, model_width = left.shape
    number, _, columns = parts.shape
    return pl.pallas_call(
        outer_kernel,
        grid=(number,),
        in_specs=[
            pl.BlockSpec((rows, model_width), lambda at: (0, 0)),
            pl.BlockSpec((None, rows, columns), lambda at: (at, 0, 0)),
        ],
        out_specs=pl.BlockSpec((model_width, columns), lambda at: (0, at)),
        out_shape=jax.ShapeDtypeStruct((model_width, number * columns), BF16),
        compiler_params=pltpu.CompilerParams(vmem_limit_bytes=48 * 1024 * 1024),
        cost_estimate=pl.CostEstimate(
            flops=2 * model_width * rows * number * columns,
            bytes_accessed=6_000_000,
            transcendentals=0,
        ),
    )(left, parts)


def attend_forward(place, seq, mix):
    number, _, tokens, width = mix.shape
    model_width = width // 3
    pairs = model_width // PAIR
    own, every = mix_specs(number, seq, tokens, pairs)
    chunk = CHUNK_BLOCKS * tokens
    block = pl.BlockSpec((tokens, PAIR), lambda h, place: (0, h))
    return kernel_call(
        forward_kernel,
        place,
        (mix, mix, mix),
        [own(0), every(1), every(2)],
        (
            jax.ShapeDtypeStruct((tokens, model_width), F32),
            jax.ShapeDtypeStruct((tokens, model_width), BF16),
            jax.ShapeDtypeStruct((tokens, model_width), F32),
            jax.ShapeDtypeStruct((pairs, 2, tokens), F32),
        ),
        (block, block, block, pl.BlockSpec((1, 2, tokens), lambda h, place: (h, 0, 0))),
        pairs,
        [pltpu.VMEM((2, number // CHUNK_BLOCKS, tokens, chunk), F32)],
        56 * number * tokens * tokens * model_width,
    )


def attend_queries(place, seq, mix, grads, attended, column):
    number, _, tokens, width = mix.shape
    model_width = width // 3
    pairs = model_width // PAIR
    own, every = mix_specs(number, seq, tokens, pairs)
    block = pl.BlockSpec((tokens, PAIR), lambda h, place: (0, h))
    return kernel_call(
        query_kernel,
        place,
        (mix, mix, mix, grads, attended, column),
        [own(0), every(1), every(2), block, block, block],
        jax.ShapeDtypeStruct((tokens, model_width), BF16),
        block,
        pairs,
        [],
        56 * number * tokens * tokens * model_width,
    )


def attend_keys(place, seq, mix, all_grads, stats):
    number, _, tokens, width = mix.shape
    model_width = width // 3
    pairs = model_width // PAIR
    own, every = mix_specs(number, seq, tokens, pairs)
    block = pl.BlockSpec((tokens, PAIR), lambda h, place: (0, h))
    return kernel_call(
        key_kernel,
        place,
        (mix, mix, mix, all_grads, stats),
        [
            own(1),
            own(2),
            every(0),
            pl.BlockSpec((number, None, tokens, PAIR), lambda h, place: (0, seq, 0, h)),
            pl.BlockSpec((number, None, 1, 4, tokens), lambda h, place: (0, seq, h, 0, 0)),
        ],
        (
            jax.ShapeDtypeStruct((tokens, model_width), BF16),
            jax.ShapeDtypeStruct((tokens, model_width), BF16),
        ),
        (block, block),
        pairs,
        [],
        72 * number * tokens * tokens * model_width,
    )


def on_device(
    hidden_states,
    lengths,
    cotangent,
    attend_weight,
    query_bias,
    value_bias,
    output_weight,
    output_bias,
    first_gain,
    first_shift,
    raise_weight,
    raise_bias,
    lower_weight,
    lower_bias,
    second_gain,
    second_shift,
):
    seq_count, tok_count, model_width = hidden_states.shape
    row_count = seq_count * tok_count
    block_shape = (seq_count, tok_count, model_width)
    number = lax.axis_size("ctx")
    pairs = model_width // PAIR
    me = lax.axis_index("ctx")
    places = jnp.stack([me, lax.axis_index("fsdp")]).astype(jnp.int32)

    tokens_all = lax.all_gather(hidden_states, "ctx", axis=0, tiled=False)
    attend_stages = weight_by_core(attend_weight, places)
    attend_piece = next(attend_stages)
    vectors = after(
        [
            query_bias,
            value_bias,
            output_bias,
            first_gain,
            first_shift,
            lower_bias,
            second_gain,
            second_shift,
        ],
        attend_piece,
    )
    packed_vectors = pack_vectors(vectors, raise_bias)
    attend_stages.send(packed_vectors)
    attend_sign = attend_stages.send(packed_vectors)
    attend_full = next(attend_stages)
    vector_rows, raise_add, mix_add = gather_vectors(
        packed_vectors, len(vectors), query_bias.shape[0], places
    )
    output_add, gain_first, shift_first, lower_add, gain_second, shift_second = [
        vector_rows[at : at + 1] for at in range(2, 8)
    ]
    packed = (raise_weight.shape[1] // number) == output_weight.shape[1] // 2
    if packed:
        raise_stages = two_weights_by_ctx(
            after(raise_weight, attend_sign), output_weight, places
        )
        raise_sign = next(raise_stages)
    else:
        raise_stages = weight_by_core(raise_weight, places)
        output_stages = weight_by_core(output_weight, places)
        raise_sign = (next(raise_stages), next(output_stages))
    mix = mix_tokens(after(tokens_all, raise_sign), attend_full, mix_add, 0, number, None)
    if packed:
        raise_sign = raise_stages.send(mix)
    lower_stages = weight_by_core(after(lower_weight, raise_sign), places)
    mix = after(mix, raise_sign, next(lower_stages))

    seq_places = [
        jnp.stack([me.astype(jnp.int32), lengths[at].astype(jnp.int32)]) for at in range(seq_count)
    ]
    attended, attended_lows, columns, lse_rows = [], [], [], []
    for at in range(seq_count):
        one, low, column, lse_row = attend_forward(seq_places[at], at, mix)
        attended.append(one)
        attended_lows.append(low)
        columns.append(column)
        lse_rows.append(lse_row)
        if at == 0:
            lower_sign = lower_stages.send(low)
            mix = after(mix, raise_stages.send(low) if packed else None, lower_sign)
    if packed:
        raise_full, output_full = next(raise_stages)
    else:
        for stages in (raise_stages, output_stages):
            stages.send(None)
            stages.send(None)
        next_stage = next(raise_stages), next(output_stages)
        raise_full, output_full = next_stage
    lower_stages.send(attended_lows[-1])
    attended_low = jnp.concatenate(attended_lows, axis=0)

    token_rows = hidden_states.reshape(row_count, model_width)
    projected = jnp.dot(attended_low, output_full, preferred_element_type=F32) + output_add
    normed_first, first_back = jax.vjp(
        layer_norm, token_rows.astype(F32) + projected, gain_first, shift_first
    )
    first_low = normed_first.astype(BF16)
    raised = jnp.dot(first_low, raise_full, preferred_element_type=F32) + raise_add
    active, slope = gelu_and_slope(raised)
    active_low, slope = lax.optimization_barrier((active.astype(BF16), slope))
    lower_full = next(lower_stages)
    lowered = jnp.dot(active_low, lower_full, preferred_element_type=F32) + lower_add
    result, second_back = jax.vjp(layer_norm, normed_first + lowered, gain_second, shift_second)
    layer_output = result.astype(BF16).reshape(block_shape)
    grad_out = cotangent.reshape(row_count, model_width).astype(F32)
    grad_mid, grad_gain_second, grad_shift_second = second_back(grad_out)
    grad_gain_second, grad_shift_second = grad_gain_second[0], grad_shift_second[0]
    mid_low = grad_mid.astype(BF16)
    shared = model_width % (8 * number * lax.axis_size("fsdp")) == 0
    grad_lower_weight = jnp.einsum("rf,rd->fd", active_low, mid_low, preferred_element_type=F32).astype(BF16)
    if shared:
        lower_pack = sum_pack([grad_lower_weight], [1], [], places, True)
        mid_low = after(mid_low, next(lower_pack))
    grad_lower_add = jnp.sum(mid_low.astype(F32), axis=0)
    grad_active = jnp.einsum("rd,fd->rf", mid_low, lower_full, preferred_element_type=F32)
    raised_low = (slope * grad_active).astype(BF16)
    lower_send = lower_pack.send(raised_low) if shared else None
    grad_raise_weight = jnp.einsum("rd,rf->df", first_low, raised_low, preferred_element_type=F32).astype(BF16)
    grad_raise_add = jnp.sum(raised_low.astype(F32), axis=0)
    grad_first = grad_mid + jnp.einsum(
        "rf,df->rd", raised_low, raise_full, preferred_element_type=F32
    )
    grad_resid, grad_gain_first, grad_shift_first = first_back(grad_first)
    grad_gain_first, grad_shift_first = grad_gain_first[0], grad_shift_first[0]
    resid_low = grad_resid.astype(BF16)
    grad_output_weight = jnp.einsum(
        "rc,rd->cd", attended_low, resid_low, preferred_element_type=F32
    ).astype(BF16)
    grad_output_add = jnp.sum(resid_low.astype(F32), axis=0)
    grad_att = (
        jnp.einsum("rd,cd->rc", resid_low, output_full, preferred_element_type=F32)
        .astype(BF16)
        .reshape(block_shape)
    )
    head_of = lax.broadcasted_iota(jnp.int32, (HEADS, model_width), 1) // HEAD_DIM
    pick = (head_of == lax.broadcasted_iota(jnp.int32, (HEADS, model_width), 0)).astype(F32)
    stats = []
    for at in range(seq_count):
        delta = jnp.einsum(
            "hd,td->ht",
            pick,
            grad_att[at].astype(F32) * attended[at],
            precision=lax.Precision.HIGHEST,
            preferred_element_type=F32,
        ).reshape(pairs, 2, tok_count)
        stats.append(jnp.concatenate([lse_rows[at], delta], axis=1))
    stats = jnp.stack(stats)
    stat_rows = stats.size // (seq_count * model_width)
    rest, coded = stats.reshape(seq_count, stat_rows, model_width), []
    for _ in range(3):
        part = lax.reduce_precision(rest, 8, 7)
        coded.append(part.astype(BF16))
        rest = rest - part
    grads_all = lax.all_gather(
        jnp.concatenate([grad_att] + coded, axis=1), "ctx", axis=0, tiled=False
    )
    coded = grads_all[:, :, tok_count:].astype(F32)
    coded = coded.reshape(number, seq_count, 3, stat_rows, model_width)
    stats_all = (coded[:, :, 0] + coded[:, :, 1] + coded[:, :, 2]).reshape(
        (number,) + stats.shape
    )
    early = [
        grad_output_add,
        grad_gain_first,
        grad_shift_first,
        grad_raise_add,
        grad_lower_add,
        grad_gain_second,
        grad_shift_second,
    ]
    query_grads, key_grads, value_grads = [], [], []
    if shared:
        raise_pack = sum_pack(
            [grad_raise_weight, grad_output_weight], [number // 2, 1], early, places
        )
        mix = after(mix, lower_send, next(raise_pack))
    for at in range(seq_count):
        query_grads.append(
            attend_queries(seq_places[at], at, mix, grad_att[at], attended[at], columns[at])
        )
        if shared and at == 0:
            mix = after(
                mix, lower_pack.send((None, query_grads[0])), raise_pack.send(query_grads[0])
            )
    for at in range(seq_count):
        grad_keys, grad_values = attend_keys(seq_places[at], at, mix, grads_all, stats_all)
        key_grads.append(grad_keys)
        value_grads.append(grad_values)
        if shared and at == 0:
            mix = after(
                mix, raise_pack.send((grads_all, grad_keys)), lower_pack.send(grad_keys)
            )
    if shared:
        raise_sends = raise_pack.send(value_grads[-1])
        value_grads[-1] = after(
            value_grads[-1], raise_sends, lower_pack.send(value_grads[-1])
        )
    query_low = jnp.concatenate(query_grads, axis=0)
    key_low = jnp.concatenate(key_grads, axis=0)
    value_low = jnp.concatenate(value_grads, axis=0)
    grad_mixture = jnp.concatenate([query_low, key_low, value_low], axis=1)
    grad_attend_weight = outer_products(
        token_rows, jnp.stack([query_low, key_low, value_low])
    )
    grad_query_add = jnp.sum(query_low.astype(F32), axis=0)
    grad_value_add = jnp.sum(value_low.astype(F32), axis=0)
    hidden_grad = grad_resid + jnp.einsum(
        "rc,dc->rd", grad_mixture, attend_full, preferred_element_type=F32
    )
    late = [grad_query_add, grad_value_add]
    if shared:
        attend_pack = sum_pack([grad_attend_weight], [-3], late, places)
        next(attend_pack)
        attend_pack.send(None)
        lower_stack = lower_pack.send(grad_attend_weight)
        attend_partial = attend_pack.send(((lower_stack, raise_sends), None))
        raise_pack.send(attend_partial)
        attend_sends = next(attend_pack)
        raise_pack.send(attend_sends)
        next(attend_pack)
        next(attend_pack)
        (grad_attend_weight,), late = next(attend_pack)
        (grad_lower_weight,), _ = next(lower_pack)
        (grad_raise_weight, grad_output_weight), early = next(raise_pack)
    else:
        grad_lower_weight = sum_weight(grad_lower_weight)
        grad_raise_weight = sum_weight(grad_raise_weight)
        grad_output_weight = sum_weight(grad_output_weight)
        grad_attend_weight = sum_weight(grad_attend_weight)
        early, late = sum_vectors(early), sum_vectors(late)
    (
        grad_output_add,
        grad_gain_first,
        grad_shift_first,
        grad_raise_add,
        grad_lower_add,
        grad_gain_second,
        grad_shift_second,
    ) = early
    grad_query_add, grad_value_add = late
    return (
        layer_output,
        hidden_grad.reshape(block_shape),
        grad_attend_weight,
        grad_query_add,
        grad_value_add,
        grad_output_weight,
        grad_output_add,
        grad_gain_first,
        grad_shift_first,
        grad_raise_weight,
        grad_raise_add,
        grad_lower_weight,
        grad_lower_add,
        grad_gain_second,
        grad_shift_second,
    )


def solution(mesh):
    return jax.shard_map(
        on_device,
        mesh=mesh,
        in_specs=(
            P("fsdp", "ctx", None),
            P("fsdp"),
            P("fsdp", "ctx", None),
            P("fsdp", None),
            P("fsdp"),
            P("fsdp"),
            P("fsdp", None),
            P("fsdp"),
            P("fsdp"),
            P("fsdp"),
            P("fsdp", None),
            P("fsdp"),
            P("fsdp", None),
            P("fsdp"),
            P("fsdp"),
            P("fsdp"),
        ),
        out_specs=(
            P("fsdp", "ctx", None),
            P("fsdp", "ctx", None),
            P("fsdp", None),
            P("fsdp"),
            P("fsdp"),
            P("fsdp", None),
            P("fsdp"),
            P("fsdp"),
            P("fsdp"),
            P("fsdp", None),
            P("fsdp"),
            P("fsdp", None),
            P("fsdp"),
            P("fsdp"),
            P("fsdp"),
        ),
        check_vma=False,
    )
```

```python
import functools
import math

import jax
import jax.numpy as jnp
from jax import lax
from jax.experimental import pallas as pl
from jax.experimental.pallas import tpu as pltpu
from jax.sharding import PartitionSpec as P

HEADS = 12
HEAD_DIM = 64
PAIR = 2 * HEAD_DIM
LOG2E = 1.4426950408889634
SCORE = LOG2E / math.sqrt(HEAD_DIM)
F32 = jnp.float32
BF16 = jnp.bfloat16
CHUNK_BLOCKS = 2
NT = (((1,), (1,)), ((), ()))
TN = (((0,), (0,)), ((), ()))


def layer_norm(hidden, gain, shift):
    average = jnp.mean(hidden, axis=-1, keepdims=True)
    centred = hidden - average
    variance = jnp.mean(centred * centred, axis=-1, keepdims=True)
    return centred * lax.rsqrt(variance + 1e-05) * gain + shift


def gelu_and_slope(inputs):
    size = jnp.abs(inputs) * math.sqrt(0.5)
    bell = jnp.exp(-0.5 * inputs * inputs)
    step = 1.0 / (1.0 + 0.3275911 * size)
    series = 1.061405429 * step - 1.453152027
    series = series * step + 1.421413741
    series = series * step - 0.284496736
    series = series * step + 0.254829592
    tail = 0.5 * series * step * bell
    below = jnp.where(inputs < 0.0, tail, 1.0 - tail)
    return inputs * below, below + inputs * bell * (1.0 / math.sqrt(2.0 * math.pi))


def swap(value, bit):
    number = lax.axis_size("ctx")
    return lax.ppermute(value, "ctx", [(at, at ^ bit) for at in range(number)])


def shift_fsdp(value, step):
    number = lax.axis_size("fsdp")
    return lax.ppermute(value, "fsdp", [(at, (at + step) % number) for at in range(number)])


def ctx_bits():
    bits, bit = [], 2
    while bit < lax.axis_size("ctx"):
        bits.append(bit)
        bit *= 2
    return bits


def gather_ctx(piece, order):
    me = lax.axis_index("ctx")
    held, done = piece, []
    for bit in order:
        other = swap(held, bit)
        high = (me & bit) != 0
        place = sum(1 for earlier in done if earlier > bit)
        held = jnp.stack([jnp.where(high, other, held), jnp.where(high, held, other)], axis=place)
        done.append(bit)
    return held.reshape((lax.axis_size("ctx"),) + piece.shape)


def scatter_ctx_step(held, bits_left, bit):
    me = lax.axis_index("ctx")
    high = (me & bit) // bit
    axis = 1 + bits_left.index(bit)
    mine = lax.dynamic_index_in_dim(held, high, axis, keepdims=False)
    send = lax.dynamic_index_in_dim(held, 1 - high, axis, keepdims=False).astype(BF16)
    total = mine.astype(F32) + swap(send, bit).astype(F32)
    return total.astype(BF16), [left for left in bits_left if left != bit]


def sum_weight(partial):
    rows, columns = partial.shape
    number, groups = lax.axis_size("ctx"), lax.axis_size("fsdp")
    own = lax.axis_index("fsdp")
    chips = ctx_bits()
    all_bits = sorted(chips + [1], reverse=True)
    held = partial.reshape((groups,) + (2,) * len(all_bits) + (rows // (groups * number), columns))
    held, left = scatter_ctx_step(held, all_bits, 1)
    half = columns // 2
    pieces = []
    for part, order in ((held[..., :half], chips), (held[..., half:], chips[::-1])):
        part_left = left
        for bit in order:
            part, part_left = scatter_ctx_step(part, part_left, bit)
        pieces.append(part)
    piece = jnp.concatenate(pieces, axis=-1)
    total = lax.dynamic_index_in_dim(piece, own, 0, keepdims=False).astype(F32)
    for step in range(1, groups):
        send = lax.dynamic_index_in_dim(piece, (own + step) % groups, 0, keepdims=False)
        total = total + shift_fsdp(send, step).astype(F32)
    total = total.astype(BF16)
    left_half = gather_ctx(total[:, :half], chips[::-1] + [1])
    right_half = gather_ctx(total[:, half:], chips + [1])
    whole = jnp.concatenate([left_half, right_half], axis=-1)
    return whole.reshape(rows // groups, columns).astype(F32)


def sum_vectors(vectors):
    groups = lax.axis_size("fsdp")
    own = lax.axis_index("fsdp")
    packed = jnp.concatenate([vector.reshape(groups, -1) for vector in vectors], axis=1)
    for bit in [1] + ctx_bits():
        packed = packed + swap(packed, bit)
    total = lax.dynamic_index_in_dim(packed, own, 0, keepdims=False)
    for step in range(1, groups):
        send = lax.dynamic_index_in_dim(packed, (own + step) % groups, 0, keepdims=False)
        total = total + shift_fsdp(send, step)
    owned, at = [], 0
    for vector in vectors:
        width = vector.shape[0] // groups
        owned.append(total[at : at + width])
        at += width
    return owned


def vector_kernel(number, at_ref, *refs):
    rows, (vectors_ref, wide_ref, mix_ref, held) = refs[:-4], refs[-4:]
    groups = len(rows)
    for step in range(groups):
        held[pl.ds(lax.rem(at_ref[1] + groups - step, groups), 1), :] = rows[step][...]
    width = vectors_ref.shape[1] // groups
    wide = wide_ref.shape[1] // groups
    for group in range(groups):
        for at in range(number):
            part = held[group : group + 1, at * width : (at + 1) * width]
            vectors_ref[at : at + 1, group * width : (group + 1) * width] = part
        wide_ref[:, group * wide : (group + 1) * wide] = held[group : group + 1, number * width :]
    model_width = vectors_ref.shape[1]
    mix_ref[...] = jnp.zeros(mix_ref.shape, F32)
    mix_ref[:, :model_width] = vectors_ref[0:1, :]
    mix_ref[:, 2 * model_width :] = vectors_ref[1:2, :]


def pack_vectors(vectors, wide):
    return jnp.concatenate(vectors + [wide])[None].astype(F32)


def gather_vectors(packed, count, width, places):
    groups = lax.axis_size("fsdp")
    rows = [packed] + [shift_fsdp(packed, step) for step in range(1, groups)]
    model_width, wide_width = groups * width, groups * (packed.shape[1] - count * width)
    vmem = pl.BlockSpec(memory_space=pltpu.VMEM)
    return pl.pallas_call(
        functools.partial(vector_kernel, count),
        in_specs=[pl.BlockSpec(memory_space=pltpu.SMEM)] + [vmem] * groups,
        out_specs=[vmem] * 3,
        out_shape=[
            jax.ShapeDtypeStruct((count, model_width), F32),
            jax.ShapeDtypeStruct((1, wide_width), F32),
            jax.ShapeDtypeStruct((1, 3 * model_width), F32),
        ],
        scratch_shapes=[pltpu.VMEM((groups, packed.shape[1]), F32)],
    )(places, *rows)


def after(values, *signs):
    signs = [sign for sign in signs if sign is not None]
    if not signs:
        return values
    return lax.optimization_barrier((values, signs))[0]


def spread_chips(block):
    found = {0: block}
    for bit in range(2, lax.axis_size("ctx"), 2):
        found[bit] = swap(block, bit)
    return found


def copy_kernel(plan, count, at_ref, *refs):
    sources, targets = refs[:count], refs[count : count + 1]
    slots, in_sems, out_sems = refs[count + 1 : -2], refs[-2], refs[-1]
    arrivals = []
    for at in range(count):
        arrivals.append(pltpu.make_async_copy(sources[at], slots[at], in_sems.at[at]))
        arrivals[at].start()
    leaving = []
    for at, moves in enumerate(plan(at_ref, slots, targets[0])):
        arrivals[at].wait()
        for source, target in moves:
            leaving.append(pltpu.make_async_copy(source, target, out_sems.at[len(leaving)]))
            leaving[-1].start()
    for copy in leaving:
        copy.wait()


def assemble(places, sources, shape, plan, copies):
    anywhere = pl.BlockSpec(memory_space=pl.ANY)
    return pl.pallas_call(
        functools.partial(copy_kernel, plan, len(sources)),
        in_specs=[pl.BlockSpec(memory_space=pltpu.SMEM)] + [anywhere] * len(sources),
        out_specs=anywhere,
        out_shape=shape,
        scratch_shapes=[pltpu.VMEM(source.shape, source.dtype) for source in sources]
        + [pltpu.SemaphoreType.DMA((len(sources),)), pltpu.SemaphoreType.DMA((copies,))],
        compiler_params=pltpu.CompilerParams(vmem_limit_bytes=32 * 1024 * 1024),
        cost_estimate=pl.CostEstimate(flops=0, bytes_accessed=10_000_000, transcendentals=0),
    )(places, *sources)


def shift_all(piece):
    return {step: shift_fsdp(piece, step) for step in range(1, lax.axis_size("fsdp"))}


def row_of_step(own, step, rows):
    groups = lax.axis_size("fsdp")
    return pl.ds(lax.rem(own + groups - step, groups) * rows, rows)


def halves_plan(rows, half):
    groups = lax.axis_size("fsdp")

    def plan(at_ref, slots, target):
        own, core_at = at_ref[1], at_ref[0] & 1
        moves = [[(slots[0], target.at[pl.ds(own * rows, rows)])]]
        for at, side in ((1, core_at), (2, 1 - core_at)):
            column = pl.ds(pl.multiple_of(side * half, 128), half)
            moves.append(
                [
                    (slots[at].at[step - 1], target.at[row_of_step(own, step, rows), column])
                    for step in range(1, groups)
                ]
            )
        return moves

    return plan


def core_half(shard):
    rows, columns = shard.shape
    core = lax.axis_index("ctx") % 2
    return lax.dynamic_slice(shard, (0, core * (columns // 2)), (rows, columns // 2))


def stack_steps(fetched):
    return jnp.stack([fetched[step] for step in sorted(fetched)])


def whole_of_halves(shard, mine, theirs, places):
    rows, columns = shard.shape
    groups = lax.axis_size("fsdp")
    shape = jax.ShapeDtypeStruct((groups * rows, columns), shard.dtype)
    plan = halves_plan(rows, columns // 2)
    return assemble(places, [shard, mine, theirs], shape, plan, 2 * groups - 1)


def weight_by_core(shard, places):
    piece = core_half(shard)
    sign = yield piece
    fetched = shift_all(piece)
    far = lax.axis_size("fsdp") // 2
    fetched[far] = after(fetched[far], sign)
    sign = yield fetched[far]
    mine = stack_steps(after(fetched, sign))
    yield mine
    yield whole_of_halves(shard, mine, swap(mine, 1), places)


def two_weights_by_ctx(shard, second, places):
    rows, columns = shard.shape
    number, groups = lax.axis_size("ctx"), lax.axis_size("fsdp")
    me = lax.axis_index("ctx")
    width = columns // number
    piece = lax.dynamic_slice(shard, (0, me * width), (rows, width))
    pieces = jnp.stack([piece, core_half(second)])
    sign = yield pieces
    fetched = stack_steps(after(shift_all(pieces), sign))
    stack, mine = fetched[:, 0], fetched[:, 1]
    sign = yield fetched
    theirs = swap(mine, 1)
    near = spread_chips(stack)
    near_bits = sorted(near)
    near_list = after([near[bit] for bit in near_bits], sign)
    near_stack = jnp.stack(near_list)
    yield near_stack
    across = swap(near_stack, 1)

    def plan(at_ref, slots, target):
        own, at = at_ref[1], at_ref[0]

        def moves_of(slot, other):
            column = pl.ds(pl.multiple_of(other * width, 128), width)
            return [
                (slot.at[step - 1], target.at[row_of_step(own, step, rows), column])
                for step in range(1, groups)
            ]

        moves = [moves_of(slots[index], at ^ bit) for index, bit in enumerate(near_bits)]
        last = []
        for index, bit in enumerate(near_bits):
            last += moves_of(slots[-2].at[index], at ^ bit ^ 1)
        return moves + [last, [(slots[-1], target.at[pl.ds(own * rows, rows)])]]

    shape = jax.ShapeDtypeStruct((groups * rows, columns), shard.dtype)
    whole = assemble(
        places, near_list + [across, shard], shape, plan, number * (groups - 1) + 1
    )
    yield whole, whole_of_halves(second, mine, theirs, places)


def stacked_pieces(grad, blocks):
    groups, chips = lax.axis_size("fsdp"), lax.axis_size("ctx") // 2
    rows, width = grad.shape[0], grad.shape[1] // blocks
    parts = [
        grad[:, at * width : (at + 1) * width].reshape(
            groups, chips, 2, rows // (2 * groups * chips), width
        )
        for at in range(blocks)
    ]
    return jnp.concatenate(parts, axis=3)


def pieces_of(grad, column_blocks):
    groups, chips = lax.axis_size("fsdp"), lax.axis_size("ctx") // 2
    rows, columns = grad.shape
    if column_blocks < 0:
        return stacked_pieces(grad, -column_blocks)
    if column_blocks == 1:
        return grad.reshape(groups, chips, 2, rows // (2 * groups * chips), columns)
    width = columns // chips
    viewed = jnp.stack([grad[:, at * width : (at + 1) * width] for at in range(chips)])
    viewed = viewed.reshape(chips, groups, 2, rows // (2 * groups), width)
    return jnp.swapaxes(viewed, 0, 1)


VECTOR_ROWS = 8


def finish_kernel(near_bits, parts, at_ref, *refs):
    me = at_ref[0]
    sources, outs = refs[: len(near_bits) + 1], refs[len(near_bits) + 1 :]

    def put(values, other):
        first = 0
        for out_ref, (rows, column_blocks) in zip(outs, parts):
            part = values[first : first + rows]
            width = part.shape[1]
            if column_blocks < 0:
                each = rows // -column_blocks
                row = pl.ds(pl.multiple_of(other * each, 8), each)
                for at in range(-column_blocks):
                    piece = part[at * each : (at + 1) * each]
                    out_ref[row, at * width : (at + 1) * width] = piece
            elif column_blocks == 1:
                out_ref[pl.ds(pl.multiple_of(other * rows, 8), rows), :] = part
            else:
                row = pl.ds(pl.multiple_of((other & 1) * rows, 8), rows)
                out_ref[row, pl.ds(pl.multiple_of((other >> 1) * width, 128), width)] = part
            first += rows

    for index, bit in enumerate(near_bits):
        put(sources[index][...].astype(F32), me ^ bit)
        put(sources[-1][index].astype(F32), me ^ bit ^ 1)


def sum_pack(grads, blocks, vectors, places, fsdp_first=False):
    number, groups = lax.axis_size("ctx"), lax.axis_size("fsdp")
    me, own = lax.axis_index("ctx"), lax.axis_index("fsdp")
    core, chip, chips = me % 2, me // 2, number // 2
    views = [pieces_of(grad, block) for grad, block in zip(grads, blocks)]
    width = views[0].shape[4]
    if vectors:
        rows = [vector.reshape(groups, 1, -1) for vector in vectors]
        rows = [jnp.pad(row, ((0, 0), (0, 0), (0, width - row.shape[2]))) for row in rows]
        rows += [jnp.zeros_like(rows[0])] * (number - len(rows))
        view = jnp.concatenate(rows, axis=1).astype(BF16)
        view = view.reshape(groups, chips, 2, 1, width)
        views.append(jnp.pad(view, ((0, 0), (0, 0), (0, 0), (0, VECTOR_ROWS - 1), (0, 0))))

    def side(which):
        parts = [
            jnp.swapaxes(lax.dynamic_index_in_dim(view, which, 2, keepdims=False), 0, 1)
            for view in views
        ]
        return jnp.concatenate(parts, axis=2) if len(parts) > 1 else parts[0]

    send = side(1 - core)
    done_after = yield send
    other = after(swap(send, 1), done_after)
    held = (side(core).astype(F32) + other.astype(F32)).astype(BF16)

    def over_chips(array, axis):
        def part(at):
            return lax.dynamic_index_in_dim(array, at, axis, keepdims=False)

        bits = range(2, number, 2)
        sends = [part(chip ^ (bit // 2)) for bit in bits]
        return part(chip), sends, lambda all_sends: [swap(*pair) for pair in zip(all_sends, bits)]

    def over_fsdp(array, axis):
        def part(at):
            return lax.dynamic_index_in_dim(array, at, axis, keepdims=False)

        steps = range(1, groups)
        sends = [part((own + step) % groups) for step in steps]
        return part(own), sends, lambda all_sends: [shift_fsdp(*p) for p in zip(all_sends, steps)]

    if fsdp_first:
        mine, sends, move = over_fsdp(held, 1)
    else:
        mine, sends, move = over_chips(held, 0)
    start_after, done_after = yield sends
    others = move(after(sends, start_after))
    early = 1 if fsdp_first else len(others) - 1
    total = mine.astype(F32)
    for other in after(others[:early], done_after):
        total = total + other.astype(F32)
    done_after = yield total
    for other in after(others[early:], done_after):
        total = total + other.astype(F32)
    piece = total.astype(BF16)
    mine, sends, move = over_chips(piece, 0) if fsdp_first else over_fsdp(piece, 0)
    done_after = yield sends
    total = mine.astype(F32)
    for other in after(move(sends), done_after):
        total = total + other.astype(F32)
    total = total.astype(BF16)
    done_after = yield total
    near = spread_chips(total)
    near_bits = sorted(near)
    stack = jnp.stack(after([near[bit] for bit in near_bits], done_after))
    yield stack
    across = swap(stack, 1)
    parts = [(view.shape[3], block) for view, block in zip(views, list(blocks) + [1])]
    shapes = [
        jax.ShapeDtypeStruct((grad.shape[0] // groups, grad.shape[1]), F32) for grad in grads
    ]
    if vectors:
        shapes.append(jax.ShapeDtypeStruct((number * VECTOR_ROWS, width), F32))
    vmem = pl.BlockSpec(memory_space=pltpu.VMEM)
    sums = pl.pallas_call(
        functools.partial(finish_kernel, near_bits, parts),
        in_specs=[pl.BlockSpec(memory_space=pltpu.SMEM)] + [vmem] * (len(near_bits) + 1),
        out_specs=[vmem] * len(shapes),
        out_shape=shapes,
        compiler_params=pltpu.CompilerParams(vmem_limit_bytes=32 * 1024 * 1024),
    )(places, *[near[bit] for bit in near_bits], across)
    owned = [
        sums[-1][at * VECTOR_ROWS, : vector.shape[0] // groups]
        for at, vector in enumerate(vectors)
    ]
    yield list(sums[: len(grads)]), owned


def head_masks(rows):
    lane = lax.broadcasted_iota(jnp.int32, (rows, PAIR), 1)
    first = lane < HEAD_DIM
    return (first, jnp.logical_not(first))


def of_head(pair, mask):
    return jnp.where(mask, pair.astype(F32), 0.0).astype(BF16)


def lane_fold(values, combine):
    width = values.shape[1]
    folded = values[:, :PAIR]
    for at in range(PAIR, width, PAIR):
        folded = combine(folded, values[:, at : at + PAIR])
    return folded


def chunk_of(ref, index):
    part = ref[pl.ds(index * CHUNK_BLOCKS, CHUNK_BLOCKS)]
    return part.reshape(part.shape[0] * part.shape[1], PAIR)


def key_bias(length, index, width):
    place = index * width + lax.broadcasted_iota(jnp.int32, (1, width), 1)
    return jnp.where(place < length, 0.0, -1e30)


def by_chunks(length, full, width, run):
    chunks = (length + width - 1) // width
    for number in range(1, full // width + 1):

        def loop(body, state, number=number):
            for index in range(number):
                state = body(index, state)
            return state

        def bias_of(index, number=number):
            return key_bias(length, index, width) if index == number - 1 else None

        pl.when(chunks == number)(functools.partial(run, loop, bias_of))


def forward_kernel(place_ref, q_ref, k_ref, v_ref, att_ref, low_ref, col_ref, row_ref, scores):
    rows = q_ref.shape[1]
    width = CHUNK_BLOCKS * k_ref.shape[1]
    masks = head_masks(rows)
    queries = q_ref[0]
    split = [of_head(queries, mask) for mask in masks]

    def run(loop, bias_of):
        def score_chunk(index, tops):
            keys = chunk_of(k_ref, index)
            new = []
            for head in range(2):
                part = lax.dot_general(split[head], keys, NT, preferred_element_type=F32)
                bias = bias_of(index)
                if bias is not None:
                    part = part + bias
                scores[head, index] = part
                new.append(jnp.maximum(tops[head], lane_fold(part, jnp.maximum)))
            return tuple(new)

        low_start = jnp.full((rows, PAIR), -1e30, F32)
        tops = loop(score_chunk, (low_start, low_start))
        top = [jnp.max(one, axis=1, keepdims=True) * SCORE for one in tops]

        def weigh_chunk(index, state):
            values = chunk_of(v_ref, index)
            new = []
            for head in range(2):
                summed, weighted = state[head]
                weights = jnp.exp2(scores[head, index] * SCORE - top[head])
                summed = summed + lane_fold(weights, jnp.add)
                weighted = weighted + jnp.dot(
                    weights.astype(BF16), values, preferred_element_type=F32
                )
                new.append((summed, weighted))
            return tuple(new)

        zero = jnp.zeros((rows, PAIR), F32)
        state = loop(weigh_chunk, ((zero, zero), (zero, zero)))
        totals = [jnp.sum(state[head][0], axis=1, keepdims=True) for head in range(2)]
        attended = jnp.where(masks[0], state[0][1] / totals[0], state[1][1] / totals[1])
        att_ref[...] = attended
        low_ref[...] = attended.astype(BF16)
        lse = [top[head] + jnp.log2(totals[head]) for head in range(2)]
        column = jnp.where(masks[0], lse[0], lse[1])
        col_ref[...] = column
        turned = jnp.transpose(column)
        row_ref[0, 0:1, :] = turned[0:1, :]
        row_ref[0, 1:2, :] = turned[HEAD_DIM : HEAD_DIM + 1, :]

    by_chunks(place_ref[1], k_ref.shape[0] * k_ref.shape[1], width, run)


def query_kernel(place_ref, q_ref, k_ref, v_ref, g_ref, att_ref, col_ref, out_ref):
    rows = q_ref.shape[1]
    width = CHUNK_BLOCKS * k_ref.shape[1]
    masks = head_masks(rows)
    grads = g_ref[...]
    products = grads.astype(F32) * att_ref[...]
    query_split = [of_head(q_ref[0], mask) for mask in masks]
    grad_split = [of_head(grads, mask) for mask in masks]
    delta = [jnp.sum(jnp.where(mask, products, 0.0), axis=1, keepdims=True) for mask in masks]
    lse = [col_ref[:, 0:1], col_ref[:, HEAD_DIM : HEAD_DIM + 1]]

    def run(loop, bias_of):
        def chunk(index, totals):
            keys = chunk_of(k_ref, index)
            values = chunk_of(v_ref, index)
            new = []
            for head in range(2):
                part = lax.dot_general(query_split[head], keys, NT, preferred_element_type=F32)
                part = part * SCORE - lse[head]
                bias = bias_of(index)
                if bias is not None:
                    part = part + bias
                moved = lax.dot_general(grad_split[head], values, NT, preferred_element_type=F32)
                grad_scores = (jnp.exp2(part) * (moved - delta[head])).astype(BF16)
                new.append(totals[head] + jnp.dot(grad_scores, keys, preferred_element_type=F32))
            return tuple(new)

        zero = jnp.zeros((rows, PAIR), F32)
        totals = loop(chunk, (zero, zero))
        total = jnp.where(masks[0], totals[0], totals[1])
        out_ref[...] = (total * (1.0 / math.sqrt(HEAD_DIM))).astype(BF16)

    by_chunks(place_ref[1], k_ref.shape[0] * k_ref.shape[1], width, run)


def key_kernel(place_ref, k_ref, v_ref, q_ref, g_ref, stat_ref, dk_ref, dv_ref):
    offset, length = place_ref[0] * k_ref.shape[1], place_ref[1]
    rows = k_ref.shape[1]
    chunks = q_ref.shape[0] // CHUNK_BLOCKS
    masks = head_masks(rows)

    @pl.when(offset >= length)
    def _():
        dk_ref[...] = jnp.zeros(dk_ref.shape, BF16)
        dv_ref[...] = jnp.zeros(dv_ref.shape, BF16)

    @pl.when(offset < length)
    def _():
        key_split = [of_head(k_ref[0], mask) for mask in masks]
        value_split = [of_head(v_ref[0], mask) for mask in masks]

        def chunk(index, totals):
            queries = chunk_of(q_ref, index)
            grads = chunk_of(g_ref, index)
            stats = stat_ref[pl.ds(index * CHUNK_BLOCKS, CHUNK_BLOCKS), 0]

            def stat(which):
                return jnp.concatenate(
                    [stats[at, which : which + 1, :] for at in range(CHUNK_BLOCKS)], axis=1
                )

            new = []
            for head in range(2):
                part = lax.dot_general(key_split[head], queries, NT, preferred_element_type=F32)
                weights = jnp.exp2(part * SCORE - stat(head))
                moved = lax.dot_general(value_split[head], grads, NT, preferred_element_type=F32)
                grad_scores = (weights * (moved - stat(2 + head))).astype(BF16)
                grad_keys, grad_values = totals[head]
                grad_keys = grad_keys + jnp.dot(grad_scores, queries, preferred_element_type=F32)
                grad_values = grad_values + jnp.dot(
                    weights.astype(BF16), grads, preferred_element_type=F32
                )
                new.append((grad_keys, grad_values))
            return tuple(new)

        zero = jnp.zeros((rows, PAIR), F32)
        totals = ((zero, zero), (zero, zero))
        for index in range(chunks):
            totals = chunk(index, totals)
        usable = offset + lax.broadcasted_iota(jnp.int32, (rows, PAIR), 0) < length
        grad_keys = jnp.where(masks[0], totals[0][0], totals[1][0])
        grad_values = jnp.where(masks[0], totals[0][1], totals[1][1])
        grad_keys = grad_keys * (1.0 / math.sqrt(HEAD_DIM))
        dk_ref[...] = jnp.where(usable, grad_keys, 0.0).astype(BF16)
        dv_ref[...] = jnp.where(usable, grad_values, 0.0).astype(BF16)


def kernel_call(body, place, operands, in_specs, outs, out_specs, pairs, scratch, flops):
    return pl.pallas_call(
        body,
        grid_spec=pltpu.PrefetchScalarGridSpec(
            num_scalar_prefetch=1,
            grid=(pairs,),
            in_specs=in_specs,
            out_specs=out_specs,
            scratch_shapes=scratch,
        ),
        out_shape=outs,
        compiler_params=pltpu.CompilerParams(vmem_limit_bytes=48 * 1024 * 1024),
        cost_estimate=pl.CostEstimate(flops=flops, bytes_accessed=10_000_000, transcendentals=0),
    )(place, *operands)


def mix_specs(number, seq, tokens, pairs):
    def own(part):
        return pl.BlockSpec(
            (1, None, tokens, PAIR), lambda h, place: (place[0], seq, 0, part * pairs + h)
        )

    def every(part):
        return pl.BlockSpec(
            (number, None, tokens, PAIR), lambda h, place: (0, seq, 0, part * pairs + h)
        )

    return own, every


def mix_kernel(x_ref, weight_ref, add_ref, *refs):
    out_ref = refs[-1]
    for at in range(x_ref.shape[0]):
        mixed = jnp.dot(x_ref[at], weight_ref[...], preferred_element_type=F32)
        out_ref[at] = (mixed + add_ref[...]).astype(BF16)


def mix_tokens(tokens_all, weight, add, first, count, earlier):
    number, seqs, tokens, model_width = tokens_all.shape
    width = weight.shape[1]
    kept = [] if earlier is None else [earlier]
    return pl.pallas_call(
        mix_kernel,
        grid=(count,),
        in_specs=[
            pl.BlockSpec((None, seqs, tokens, model_width), lambda at: (first + at, 0, 0, 0)),
            pl.BlockSpec((model_width, width), lambda at: (0, 0)),
            pl.BlockSpec((1, width), lambda at: (0, 0)),
        ]
        + [pl.BlockSpec(memory_space=pl.ANY)] * len(kept),
        out_specs=pl.BlockSpec((None, seqs, tokens, width), lambda at: (first + at, 0, 0, 0)),
        out_shape=jax.ShapeDtypeStruct((number, seqs, tokens, width), BF16),
        input_output_aliases={3: 0} if kept else {},
        compiler_params=pltpu.CompilerParams(vmem_limit_bytes=48 * 1024 * 1024),
        cost_estimate=pl.CostEstimate(
            flops=2 * count * seqs * tokens * model_width * width,
            bytes_accessed=2 * count * seqs * tokens * (model_width + width),
            transcendentals=0,
        ),
    )(tokens_all, weight, add, *kept)


def outer_kernel(left_ref, right_ref, out_ref):
    out_ref[...] = lax.dot_general(
        left_ref[...], right_ref[...], TN, preferred_element_type=F32
    ).astype(BF16)


def outer_products(left, parts):
    rows, model_width = left.shape
    number, _, columns = parts.shape
    return pl.pallas_call(
        outer_kernel,
        grid=(number,),
        in_specs=[
            pl.BlockSpec((rows, model_width), lambda at: (0, 0)),
            pl.BlockSpec((None, rows, columns), lambda at: (at, 0, 0)),
        ],
        out_specs=pl.BlockSpec((model_width, columns), lambda at: (0, at)),
        out_shape=jax.ShapeDtypeStruct((model_width, number * columns), BF16),
        compiler_params=pltpu.CompilerParams(vmem_limit_bytes=48 * 1024 * 1024),
        cost_estimate=pl.CostEstimate(
            flops=2 * model_width * rows * number * columns,
            bytes_accessed=6_000_000,
            transcendentals=0,
        ),
    )(left, parts)


def attend_forward(place, seq, mix):
    number, _, tokens, width = mix.shape
    model_width = width // 3
    pairs = model_width // PAIR
    own, every = mix_specs(number, seq, tokens, pairs)
    chunk = CHUNK_BLOCKS * tokens
    block = pl.BlockSpec((tokens, PAIR), lambda h, place: (0, h))
    return kernel_call(
        forward_kernel,
        place,
        (mix, mix, mix),
        [own(0), every(1), every(2)],
        (
            jax.ShapeDtypeStruct((tokens, model_width), F32),
            jax.ShapeDtypeStruct((tokens, model_width), BF16),
            jax.ShapeDtypeStruct((tokens, model_width), F32),
            jax.ShapeDtypeStruct((pairs, 2, tokens), F32),
        ),
        (block, block, block, pl.BlockSpec((1, 2, tokens), lambda h, place: (h, 0, 0))),
        pairs,
        [pltpu.VMEM((2, number // CHUNK_BLOCKS, tokens, chunk), F32)],
        56 * number * tokens * tokens * model_width,
    )


def attend_queries(place, seq, mix, grads, attended, column):
    number, _, tokens, width = mix.shape
    model_width = width // 3
    pairs = model_width // PAIR
    own, every = mix_specs(number, seq, tokens, pairs)
    block = pl.BlockSpec((tokens, PAIR), lambda h, place: (0, h))
    return kernel_call(
        query_kernel,
        place,
        (mix, mix, mix, grads, attended, column),
        [own(0), every(1), every(2), block, block, block],
        jax.ShapeDtypeStruct((tokens, model_width), BF16),
        block,
        pairs,
        [],
        56 * number * tokens * tokens * model_width,
    )


def attend_keys(place, seq, mix, all_grads, stats):
    number, _, tokens, width = mix.shape
    model_width = width // 3
    pairs = model_width // PAIR
    own, every = mix_specs(number, seq, tokens, pairs)
    block = pl.BlockSpec((tokens, PAIR), lambda h, place: (0, h))
    return kernel_call(
        key_kernel,
        place,
        (mix, mix, mix, all_grads, stats),
        [
            own(1),
            own(2),
            every(0),
            pl.BlockSpec((number, None, tokens, PAIR), lambda h, place: (0, seq, 0, h)),
            pl.BlockSpec((number, None, 1, 4, tokens), lambda h, place: (0, seq, h, 0, 0)),
        ],
        (
            jax.ShapeDtypeStruct((tokens, model_width), BF16),
            jax.ShapeDtypeStruct((tokens, model_width), BF16),
        ),
        (block, block),
        pairs,
        [],
        72 * number * tokens * tokens * model_width,
    )


def on_device(
    hidden_states,
    lengths,
    cotangent,
    attend_weight,
    query_bias,
    value_bias,
    output_weight,
    output_bias,
    first_gain,
    first_shift,
    raise_weight,
    raise_bias,
    lower_weight,
    lower_bias,
    second_gain,
    second_shift,
):
    seq_count, tok_count, model_width = hidden_states.shape
    row_count = seq_count * tok_count
    block_shape = (seq_count, tok_count, model_width)
    number = lax.axis_size("ctx")
    pairs = model_width // PAIR
    me = lax.axis_index("ctx")
    places = jnp.stack([me, lax.axis_index("fsdp")]).astype(jnp.int32)

    tokens_all = lax.all_gather(hidden_states, "ctx", axis=0, tiled=False)
    attend_stages = weight_by_core(attend_weight, places)
    attend_piece = next(attend_stages)
    vectors = after(
        [
            query_bias,
            value_bias,
            output_bias,
            first_gain,
            first_shift,
            lower_bias,
            second_gain,
            second_shift,
        ],
        attend_piece,
    )
    packed_vectors = pack_vectors(vectors, raise_bias)
    attend_stages.send(packed_vectors)
    attend_sign = attend_stages.send(packed_vectors)
    attend_full = next(attend_stages)
    vector_rows, raise_add, mix_add = gather_vectors(
        packed_vectors, len(vectors), query_bias.shape[0], places
    )
    output_add, gain_first, shift_first, lower_add, gain_second, shift_second = [
        vector_rows[at : at + 1] for at in range(2, 8)
    ]
    packed = (raise_weight.shape[1] // number) == output_weight.shape[1] // 2
    if packed:
        raise_stages = two_weights_by_ctx(
            after(raise_weight, attend_sign), output_weight, places
        )
        raise_sign = next(raise_stages)
    else:
        raise_stages = weight_by_core(raise_weight, places)
        output_stages = weight_by_core(output_weight, places)
        raise_sign = (next(raise_stages), next(output_stages))
    mix = mix_tokens(after(tokens_all, raise_sign), attend_full, mix_add, 0, number, None)
    if packed:
        raise_sign = raise_stages.send(mix)
    lower_stages = weight_by_core(after(lower_weight, raise_sign), places)
    mix = after(mix, raise_sign, next(lower_stages))

    seq_places = [
        jnp.stack([me.astype(jnp.int32), lengths[at].astype(jnp.int32)]) for at in range(seq_count)
    ]
    attended, attended_lows, columns, lse_rows = [], [], [], []
    for at in range(seq_count):
        one, low, column, lse_row = attend_forward(seq_places[at], at, mix)
        attended.append(one)
        attended_lows.append(low)
        columns.append(column)
        lse_rows.append(lse_row)
        if at == 0:
            lower_sign = lower_stages.send(low)
            mix = after(mix, raise_stages.send(low) if packed else None, lower_sign)
    if packed:
        raise_full, output_full = next(raise_stages)
    else:
        for stages in (raise_stages, output_stages):
            stages.send(None)
            stages.send(None)
        next_stage = next(raise_stages), next(output_stages)
        raise_full, output_full = next_stage
    attended_low = jnp.concatenate(attended_lows, axis=0)

    token_rows = hidden_states.reshape(row_count, model_width)
    projected = jnp.dot(attended_low, output_full, preferred_element_type=F32) + output_add
    normed_first, first_back = jax.vjp(
        layer_norm, token_rows.astype(F32) + projected, gain_first, shift_first
    )
    first_low = normed_first.astype(BF16)
    raised = jnp.dot(first_low, raise_full, preferred_element_type=F32) + raise_add
    active, slope = gelu_and_slope(raised)
    active_low, slope = lax.optimization_barrier((active.astype(BF16), slope))
    lower_stages.send(first_low)
    lower_full = next(lower_stages)
    lowered = jnp.dot(active_low, lower_full, preferred_element_type=F32) + lower_add
    result, second_back = jax.vjp(layer_norm, normed_first + lowered, gain_second, shift_second)
    layer_output = result.astype(BF16).reshape(block_shape)
    grad_out = cotangent.reshape(row_count, model_width).astype(F32)
    grad_mid, grad_gain_second, grad_shift_second = second_back(grad_out)
    grad_gain_second, grad_shift_second = grad_gain_second[0], grad_shift_second[0]
    mid_low = grad_mid.astype(BF16)
    shared = model_width % (8 * number * lax.axis_size("fsdp")) == 0
    grad_lower_weight = jnp.einsum("rf,rd->fd", active_low, mid_low, preferred_element_type=F32).astype(BF16)
    if shared:
        lower_pack = sum_pack([grad_lower_weight], [1], [], places, True)
        mid_low = after(mid_low, next(lower_pack))
    grad_lower_add = jnp.sum(mid_low.astype(F32), axis=0)
    grad_active = jnp.einsum("rd,fd->rf", mid_low, lower_full, preferred_element_type=F32)
    raised_low = (slope * grad_active).astype(BF16)
    lower_send = lower_pack.send(raised_low) if shared else None
    grad_raise_weight = jnp.einsum("rd,rf->df", first_low, raised_low, preferred_element_type=F32).astype(BF16)
    grad_raise_add = jnp.sum(raised_low.astype(F32), axis=0)
    grad_first = grad_mid + jnp.einsum(
        "rf,df->rd", raised_low, raise_full, preferred_element_type=F32
    )
    grad_resid, grad_gain_first, grad_shift_first = first_back(grad_first)
    grad_gain_first, grad_shift_first = grad_gain_first[0], grad_shift_first[0]
    resid_low = grad_resid.astype(BF16)
    grad_output_weight = jnp.einsum(
        "rc,rd->cd", attended_low, resid_low, preferred_element_type=F32
    ).astype(BF16)
    grad_output_add = jnp.sum(resid_low.astype(F32), axis=0)
    grad_att = (
        jnp.einsum("rd,cd->rc", resid_low, output_full, preferred_element_type=F32)
        .astype(BF16)
        .reshape(block_shape)
    )
    head_of = lax.broadcasted_iota(jnp.int32, (HEADS, model_width), 1) // HEAD_DIM
    pick = (head_of == lax.broadcasted_iota(jnp.int32, (HEADS, model_width), 0)).astype(F32)
    stats = []
    for at in range(seq_count):
        delta = jnp.einsum(
            "hd,td->ht",
            pick,
            grad_att[at].astype(F32) * attended[at],
            precision=lax.Precision.HIGHEST,
            preferred_element_type=F32,
        ).reshape(pairs, 2, tok_count)
        stats.append(jnp.concatenate([lse_rows[at], delta], axis=1))
    stats = jnp.stack(stats)
    stat_rows = stats.size // (seq_count * model_width)
    rest, coded = stats.reshape(seq_count, stat_rows, model_width), []
    for _ in range(3):
        part = lax.reduce_precision(rest, 8, 7)
        coded.append(part.astype(BF16))
        rest = rest - part
    grads_all = lax.all_gather(
        jnp.concatenate([grad_att] + coded, axis=1), "ctx", axis=0, tiled=False
    )
    coded = grads_all[:, :, tok_count:].astype(F32)
    coded = coded.reshape(number, seq_count, 3, stat_rows, model_width)
    stats_all = (coded[:, :, 0] + coded[:, :, 1] + coded[:, :, 2]).reshape(
        (number,) + stats.shape
    )
    early = [
        grad_output_add,
        grad_gain_first,
        grad_shift_first,
        grad_raise_add,
        grad_lower_add,
        grad_gain_second,
        grad_shift_second,
    ]
    query_grads, key_grads, value_grads = [], [], []
    if shared:
        raise_pack = sum_pack(
            [grad_raise_weight, grad_output_weight], [number // 2, 1], early, places
        )
        mix = after(mix, lower_send, next(raise_pack))
    for at in range(seq_count):
        query_grads.append(
            attend_queries(seq_places[at], at, mix, grad_att[at], attended[at], columns[at])
        )
        if shared and at == 0:
            mix = after(
                mix, lower_pack.send((None, query_grads[0])), raise_pack.send(query_grads[0])
            )
    for at in range(seq_count):
        grad_keys, grad_values = attend_keys(seq_places[at], at, mix, grads_all, stats_all)
        key_grads.append(grad_keys)
        value_grads.append(grad_values)
        if shared and at == 0:
            mix = after(
                mix, raise_pack.send((grads_all, grad_keys)), lower_pack.send(grad_keys)
            )
    if shared:
        raise_sends = raise_pack.send(value_grads[-1])
        value_grads[-1] = after(
            value_grads[-1], raise_sends, lower_pack.send(value_grads[-1])
        )
    query_low = jnp.concatenate(query_grads, axis=0)
    key_low = jnp.concatenate(key_grads, axis=0)
    value_low = jnp.concatenate(value_grads, axis=0)
    grad_mixture = jnp.concatenate([query_low, key_low, value_low], axis=1)
    grad_attend_weight = outer_products(
        token_rows, jnp.stack([query_low, key_low, value_low])
    )
    grad_query_add = jnp.sum(query_low.astype(F32), axis=0)
    grad_value_add = jnp.sum(value_low.astype(F32), axis=0)
    hidden_grad = grad_resid + jnp.einsum(
        "rc,dc->rd", grad_mixture, attend_full, preferred_element_type=F32
    )
    late = [grad_query_add, grad_value_add]
    if shared:
        attend_pack = sum_pack([grad_attend_weight], [-3], late, places)
        next(attend_pack)
        attend_pack.send(None)
        lower_stack = lower_pack.send(grad_attend_weight)
        attend_partial = attend_pack.send(((lower_stack, raise_sends), None))
        raise_pack.send(attend_partial)
        attend_sends = next(attend_pack)
        raise_pack.send(attend_sends)
        next(attend_pack)
        next(attend_pack)
        (grad_attend_weight,), late = next(attend_pack)
        (grad_lower_weight,), _ = next(lower_pack)
        (grad_raise_weight, grad_output_weight), early = next(raise_pack)
    else:
        grad_lower_weight = sum_weight(grad_lower_weight)
        grad_raise_weight = sum_weight(grad_raise_weight)
        grad_output_weight = sum_weight(grad_output_weight)
        grad_attend_weight = sum_weight(grad_attend_weight)
        early, late = sum_vectors(early), sum_vectors(late)
    (
        grad_output_add,
        grad_gain_first,
        grad_shift_first,
        grad_raise_add,
        grad_lower_add,
        grad_gain_second,
        grad_shift_second,
    ) = early
    grad_query_add, grad_value_add = late
    return (
        layer_output,
        hidden_grad.reshape(block_shape),
        grad_attend_weight,
        grad_query_add,
        grad_value_add,
        grad_output_weight,
        grad_output_add,
        grad_gain_first,
        grad_shift_first,
        grad_raise_weight,
        grad_raise_add,
        grad_lower_weight,
        grad_lower_add,
        grad_gain_second,
        grad_shift_second,
    )


def solution(mesh):
    return jax.shard_map(
        on_device,
        mesh=mesh,
        in_specs=(
            P("fsdp", "ctx", None),
            P("fsdp"),
            P("fsdp", "ctx", None),
            P("fsdp", None),
            P("fsdp"),
            P("fsdp"),
            P("fsdp", None),
            P("fsdp"),
            P("fsdp"),
            P("fsdp"),
            P("fsdp", None),
            P("fsdp"),
            P("fsdp", None),
            P("fsdp"),
            P("fsdp"),
            P("fsdp"),
        ),
        out_specs=(
            P("fsdp", "ctx", None),
            P("fsdp", "ctx", None),
            P("fsdp", None),
            P("fsdp"),
            P("fsdp"),
            P("fsdp", None),
            P("fsdp"),
            P("fsdp"),
            P("fsdp"),
            P("fsdp", None),
            P("fsdp"),
            P("fsdp", None),
            P("fsdp"),
            P("fsdp"),
            P("fsdp"),
        ),
        check_vma=False,
    )
```

```python
import functools
import math

import jax
import jax.numpy as jnp
from jax import lax
from jax.experimental import pallas as pl
from jax.experimental.pallas import tpu as pltpu
from jax.sharding import PartitionSpec as P

HEADS = 12
HEAD_DIM = 64
PAIR = 2 * HEAD_DIM
LOG2E = 1.4426950408889634
SCORE = LOG2E / math.sqrt(HEAD_DIM)
F32 = jnp.float32
BF16 = jnp.bfloat16
CHUNK_BLOCKS = 2
NT = (((1,), (1,)), ((), ()))
TN = (((0,), (0,)), ((), ()))


def layer_norm(hidden, gain, shift):
    average = jnp.mean(hidden, axis=-1, keepdims=True)
    centred = hidden - average
    variance = jnp.mean(centred * centred, axis=-1, keepdims=True)
    return centred * lax.rsqrt(variance + 1e-05) * gain + shift


def gelu_and_slope(inputs):
    size = jnp.abs(inputs) * math.sqrt(0.5)
    bell = jnp.exp(-0.5 * inputs * inputs)
    step = 1.0 / (1.0 + 0.3275911 * size)
    series = 1.061405429 * step - 1.453152027
    series = series * step + 1.421413741
    series = series * step - 0.284496736
    series = series * step + 0.254829592
    tail = 0.5 * series * step * bell
    below = jnp.where(inputs < 0.0, tail, 1.0 - tail)
    return inputs * below, below + inputs * bell * (1.0 / math.sqrt(2.0 * math.pi))


def swap(value, bit):
    number = lax.axis_size("ctx")
    return lax.ppermute(value, "ctx", [(at, at ^ bit) for at in range(number)])


def shift_fsdp(value, step):
    number = lax.axis_size("fsdp")
    return lax.ppermute(value, "fsdp", [(at, (at + step) % number) for at in range(number)])


def ctx_bits():
    bits, bit = [], 2
    while bit < lax.axis_size("ctx"):
        bits.append(bit)
        bit *= 2
    return bits


def gather_ctx(piece, order):
    me = lax.axis_index("ctx")
    held, done = piece, []
    for bit in order:
        other = swap(held, bit)
        high = (me & bit) != 0
        place = sum(1 for earlier in done if earlier > bit)
        held = jnp.stack([jnp.where(high, other, held), jnp.where(high, held, other)], axis=place)
        done.append(bit)
    return held.reshape((lax.axis_size("ctx"),) + piece.shape)


def scatter_ctx_step(held, bits_left, bit):
    me = lax.axis_index("ctx")
    high = (me & bit) // bit
    axis = 1 + bits_left.index(bit)
    mine = lax.dynamic_index_in_dim(held, high, axis, keepdims=False)
    send = lax.dynamic_index_in_dim(held, 1 - high, axis, keepdims=False).astype(BF16)
    total = mine.astype(F32) + swap(send, bit).astype(F32)
    return total.astype(BF16), [left for left in bits_left if left != bit]


def sum_weight(partial):
    rows, columns = partial.shape
    number, groups = lax.axis_size("ctx"), lax.axis_size("fsdp")
    own = lax.axis_index("fsdp")
    chips = ctx_bits()
    all_bits = sorted(chips + [1], reverse=True)
    held = partial.reshape((groups,) + (2,) * len(all_bits) + (rows // (groups * number), columns))
    held, left = scatter_ctx_step(held, all_bits, 1)
    half = columns // 2
    pieces = []
    for part, order in ((held[..., :half], chips), (held[..., half:], chips[::-1])):
        part_left = left
        for bit in order:
            part, part_left = scatter_ctx_step(part, part_left, bit)
        pieces.append(part)
    piece = jnp.concatenate(pieces, axis=-1)
    total = lax.dynamic_index_in_dim(piece, own, 0, keepdims=False).astype(F32)
    for step in range(1, groups):
        send = lax.dynamic_index_in_dim(piece, (own + step) % groups, 0, keepdims=False)
        total = total + shift_fsdp(send, step).astype(F32)
    total = total.astype(BF16)
    left_half = gather_ctx(total[:, :half], chips[::-1] + [1])
    right_half = gather_ctx(total[:, half:], chips + [1])
    whole = jnp.concatenate([left_half, right_half], axis=-1)
    return whole.reshape(rows // groups, columns).astype(F32)


def sum_vectors(vectors):
    groups = lax.axis_size("fsdp")
    own = lax.axis_index("fsdp")
    packed = jnp.concatenate([vector.reshape(groups, -1) for vector in vectors], axis=1)
    for bit in [1] + ctx_bits():
        packed = packed + swap(packed, bit)
    total = lax.dynamic_index_in_dim(packed, own, 0, keepdims=False)
    for step in range(1, groups):
        send = lax.dynamic_index_in_dim(packed, (own + step) % groups, 0, keepdims=False)
        total = total + shift_fsdp(send, step)
    owned, at = [], 0
    for vector in vectors:
        width = vector.shape[0] // groups
        owned.append(total[at : at + width])
        at += width
    return owned


def vector_kernel(number, at_ref, *refs):
    rows, (vectors_ref, wide_ref, mix_ref, held) = refs[:-4], refs[-4:]
    groups = len(rows)
    for step in range(groups):
        held[pl.ds(lax.rem(at_ref[1] + groups - step, groups), 1), :] = rows[step][...]
    width = vectors_ref.shape[1] // groups
    wide = wide_ref.shape[1] // groups
    for group in range(groups):
        for at in range(number):
            part = held[group : group + 1, at * width : (at + 1) * width]
            vectors_ref[at : at + 1, group * width : (group + 1) * width] = part
        wide_ref[:, group * wide : (group + 1) * wide] = held[group : group + 1, number * width :]
    model_width = vectors_ref.shape[1]
    mix_ref[...] = jnp.zeros(mix_ref.shape, F32)
    mix_ref[:, :model_width] = vectors_ref[0:1, :]
    mix_ref[:, 2 * model_width :] = vectors_ref[1:2, :]


def pack_vectors(vectors, wide):
    return jnp.concatenate(vectors + [wide])[None].astype(F32)


def gather_vectors(packed, count, width, places):
    groups = lax.axis_size("fsdp")
    rows = [packed] + [shift_fsdp(packed, step) for step in range(1, groups)]
    model_width, wide_width = groups * width, groups * (packed.shape[1] - count * width)
    vmem = pl.BlockSpec(memory_space=pltpu.VMEM)
    return pl.pallas_call(
        functools.partial(vector_kernel, count),
        in_specs=[pl.BlockSpec(memory_space=pltpu.SMEM)] + [vmem] * groups,
        out_specs=[vmem] * 3,
        out_shape=[
            jax.ShapeDtypeStruct((count, model_width), F32),
            jax.ShapeDtypeStruct((1, wide_width), F32),
            jax.ShapeDtypeStruct((1, 3 * model_width), F32),
        ],
        scratch_shapes=[pltpu.VMEM((groups, packed.shape[1]), F32)],
    )(places, *rows)


def after(values, *signs):
    signs = [sign for sign in signs if sign is not None]
    if not signs:
        return values
    return lax.optimization_barrier((values, signs))[0]


def spread_chips(block):
    found = {0: block}
    for bit in range(2, lax.axis_size("ctx"), 2):
        found[bit] = swap(block, bit)
    return found


def copy_kernel(plan, count, at_ref, *refs):
    sources, targets = refs[:count], refs[count : count + 1]
    slots, in_sems, out_sems = refs[count + 1 : -2], refs[-2], refs[-1]
    arrivals = []
    for at in range(count):
        arrivals.append(pltpu.make_async_copy(sources[at], slots[at], in_sems.at[at]))
        arrivals[at].start()
    leaving = []
    for at, moves in enumerate(plan(at_ref, slots, targets[0])):
        arrivals[at].wait()
        for source, target in moves:
            leaving.append(pltpu.make_async_copy(source, target, out_sems.at[len(leaving)]))
            leaving[-1].start()
    for copy in leaving:
        copy.wait()


def assemble(places, sources, shape, plan, copies):
    anywhere = pl.BlockSpec(memory_space=pl.ANY)
    return pl.pallas_call(
        functools.partial(copy_kernel, plan, len(sources)),
        in_specs=[pl.BlockSpec(memory_space=pltpu.SMEM)] + [anywhere] * len(sources),
        out_specs=anywhere,
        out_shape=shape,
        scratch_shapes=[pltpu.VMEM(source.shape, source.dtype) for source in sources]
        + [pltpu.SemaphoreType.DMA((len(sources),)), pltpu.SemaphoreType.DMA((copies,))],
        compiler_params=pltpu.CompilerParams(vmem_limit_bytes=32 * 1024 * 1024),
        cost_estimate=pl.CostEstimate(flops=0, bytes_accessed=10_000_000, transcendentals=0),
    )(places, *sources)


def shift_all(piece):
    return {step: shift_fsdp(piece, step) for step in range(1, lax.axis_size("fsdp"))}


def row_of_step(own, step, rows):
    groups = lax.axis_size("fsdp")
    return pl.ds(lax.rem(own + groups - step, groups) * rows, rows)


def halves_plan(rows, half):
    groups = lax.axis_size("fsdp")

    def plan(at_ref, slots, target):
        own, core_at = at_ref[1], at_ref[0] & 1
        moves = [[(slots[0], target.at[pl.ds(own * rows, rows)])]]
        for at, side in ((1, core_at), (2, 1 - core_at)):
            column = pl.ds(pl.multiple_of(side * half, 128), half)
            moves.append(
                [
                    (slots[at].at[step - 1], target.at[row_of_step(own, step, rows), column])
                    for step in range(1, groups)
                ]
            )
        return moves

    return plan


def core_half(shard):
    rows, columns = shard.shape
    core = lax.axis_index("ctx") % 2
    return lax.dynamic_slice(shard, (0, core * (columns // 2)), (rows, columns // 2))


def stack_steps(fetched):
    return jnp.stack([fetched[step] for step in sorted(fetched)])


def whole_of_halves(shard, mine, theirs, places):
    rows, columns = shard.shape
    groups = lax.axis_size("fsdp")
    shape = jax.ShapeDtypeStruct((groups * rows, columns), shard.dtype)
    plan = halves_plan(rows, columns // 2)
    return assemble(places, [shard, mine, theirs], shape, plan, 2 * groups - 1)


def weight_by_core(shard, places):
    piece = core_half(shard)
    sign = yield piece
    fetched = shift_all(piece)
    far = lax.axis_size("fsdp") // 2
    fetched[far] = after(fetched[far], sign)
    sign = yield fetched[far]
    mine = stack_steps(after(fetched, sign))
    yield mine
    yield whole_of_halves(shard, mine, swap(mine, 1), places)


def two_weights_by_ctx(shard, second, places):
    rows, columns = shard.shape
    number, groups = lax.axis_size("ctx"), lax.axis_size("fsdp")
    me = lax.axis_index("ctx")
    width = columns // number
    piece = lax.dynamic_slice(shard, (0, me * width), (rows, width))
    pieces = jnp.stack([piece, core_half(second)])
    sign = yield pieces
    fetched = stack_steps(after(shift_all(pieces), sign))
    stack, mine = fetched[:, 0], fetched[:, 1]
    sign = yield fetched
    theirs = swap(mine, 1)
    near = spread_chips(stack)
    near_bits = sorted(near)
    near_list = after([near[bit] for bit in near_bits], sign)
    near_stack = jnp.stack(near_list)
    yield near_stack
    across = swap(near_stack, 1)

    def plan(at_ref, slots, target):
        own, at = at_ref[1], at_ref[0]

        def moves_of(slot, other):
            column = pl.ds(pl.multiple_of(other * width, 128), width)
            return [
                (slot.at[step - 1], target.at[row_of_step(own, step, rows), column])
                for step in range(1, groups)
            ]

        moves = [moves_of(slots[index], at ^ bit) for index, bit in enumerate(near_bits)]
        last = []
        for index, bit in enumerate(near_bits):
            last += moves_of(slots[-2].at[index], at ^ bit ^ 1)
        return moves + [last, [(slots[-1], target.at[pl.ds(own * rows, rows)])]]

    shape = jax.ShapeDtypeStruct((groups * rows, columns), shard.dtype)
    whole = assemble(
        places, near_list + [across, shard], shape, plan, number * (groups - 1) + 1
    )
    yield whole, whole_of_halves(second, mine, theirs, places)


def stacked_pieces(grad, blocks):
    groups, chips = lax.axis_size("fsdp"), lax.axis_size("ctx") // 2
    rows, width = grad.shape[0], grad.shape[1] // blocks
    parts = [
        grad[:, at * width : (at + 1) * width].reshape(
            groups, chips, 2, rows // (2 * groups * chips), width
        )
        for at in range(blocks)
    ]
    return jnp.concatenate(parts, axis=3)


def pieces_of(grad, column_blocks):
    groups, chips = lax.axis_size("fsdp"), lax.axis_size("ctx") // 2
    rows, columns = grad.shape
    if column_blocks < 0:
        return stacked_pieces(grad, -column_blocks)
    if column_blocks == 1:
        return grad.reshape(groups, chips, 2, rows // (2 * groups * chips), columns)
    width = columns // chips
    viewed = jnp.stack([grad[:, at * width : (at + 1) * width] for at in range(chips)])
    viewed = viewed.reshape(chips, groups, 2, rows // (2 * groups), width)
    return jnp.swapaxes(viewed, 0, 1)


VECTOR_ROWS = 8


def finish_kernel(near_bits, parts, at_ref, *refs):
    me = at_ref[0]
    sources, outs = refs[: len(near_bits) + 1], refs[len(near_bits) + 1 :]

    def put(values, other):
        first = 0
        for out_ref, (rows, column_blocks) in zip(outs, parts):
            part = values[first : first + rows]
            width = part.shape[1]
            if column_blocks < 0:
                each = rows // -column_blocks
                row = pl.ds(pl.multiple_of(other * each, 8), each)
                for at in range(-column_blocks):
                    piece = part[at * each : (at + 1) * each]
                    out_ref[row, at * width : (at + 1) * width] = piece
            elif column_blocks == 1:
                out_ref[pl.ds(pl.multiple_of(other * rows, 8), rows), :] = part
            else:
                row = pl.ds(pl.multiple_of((other & 1) * rows, 8), rows)
                out_ref[row, pl.ds(pl.multiple_of((other >> 1) * width, 128), width)] = part
            first += rows

    for index, bit in enumerate(near_bits):
        put(sources[index][...].astype(F32), me ^ bit)
        put(sources[-1][index].astype(F32), me ^ bit ^ 1)


def sum_pack(grads, blocks, vectors, places, fsdp_first=False):
    number, groups = lax.axis_size("ctx"), lax.axis_size("fsdp")
    me, own = lax.axis_index("ctx"), lax.axis_index("fsdp")
    core, chip, chips = me % 2, me // 2, number // 2
    views = [pieces_of(grad, block) for grad, block in zip(grads, blocks)]
    width = views[0].shape[4]
    if vectors:
        rows = [vector.reshape(groups, 1, -1) for vector in vectors]
        rows = [jnp.pad(row, ((0, 0), (0, 0), (0, width - row.shape[2]))) for row in rows]
        rows += [jnp.zeros_like(rows[0])] * (number - len(rows))
        view = jnp.concatenate(rows, axis=1).astype(BF16)
        view = view.reshape(groups, chips, 2, 1, width)
        views.append(jnp.pad(view, ((0, 0), (0, 0), (0, 0), (0, VECTOR_ROWS - 1), (0, 0))))

    def side(which):
        parts = [
            jnp.swapaxes(lax.dynamic_index_in_dim(view, which, 2, keepdims=False), 0, 1)
            for view in views
        ]
        return jnp.concatenate(parts, axis=2) if len(parts) > 1 else parts[0]

    send = side(1 - core)
    done_after = yield send
    other = after(swap(send, 1), done_after)
    held = (side(core).astype(F32) + other.astype(F32)).astype(BF16)

    def over_chips(array, axis):
        def part(at):
            return lax.dynamic_index_in_dim(array, at, axis, keepdims=False)

        bits = range(2, number, 2)
        sends = [part(chip ^ (bit // 2)) for bit in bits]
        return part(chip), sends, lambda all_sends: [swap(*pair) for pair in zip(all_sends, bits)]

    def over_fsdp(array, axis):
        def part(at):
            return lax.dynamic_index_in_dim(array, at, axis, keepdims=False)

        steps = range(1, groups)
        sends = [part((own + step) % groups) for step in steps]
        return part(own), sends, lambda all_sends: [shift_fsdp(*p) for p in zip(all_sends, steps)]

    if fsdp_first:
        mine, sends, move = over_fsdp(held, 1)
    else:
        mine, sends, move = over_chips(held, 0)
    start_after, done_after = yield sends
    others = move(after(sends, start_after))
    early = 1 if fsdp_first else len(others) - 1
    total = mine.astype(F32)
    for other in after(others[:early], done_after):
        total = total + other.astype(F32)
    done_after = yield total
    for other in after(others[early:], done_after):
        total = total + other.astype(F32)
    piece = total.astype(BF16)
    mine, sends, move = over_chips(piece, 0) if fsdp_first else over_fsdp(piece, 0)
    done_after = yield sends
    total = mine.astype(F32)
    for other in after(move(sends), done_after):
        total = total + other.astype(F32)
    total = total.astype(BF16)
    done_after = yield total
    near = spread_chips(total)
    near_bits = sorted(near)
    stack = jnp.stack(after([near[bit] for bit in near_bits], done_after))
    yield stack
    across = swap(stack, 1)
    parts = [(view.shape[3], block) for view, block in zip(views, list(blocks) + [1])]
    shapes = [
        jax.ShapeDtypeStruct((grad.shape[0] // groups, grad.shape[1]), F32) for grad in grads
    ]
    if vectors:
        shapes.append(jax.ShapeDtypeStruct((number * VECTOR_ROWS, width), F32))
    vmem = pl.BlockSpec(memory_space=pltpu.VMEM)
    sums = pl.pallas_call(
        functools.partial(finish_kernel, near_bits, parts),
        in_specs=[pl.BlockSpec(memory_space=pltpu.SMEM)] + [vmem] * (len(near_bits) + 1),
        out_specs=[vmem] * len(shapes),
        out_shape=shapes,
        compiler_params=pltpu.CompilerParams(vmem_limit_bytes=32 * 1024 * 1024),
    )(places, *[near[bit] for bit in near_bits], across)
    owned = [
        sums[-1][at * VECTOR_ROWS, : vector.shape[0] // groups]
        for at, vector in enumerate(vectors)
    ]
    yield list(sums[: len(grads)]), owned


def head_masks(rows):
    lane = lax.broadcasted_iota(jnp.int32, (rows, PAIR), 1)
    first = lane < HEAD_DIM
    return (first, jnp.logical_not(first))


def of_head(pair, mask):
    return jnp.where(mask, pair.astype(F32), 0.0).astype(BF16)


def lane_fold(values, combine):
    width = values.shape[1]
    folded = values[:, :PAIR]
    for at in range(PAIR, width, PAIR):
        folded = combine(folded, values[:, at : at + PAIR])
    return folded


def chunk_of(ref, index):
    part = ref[pl.ds(index * CHUNK_BLOCKS, CHUNK_BLOCKS)]
    return part.reshape(part.shape[0] * part.shape[1], PAIR)


def key_bias(length, index, width):
    place = index * width + lax.broadcasted_iota(jnp.int32, (1, width), 1)
    return jnp.where(place < length, 0.0, -1e30)


def by_chunks(length, full, width, run):
    chunks = (length + width - 1) // width
    for number in range(1, full // width + 1):

        def loop(body, state, number=number):
            for index in range(number):
                state = body(index, state)
            return state

        def bias_of(index, number=number):
            return key_bias(length, index, width) if index == number - 1 else None

        pl.when(chunks == number)(functools.partial(run, loop, bias_of))


def forward_kernel(place_ref, q_ref, k_ref, v_ref, att_ref, low_ref, col_ref, row_ref, scores):
    rows = q_ref.shape[1]
    width = CHUNK_BLOCKS * k_ref.shape[1]
    masks = head_masks(rows)
    queries = q_ref[0]
    split = [of_head(queries, mask) for mask in masks]

    def run(loop, bias_of):
        def score_chunk(index, tops):
            keys = chunk_of(k_ref, index)
            new = []
            for head in range(2):
                part = lax.dot_general(split[head], keys, NT, preferred_element_type=F32)
                bias = bias_of(index)
                if bias is not None:
                    part = part + bias
                scores[head, index] = part
                new.append(jnp.maximum(tops[head], lane_fold(part, jnp.maximum)))
            return tuple(new)

        low_start = jnp.full((rows, PAIR), -1e30, F32)
        tops = loop(score_chunk, (low_start, low_start))
        top = [jnp.max(one, axis=1, keepdims=True) * SCORE for one in tops]

        def weigh_chunk(index, state):
            values = chunk_of(v_ref, index)
            new = []
            for head in range(2):
                summed, weighted = state[head]
                weights = jnp.exp2(scores[head, index] * SCORE - top[head])
                summed = summed + lane_fold(weights, jnp.add)
                weighted = weighted + jnp.dot(
                    weights.astype(BF16), values, preferred_element_type=F32
                )
                new.append((summed, weighted))
            return tuple(new)

        zero = jnp.zeros((rows, PAIR), F32)
        state = loop(weigh_chunk, ((zero, zero), (zero, zero)))
        totals = [jnp.sum(state[head][0], axis=1, keepdims=True) for head in range(2)]
        attended = jnp.where(masks[0], state[0][1] / totals[0], state[1][1] / totals[1])
        att_ref[...] = attended
        low_ref[...] = attended.astype(BF16)
        lse = [top[head] + jnp.log2(totals[head]) for head in range(2)]
        column = jnp.where(masks[0], lse[0], lse[1])
        col_ref[...] = column
        turned = jnp.transpose(column)
        row_ref[0, 0:1, :] = turned[0:1, :]
        row_ref[0, 1:2, :] = turned[HEAD_DIM : HEAD_DIM + 1, :]

    by_chunks(place_ref[1], k_ref.shape[0] * k_ref.shape[1], width, run)


def query_kernel(place_ref, q_ref, k_ref, v_ref, g_ref, att_ref, col_ref, out_ref):
    rows = q_ref.shape[1]
    width = CHUNK_BLOCKS * k_ref.shape[1]
    masks = head_masks(rows)
    grads = g_ref[...]
    products = grads.astype(F32) * att_ref[...]
    query_split = [of_head(q_ref[0], mask) for mask in masks]
    grad_split = [of_head(grads, mask) for mask in masks]
    delta = [jnp.sum(jnp.where(mask, products, 0.0), axis=1, keepdims=True) for mask in masks]
    lse = [col_ref[:, 0:1], col_ref[:, HEAD_DIM : HEAD_DIM + 1]]

    def run(loop, bias_of):
        def chunk(index, totals):
            keys = chunk_of(k_ref, index)
            values = chunk_of(v_ref, index)
            new = []
            for head in range(2):
                part = lax.dot_general(query_split[head], keys, NT, preferred_element_type=F32)
                part = part * SCORE - lse[head]
                bias = bias_of(index)
                if bias is not None:
                    part = part + bias
                moved = lax.dot_general(grad_split[head], values, NT, preferred_element_type=F32)
                grad_scores = (jnp.exp2(part) * (moved - delta[head])).astype(BF16)
                new.append(totals[head] + jnp.dot(grad_scores, keys, preferred_element_type=F32))
            return tuple(new)

        zero = jnp.zeros((rows, PAIR), F32)
        totals = loop(chunk, (zero, zero))
        total = jnp.where(masks[0], totals[0], totals[1])
        out_ref[...] = (total * (1.0 / math.sqrt(HEAD_DIM))).astype(BF16)

    by_chunks(place_ref[1], k_ref.shape[0] * k_ref.shape[1], width, run)


def key_kernel(place_ref, k_ref, v_ref, q_ref, g_ref, stat_ref, dk_ref, dv_ref):
    offset, length = place_ref[0] * k_ref.shape[1], place_ref[1]
    rows = k_ref.shape[1]
    chunks = q_ref.shape[0] // CHUNK_BLOCKS
    masks = head_masks(rows)

    @pl.when(offset >= length)
    def _():
        dk_ref[...] = jnp.zeros(dk_ref.shape, BF16)
        dv_ref[...] = jnp.zeros(dv_ref.shape, BF16)

    @pl.when(offset < length)
    def _():
        key_split = [of_head(k_ref[0], mask) for mask in masks]
        value_split = [of_head(v_ref[0], mask) for mask in masks]

        def chunk(index, totals):
            queries = chunk_of(q_ref, index)
            grads = chunk_of(g_ref, index)
            stats = stat_ref[pl.ds(index * CHUNK_BLOCKS, CHUNK_BLOCKS), 0]

            def stat(which):
                return jnp.concatenate(
                    [stats[at, which : which + 1, :] for at in range(CHUNK_BLOCKS)], axis=1
                )

            new = []
            for head in range(2):
                part = lax.dot_general(key_split[head], queries, NT, preferred_element_type=F32)
                weights = jnp.exp2(part * SCORE - stat(head))
                moved = lax.dot_general(value_split[head], grads, NT, preferred_element_type=F32)
                grad_scores = (weights * (moved - stat(2 + head))).astype(BF16)
                grad_keys, grad_values = totals[head]
                grad_keys = grad_keys + jnp.dot(grad_scores, queries, preferred_element_type=F32)
                grad_values = grad_values + jnp.dot(
                    weights.astype(BF16), grads, preferred_element_type=F32
                )
                new.append((grad_keys, grad_values))
            return tuple(new)

        zero = jnp.zeros((rows, PAIR), F32)
        totals = ((zero, zero), (zero, zero))
        for index in range(chunks):
            totals = chunk(index, totals)
        usable = offset + lax.broadcasted_iota(jnp.int32, (rows, PAIR), 0) < length
        grad_keys = jnp.where(masks[0], totals[0][0], totals[1][0])
        grad_values = jnp.where(masks[0], totals[0][1], totals[1][1])
        grad_keys = grad_keys * (1.0 / math.sqrt(HEAD_DIM))
        dk_ref[...] = jnp.where(usable, grad_keys, 0.0).astype(BF16)
        dv_ref[...] = jnp.where(usable, grad_values, 0.0).astype(BF16)


def kernel_call(body, place, operands, in_specs, outs, out_specs, pairs, scratch, flops):
    return pl.pallas_call(
        body,
        grid_spec=pltpu.PrefetchScalarGridSpec(
            num_scalar_prefetch=1,
            grid=(pairs,),
            in_specs=in_specs,
            out_specs=out_specs,
            scratch_shapes=scratch,
        ),
        out_shape=outs,
        compiler_params=pltpu.CompilerParams(vmem_limit_bytes=48 * 1024 * 1024),
        cost_estimate=pl.CostEstimate(flops=flops, bytes_accessed=10_000_000, transcendentals=0),
    )(place, *operands)


def mix_specs(number, seq, tokens, pairs):
    def own(part):
        return pl.BlockSpec(
            (1, None, tokens, PAIR), lambda h, place: (place[0], seq, 0, part * pairs + h)
        )

    def every(part):
        return pl.BlockSpec(
            (number, None, tokens, PAIR), lambda h, place: (0, seq, 0, part * pairs + h)
        )

    return own, every


def mix_kernel(x_ref, weight_ref, add_ref, *refs):
    out_ref = refs[-1]
    for at in range(x_ref.shape[0]):
        mixed = jnp.dot(x_ref[at], weight_ref[...], preferred_element_type=F32)
        out_ref[at] = (mixed + add_ref[...]).astype(BF16)


def mix_tokens(tokens_all, weight, add, first, count, earlier):
    number, seqs, tokens, model_width = tokens_all.shape
    width = weight.shape[1]
    kept = [] if earlier is None else [earlier]
    return pl.pallas_call(
        mix_kernel,
        grid=(count,),
        in_specs=[
            pl.BlockSpec((None, seqs, tokens, model_width), lambda at: (first + at, 0, 0, 0)),
            pl.BlockSpec((model_width, width), lambda at: (0, 0)),
            pl.BlockSpec((1, width), lambda at: (0, 0)),
        ]
        + [pl.BlockSpec(memory_space=pl.ANY)] * len(kept),
        out_specs=pl.BlockSpec((None, seqs, tokens, width), lambda at: (first + at, 0, 0, 0)),
        out_shape=jax.ShapeDtypeStruct((number, seqs, tokens, width), BF16),
        input_output_aliases={3: 0} if kept else {},
        compiler_params=pltpu.CompilerParams(vmem_limit_bytes=48 * 1024 * 1024),
        cost_estimate=pl.CostEstimate(
            flops=2 * count * seqs * tokens * model_width * width,
            bytes_accessed=2 * count * seqs * tokens * (model_width + width),
            transcendentals=0,
        ),
    )(tokens_all, weight, add, *kept)


def outer_kernel(left_ref, right_ref, out_ref):
    out_ref[...] = lax.dot_general(
        left_ref[...], right_ref[...], TN, preferred_element_type=F32
    ).astype(BF16)


def outer_products(left, parts):
    rows, model_width = left.shape
    number, _, columns = parts.shape
    return pl.pallas_call(
        outer_kernel,
        grid=(number,),
        in_specs=[
            pl.BlockSpec((rows, model_width), lambda at: (0, 0)),
            pl.BlockSpec((None, rows, columns), lambda at: (at, 0, 0)),
        ],
        out_specs=pl.BlockSpec((model_width, columns), lambda at: (0, at)),
        out_shape=jax.ShapeDtypeStruct((model_width, number * columns), BF16),
        compiler_params=pltpu.CompilerParams(vmem_limit_bytes=48 * 1024 * 1024),
        cost_estimate=pl.CostEstimate(
            flops=2 * model_width * rows * number * columns,
            bytes_accessed=6_000_000,
            transcendentals=0,
        ),
    )(left, parts)


def attend_forward(place, seq, mix):
    number, _, tokens, width = mix.shape
    model_width = width // 3
    pairs = model_width // PAIR
    own, every = mix_specs(number, seq, tokens, pairs)
    chunk = CHUNK_BLOCKS * tokens
    block = pl.BlockSpec((tokens, PAIR), lambda h, place: (0, h))
    return kernel_call(
        forward_kernel,
        place,
        (mix, mix, mix),
        [own(0), every(1), every(2)],
        (
            jax.ShapeDtypeStruct((tokens, model_width), F32),
            jax.ShapeDtypeStruct((tokens, model_width), BF16),
            jax.ShapeDtypeStruct((tokens, model_width), F32),
            jax.ShapeDtypeStruct((pairs, 2, tokens), F32),
        ),
        (block, block, block, pl.BlockSpec((1, 2, tokens), lambda h, place: (h, 0, 0))),
        pairs,
        [pltpu.VMEM((2, number // CHUNK_BLOCKS, tokens, chunk), F32)],
        56 * number * tokens * tokens * model_width,
    )


def attend_queries(place, seq, mix, grads, attended, column):
    number, _, tokens, width = mix.shape
    model_width = width // 3
    pairs = model_width // PAIR
    own, every = mix_specs(number, seq, tokens, pairs)
    block = pl.BlockSpec((tokens, PAIR), lambda h, place: (0, h))
    return kernel_call(
        query_kernel,
        place,
        (mix, mix, mix, grads, attended, column),
        [own(0), every(1), every(2), block, block, block],
        jax.ShapeDtypeStruct((tokens, model_width), BF16),
        block,
        pairs,
        [],
        56 * number * tokens * tokens * model_width,
    )


def attend_keys(place, seq, mix, all_grads, stats):
    number, _, tokens, width = mix.shape
    model_width = width // 3
    pairs = model_width // PAIR
    own, every = mix_specs(number, seq, tokens, pairs)
    block = pl.BlockSpec((tokens, PAIR), lambda h, place: (0, h))
    return kernel_call(
        key_kernel,
        place,
        (mix, mix, mix, all_grads, stats),
        [
            own(1),
            own(2),
            every(0),
            pl.BlockSpec((number, None, tokens, PAIR), lambda h, place: (0, seq, 0, h)),
            pl.BlockSpec((number, None, 1, 4, tokens), lambda h, place: (0, seq, h, 0, 0)),
        ],
        (
            jax.ShapeDtypeStruct((tokens, model_width), BF16),
            jax.ShapeDtypeStruct((tokens, model_width), BF16),
        ),
        (block, block),
        pairs,
        [],
        72 * number * tokens * tokens * model_width,
    )


def on_device(
    hidden_states,
    lengths,
    cotangent,
    attend_weight,
    query_bias,
    value_bias,
    output_weight,
    output_bias,
    first_gain,
    first_shift,
    raise_weight,
    raise_bias,
    lower_weight,
    lower_bias,
    second_gain,
    second_shift,
):
    seq_count, tok_count, model_width = hidden_states.shape
    row_count = seq_count * tok_count
    block_shape = (seq_count, tok_count, model_width)
    number = lax.axis_size("ctx")
    pairs = model_width // PAIR
    me = lax.axis_index("ctx")
    places = jnp.stack([me, lax.axis_index("fsdp")]).astype(jnp.int32)

    tokens_all = lax.all_gather(hidden_states, "ctx", axis=0, tiled=False)
    attend_stages = weight_by_core(attend_weight, places)
    attend_piece = next(attend_stages)
    vectors = after(
        [
            query_bias,
            value_bias,
            output_bias,
            first_gain,
            first_shift,
            lower_bias,
            second_gain,
            second_shift,
        ],
        attend_piece,
    )
    packed_vectors = pack_vectors(vectors, raise_bias)
    attend_stages.send(packed_vectors)
    attend_sign = attend_stages.send(packed_vectors)
    attend_full = next(attend_stages)
    vector_rows, raise_add, mix_add = gather_vectors(
        packed_vectors, len(vectors), query_bias.shape[0], places
    )
    output_add, gain_first, shift_first, lower_add, gain_second, shift_second = [
        vector_rows[at : at + 1] for at in range(2, 8)
    ]
    packed = (raise_weight.shape[1] // number) == output_weight.shape[1] // 2
    if packed:
        raise_stages = two_weights_by_ctx(
            after(raise_weight, attend_sign), output_weight, places
        )
        raise_sign = next(raise_stages)
    else:
        raise_stages = weight_by_core(raise_weight, places)
        output_stages = weight_by_core(output_weight, places)
        raise_sign = (next(raise_stages), next(output_stages))
    mix = mix_tokens(after(tokens_all, raise_sign), attend_full, mix_add, 0, number, None)
    if packed:
        raise_sign = raise_stages.send(mix)
    lower_stages = weight_by_core(after(lower_weight, raise_sign), places)
    mix = after(mix, raise_sign, next(lower_stages))

    seq_places = [
        jnp.stack([me.astype(jnp.int32), lengths[at].astype(jnp.int32)]) for at in range(seq_count)
    ]
    attended, attended_lows, columns, lse_rows = [], [], [], []
    for at in range(seq_count):
        one, low, column, lse_row = attend_forward(seq_places[at], at, mix)
        attended.append(one)
        attended_lows.append(low)
        columns.append(column)
        lse_rows.append(lse_row)
        if at == 0:
            lower_sign = lower_stages.send(low)
            mix = after(mix, raise_stages.send(low) if packed else None, lower_sign)
    if packed:
        raise_full, output_full = next(raise_stages)
    else:
        for stages in (raise_stages, output_stages):
            stages.send(None)
            stages.send(None)
        next_stage = next(raise_stages), next(output_stages)
        raise_full, output_full = next_stage
    attended_low = jnp.concatenate(attended_lows, axis=0)

    token_rows = hidden_states.reshape(row_count, model_width)
    projected = jnp.dot(attended_low, output_full, preferred_element_type=F32) + output_add
    normed_first, first_back = jax.vjp(
        layer_norm, token_rows.astype(F32) + projected, gain_first, shift_first
    )
    first_low = normed_first.astype(BF16)
    raised = jnp.dot(first_low, raise_full, preferred_element_type=F32) + raise_add
    active, slope = gelu_and_slope(raised)
    active_low, slope = lax.optimization_barrier((active.astype(BF16), slope))
    lower_stages.send(first_low)
    lower_full = next(lower_stages)
    lowered = jnp.dot(active_low, lower_full, preferred_element_type=F32) + lower_add
    result, second_back = jax.vjp(layer_norm, normed_first + lowered, gain_second, shift_second)
    layer_output = result.astype(BF16).reshape(block_shape)
    grad_out = cotangent.reshape(row_count, model_width).astype(F32)
    grad_mid, grad_gain_second, grad_shift_second = second_back(grad_out)
    grad_gain_second, grad_shift_second = grad_gain_second[0], grad_shift_second[0]
    mid_low = grad_mid.astype(BF16)
    shared = model_width % (8 * number * lax.axis_size("fsdp")) == 0
    grad_lower_weight = jnp.einsum("rf,rd->fd", active_low, mid_low, preferred_element_type=F32).astype(BF16)
    if shared:
        lower_pack = sum_pack([grad_lower_weight], [1], [], places, True)
        mid_low = after(mid_low, next(lower_pack))
    grad_lower_add = jnp.sum(mid_low.astype(F32), axis=0)
    grad_active = jnp.einsum("rd,fd->rf", mid_low, lower_full, preferred_element_type=F32)
    raised_low = (slope * grad_active).astype(BF16)
    lower_send = lower_pack.send(raised_low) if shared else None
    grad_raise_weight = jnp.einsum("rd,rf->df", first_low, raised_low, preferred_element_type=F32).astype(BF16)
    grad_raise_add = jnp.sum(raised_low.astype(F32), axis=0)
    grad_first = grad_mid + jnp.einsum(
        "rf,df->rd", raised_low, raise_full, preferred_element_type=F32
    )
    grad_resid, grad_gain_first, grad_shift_first = first_back(grad_first)
    grad_gain_first, grad_shift_first = grad_gain_first[0], grad_shift_first[0]
    resid_low = grad_resid.astype(BF16)
    grad_output_weight = jnp.einsum(
        "rc,rd->cd", attended_low, resid_low, preferred_element_type=F32
    ).astype(BF16)
    grad_output_add = jnp.sum(resid_low.astype(F32), axis=0)
    grad_att = (
        jnp.einsum("rd,cd->rc", resid_low, output_full, preferred_element_type=F32)
        .astype(BF16)
        .reshape(block_shape)
    )
    head_of = lax.broadcasted_iota(jnp.int32, (HEADS, model_width), 1) // HEAD_DIM
    pick = (head_of == lax.broadcasted_iota(jnp.int32, (HEADS, model_width), 0)).astype(F32)
    stats = []
    for at in range(seq_count):
        delta = jnp.einsum(
            "hd,td->ht",
            pick,
            grad_att[at].astype(F32) * attended[at],
            precision=lax.Precision.HIGHEST,
            preferred_element_type=F32,
        ).reshape(pairs, 2, tok_count)
        stats.append(jnp.concatenate([lse_rows[at], delta], axis=1))
    stats = jnp.stack(stats)
    stat_rows = stats.size // (seq_count * model_width)
    rest, coded = stats.reshape(seq_count, stat_rows, model_width), []
    for _ in range(3):
        part = lax.reduce_precision(rest, 8, 7)
        coded.append(part.astype(BF16))
        rest = rest - part
    grads_all = lax.all_gather(
        jnp.concatenate([grad_att] + coded, axis=1), "ctx", axis=0, tiled=False
    )
    coded = grads_all[:, :, tok_count:].astype(F32)
    coded = coded.reshape(number, seq_count, 3, stat_rows, model_width)
    stats_all = (coded[:, :, 0] + coded[:, :, 1] + coded[:, :, 2]).reshape(
        (number,) + stats.shape
    )
    early = [
        grad_output_add,
        grad_gain_first,
        grad_shift_first,
        grad_raise_add,
        grad_lower_add,
        grad_gain_second,
        grad_shift_second,
    ]
    query_grads, key_grads, value_grads = [], [], []
    if shared:
        raise_pack = sum_pack(
            [grad_raise_weight, grad_output_weight], [number // 2, 1], early, places
        )
        mix = after(mix, lower_send, next(raise_pack))
    for at in range(seq_count):
        query_grads.append(
            attend_queries(seq_places[at], at, mix, grad_att[at], attended[at], columns[at])
        )
        if shared and at == 0:
            mix = after(
                mix, lower_pack.send((None, query_grads[0])), raise_pack.send(query_grads[0])
            )
    for at in range(seq_count):
        grad_keys, grad_values = attend_keys(seq_places[at], at, mix, grads_all, stats_all)
        key_grads.append(grad_keys)
        value_grads.append(grad_values)
        if shared and at == 0:
            mix = after(
                mix, raise_pack.send((grads_all, grad_keys)), lower_pack.send(grad_keys)
            )
    if shared:
        raise_sends = raise_pack.send(value_grads[-1])
        value_grads[-1] = after(
            value_grads[-1], raise_sends, lower_pack.send(value_grads[-1])
        )
    query_low = jnp.concatenate(query_grads, axis=0)
    key_low = jnp.concatenate(key_grads, axis=0)
    value_low = jnp.concatenate(value_grads, axis=0)
    grad_mixture = jnp.concatenate([query_low, key_low, value_low], axis=1)
    grad_attend_weight = outer_products(
        token_rows, jnp.stack([query_low, key_low, value_low])
    )
    grad_query_add = jnp.sum(query_low.astype(F32), axis=0)
    grad_value_add = jnp.sum(value_low.astype(F32), axis=0)
    hidden_grad = grad_resid + jnp.einsum(
        "rc,dc->rd", grad_mixture, attend_full, preferred_element_type=F32
    )
    late = [grad_query_add, grad_value_add]
    if shared:
        attend_pack = sum_pack([grad_attend_weight], [-3], late, places)
        next(attend_pack)
        attend_pack.send(None)
        lower_pack.send(grad_attend_weight)
        attend_partial = attend_pack.send((None, None))
        raise_pack.send(attend_partial)
        attend_sends = next(attend_pack)
        raise_pack.send(attend_sends)
        next(attend_pack)
        next(attend_pack)
        (grad_attend_weight,), late = next(attend_pack)
        (grad_lower_weight,), _ = next(lower_pack)
        (grad_raise_weight, grad_output_weight), early = next(raise_pack)
    else:
        grad_lower_weight = sum_weight(grad_lower_weight)
        grad_raise_weight = sum_weight(grad_raise_weight)
        grad_output_weight = sum_weight(grad_output_weight)
        grad_attend_weight = sum_weight(grad_attend_weight)
        early, late = sum_vectors(early), sum_vectors(late)
    (
        grad_output_add,
        grad_gain_first,
        grad_shift_first,
        grad_raise_add,
        grad_lower_add,
        grad_gain_second,
        grad_shift_second,
    ) = early
    grad_query_add, grad_value_add = late
    return (
        layer_output,
        hidden_grad.reshape(block_shape),
        grad_attend_weight,
        grad_query_add,
        grad_value_add,
        grad_output_weight,
        grad_output_add,
        grad_gain_first,
        grad_shift_first,
        grad_raise_weight,
        grad_raise_add,
        grad_lower_weight,
        grad_lower_add,
        grad_gain_second,
        grad_shift_second,
    )


def solution(mesh):
    return jax.shard_map(
        on_device,
        mesh=mesh,
        in_specs=(
            P("fsdp", "ctx", None),
            P("fsdp"),
            P("fsdp", "ctx", None),
            P("fsdp", None),
            P("fsdp"),
            P("fsdp"),
            P("fsdp", None),
            P("fsdp"),
            P("fsdp"),
            P("fsdp"),
            P("fsdp", None),
            P("fsdp"),
            P("fsdp", None),
            P("fsdp"),
            P("fsdp"),
            P("fsdp"),
        ),
        out_specs=(
            P("fsdp", "ctx", None),
            P("fsdp", "ctx", None),
            P("fsdp", None),
            P("fsdp"),
            P("fsdp"),
            P("fsdp", None),
            P("fsdp"),
            P("fsdp"),
            P("fsdp"),
            P("fsdp", None),
            P("fsdp"),
            P("fsdp", None),
            P("fsdp"),
            P("fsdp"),
            P("fsdp"),
        ),
        check_vma=False,
    )
```
